32 devices in a mesh: frame: 4 (over z), patch: 8 (over y, x, core).
Axes of the slice: x: 2, y: 2, z: 4, core: 2. Of those that a mesh axis runs over, the one named last changes fastest.
Arguments:
- video: bfloat16 [8, 512, 1152], P('frame', 'patch'), may hold values from -6 to 6
- cotangent: bfloat16 [8, 512, 1152], P('frame', 'patch'), may hold values from -6 to 6
- frame_mask: int32 [8], replicated, may hold values 0 or 1
- spatial_project: bfloat16 [1152, 3456], replicated, may hold values from -0.1875 to 0.1875
- spatial_output: bfloat16 [1152, 1152], replicated, may hold values from -0.1875 to 0.1875
- temporal_project: bfloat16 [1152, 3456], replicated, may hold values from -0.1875 to 0.1875
- temporal_output: bfloat16 [1152, 1152], replicated, may hold values from -0.1875 to 0.1875
- spatial_inward: float32 [36, 32, 32], replicated, may hold values from -0.25 to 1.25, as said below
- spatial_outward: float32 [36, 32, 32], replicated, may hold values from -0.25 to 1.25, as said below
- temporal_inward: float32 [36, 32, 32], replicated, may hold values from -0.25 to 1.25, as said below
- temporal_outward: float32 [36, 32, 32], replicated, may hold values from -0.25 to 1.25, as said below
Outputs:
- video_gradient: bfloat16 [8, 512, 1152], P('frame', 'patch')
- gradient_spatial_inward: float32 [36, 32, 32], replicated
- gradient_spatial_outward: float32 [36, 32, 32], replicated
- gradient_temporal_inward: float32 [36, 32, 32], replicated
- gradient_temporal_outward: float32 [36, 32, 32], replicated
The draws below stay inside these ranges and needn't reach their ends.
Inputs may be any that keep to these rules, and one draw needn't show every extreme that they name: `spatial_inward`: identity blocks plus independent entries. `spatial_outward`: identity blocks plus independent entries. `temporal_inward`: identity blocks plus independent entries. `temporal_outward`: identity blocks plus independent entries.
All inputs are finite; a program needn't handle non-finite values.
Results may differ from the reference program's by a relative error of at most 0.028.
Values may be sent and summed in bfloat16 or wider, within the bound.
No kernel may reach another device: no remote copies, remote signals or barrier semaphores. Data moves between devices by JAX's collectives and lax.ppermute only.
A program may use at most 192 MiB of HBM per device.

```python
import math
import jax
import jax.numpy as jnp
from jax import lax

D = 1152
HEADS = 16
HEAD_DIM = 72
BLOCK = 32
NBLOCK = 36
FRAMES = 8
PATCHES = 512


def rotation_blocks(noise):
    return jnp.eye(BLOCK, dtype=jnp.float32)[None, :, :] + noise / math.sqrt(BLOCK)


def draw_spatial_inward(key, part):
    key = jax.random.fold_in(key, 11)
    noise = 0.4 * jax.random.truncated_normal(key, -1.75, 1.75, (NBLOCK, BLOCK, BLOCK), jnp.float32)
    return rotation_blocks(noise)


def draw_spatial_outward(key, part):
    key = jax.random.fold_in(key, 12)
    noise = 0.4 * jax.random.truncated_normal(key, -1.75, 1.75, (NBLOCK, BLOCK, BLOCK), jnp.float32)
    return rotation_blocks(noise)


def draw_temporal_inward(key, part):
    key = jax.random.fold_in(key, 13)
    noise = 0.4 * jax.random.truncated_normal(key, -1.75, 1.75, (NBLOCK, BLOCK, BLOCK), jnp.float32)
    return rotation_blocks(noise)


def draw_temporal_outward(key, part):
    key = jax.random.fold_in(key, 14)
    noise = 0.4 * jax.random.truncated_normal(key, -1.75, 1.75, (NBLOCK, BLOCK, BLOCK), jnp.float32)
    return rotation_blocks(noise)


def set_ends(drawn, rng, low, high):
    spot = [jax.random.randint(jax.random.fold_in(rng, axis), (), 0, length) for axis, length in enumerate(drawn.shape)]
    widest = drawn.shape.index(max(drawn.shape))
    next_to = spot[:widest] + [(spot[widest] + 1) % drawn.shape[widest]] + spot[widest + 1:]
    return drawn.at[tuple(spot)].set(low).at[tuple(next_to)].set(high)


def block_levels(own_key, dims, shards, smallest, top_value):
    def one(dim, shards_of):
        heights = jax.random.uniform(jax.random.fold_in(jax.random.fold_in(own_key, 6), dim), (shards_of,), jnp.float32, smallest / len(shards), top_value / len(shards))
        return jnp.repeat(jnp.exp(heights), dims[dim] // shards_of).reshape((-1,) + (1,) * (len(dims) - dim - 1))

    gain = one(*shards[0])
    for cut in shards[1:]:
        gain = gain * one(*cut)
    return gain


def gaussian(rng, shape, scale, limit, split=(), held_as=jnp.bfloat16):
    loudness = block_levels(rng, shape, split, -0.22, 0.18) if split else 1.0
    entries = jax.random.normal(rng, shape, jnp.float32) * scale * loudness
    return jnp.minimum(jnp.maximum(entries, -limit), limit).astype(held_as)


def setup_inputs(seed: int = 0) -> dict:
    keys = jax.random.split(jax.random.key(seed), 12)
    video = gaussian(keys[0], (FRAMES, PATCHES, D), 1.0, 6.0, ((0, 4), (1, 8)))
    cotangent = gaussian(keys[1], (FRAMES, PATCHES, D), 1.0, 6.0, ((0, 4), (1, 8)))
    frame_mask = set_ends((jax.random.randint(keys[2], (FRAMES,), 0, 64) < 51).astype(jnp.int32), jax.random.fold_in(keys[2], 1), 0, 1)
    spatial_project = gaussian(keys[3], (D, 3 * D), D ** -0.5, 0.1875)
    spatial_output = gaussian(keys[4], (D, D), D ** -0.5, 0.1875)
    temporal_project = gaussian(keys[5], (D, 3 * D), D ** -0.5, 0.1875)
    temporal_output = gaussian(keys[6], (D, D), D ** -0.5, 0.1875)
    spatial_inward = draw_spatial_inward(jax.random.fold_in(keys[11], 71), 0)
    spatial_outward = draw_spatial_outward(jax.random.fold_in(keys[11], 71), 0)
    temporal_inward = draw_temporal_inward(jax.random.fold_in(keys[11], 71), 0)
    temporal_outward = draw_temporal_outward(jax.random.fold_in(keys[11], 71), 0)
    return dict(video=video, cotangent=cotangent, frame_mask=frame_mask, spatial_project=spatial_project, spatial_output=spatial_output, temporal_project=temporal_project, temporal_output=temporal_output, spatial_inward=spatial_inward, spatial_outward=spatial_outward, temporal_inward=temporal_inward, temporal_outward=temporal_outward)


EPSILON = 1e-06
NEGATIVE = -1e+30

def normalize(inputs):
    average = lax.optimization_barrier(jnp.mean(inputs, axis=-1, keepdims=True))
    centered = inputs - average
    variance = lax.optimization_barrier(jnp.mean(centered * centered, axis=-1, keepdims=True))
    inverse = lax.rsqrt(variance + EPSILON)
    return (centered * inverse, inverse)

def normalize_backward(adjoint, normed, inverse):
    grad_mean = lax.optimization_barrier(jnp.mean(adjoint, axis=-1, keepdims=True))
    grad_cross = lax.optimization_barrier(jnp.mean(adjoint * normed, axis=-1, keepdims=True))
    return inverse * (adjoint - grad_mean - normed * grad_cross)

def rotate(inputs, blocks):
    shaped = inputs.reshape(inputs.shape[0], blocks.shape[0], blocks.shape[1])
    turned = jnp.einsum('tnb,nbc->tnc', shaped, blocks, precision=lax.Precision.HIGHEST)
    return turned.reshape(inputs.shape)

def rotate_transposed(adjoint, blocks):
    shaped = adjoint.reshape(adjoint.shape[0], blocks.shape[0], blocks.shape[1])
    turned = jnp.einsum('tnc,nbc->tnb', shaped, blocks, precision=lax.Precision.HIGHEST)
    return turned.reshape(adjoint.shape)

def rotation_gradient(inputs, adjoint, blocks):
    left_rows = inputs.reshape(inputs.shape[0], blocks.shape[0], blocks.shape[1])
    right_rows = adjoint.reshape(adjoint.shape[0], blocks.shape[0], blocks.shape[1])
    return jnp.einsum('tnb,tnc->nbc', left_rows, right_rows, precision=lax.Precision.HIGHEST)

def attention_weights(queries, key_rows, score_bias):
    scaling = 1.0 / math.sqrt(queries.shape[-1])
    scores = jnp.einsum('nld,nmd->nlm', queries.astype(jnp.float32), key_rows.astype(jnp.float32)) * scaling + score_bias
    return jax.nn.softmax(scores, axis=-1)

def attention_forward(stacked, score_bias):
    probability = attention_weights(stacked[:, :, 0], stacked[:, :, 1], score_bias)
    rounded = lax.optimization_barrier(probability.astype(jnp.bfloat16)).astype(jnp.float32)
    result = jnp.einsum('nlm,nmd->nld', rounded, stacked[:, :, 2].astype(jnp.float32))
    return result.astype(jnp.bfloat16)

def attention_backward(stacked, adjoint, score_bias):
    queries = stacked[:, :, 0]
    key_rows = stacked[:, :, 1]
    values = stacked[:, :, 2]
    scaling = 1.0 / math.sqrt(queries.shape[-1])
    probability = attention_weights(queries, key_rows, score_bias)
    rounded = lax.optimization_barrier(probability.astype(jnp.bfloat16)).astype(jnp.float32)
    upstream = adjoint.astype(jnp.float32)
    grad_values = jnp.einsum('nlm,nld->nmd', rounded, upstream).astype(jnp.bfloat16)
    grad_weights = jnp.einsum('nld,nmd->nlm', upstream, values.astype(jnp.float32))
    delta_sum = lax.optimization_barrier(jnp.sum(probability * grad_weights, axis=-1, keepdims=True))
    grad_scores = (probability * (grad_weights - delta_sum)).astype(jnp.bfloat16)
    grad_scores = lax.optimization_barrier(grad_scores).astype(jnp.float32)
    grad_queries = (scaling * jnp.einsum('nlm,nmd->nld', grad_scores, key_rows.astype(jnp.float32))).astype(jnp.bfloat16)
    grad_keys = (scaling * jnp.einsum('nlm,nld->nmd', grad_scores, queries.astype(jnp.float32))).astype(jnp.bfloat16)
    return jnp.stack([grad_queries, grad_keys, grad_values], axis=2)

def reference(video, cotangent, frame_mask, spatial_project, spatial_output, temporal_project, temporal_output, spatial_inward, spatial_outward, temporal_inward, temporal_outward):
    token_count = FRAMES * PATCHES
    inputs = video.astype(jnp.float32).reshape(token_count, D)
    normed_one, inverse_one = normalize(inputs)
    rotated_one = rotate(normed_one, spatial_inward).astype(jnp.bfloat16)
    projected_one = jnp.dot(rotated_one, spatial_project, preferred_element_type=jnp.float32).astype(jnp.bfloat16)
    spatial_stack = projected_one.reshape(FRAMES, PATCHES, 3, HEADS, HEAD_DIM).transpose(0, 3, 1, 2, 4)
    zero_bias = jnp.zeros((1, 1), jnp.float32)

    def spatial_frame(stacked):
        return attention_forward(stacked, zero_bias)
    attended_one = lax.map(spatial_frame, spatial_stack)
    attended_one = attended_one.transpose(0, 2, 1, 3).reshape(token_count, D)
    attended_wide = lax.optimization_barrier(attended_one).astype(jnp.float32)
    outrot_one = rotate(attended_wide, spatial_outward).astype(jnp.bfloat16)
    hidden = (inputs + jnp.dot(outrot_one, spatial_output, preferred_element_type=jnp.float32)).astype(jnp.bfloat16)
    middle = lax.optimization_barrier(hidden).astype(jnp.float32)
    normed_two, inverse_two = normalize(middle)
    rotated_two = rotate(normed_two, temporal_inward).astype(jnp.bfloat16)
    projected_two = jnp.dot(rotated_two, temporal_project, preferred_element_type=jnp.float32).astype(jnp.bfloat16)
    temporal_stack = projected_two.reshape(FRAMES, PATCHES, 3, HEADS, HEAD_DIM).transpose(1, 3, 0, 2, 4)
    temporal_stack = temporal_stack.reshape(PATCHES * HEADS, FRAMES, 3, HEAD_DIM)
    positions = jnp.arange(FRAMES)
    allowed = (frame_mask[None, :] == 1) | (positions[:, None] == positions[None, :])
    score_bias = jnp.where(allowed, 0.0, NEGATIVE).astype(jnp.float32)
    attended_two = attention_forward(temporal_stack, score_bias)
    attended_two = attended_two.reshape(PATCHES, HEADS, FRAMES, HEAD_DIM).transpose(2, 0, 1, 3).reshape(token_count, D)
    validity = frame_mask.astype(jnp.float32)
    adjoint_top = (cotangent.astype(jnp.float32) * validity[:, None, None]).reshape(token_count, D)
    adjoint_outrot = jnp.dot(adjoint_top.astype(jnp.bfloat16), temporal_output.T, preferred_element_type=jnp.float32)
    term_tout = rotation_gradient(attended_two.astype(jnp.float32), adjoint_outrot, temporal_outward)
    adjoint_attended = rotate_transposed(adjoint_outrot, temporal_outward).astype(jnp.bfloat16)
    adjoint_items = adjoint_attended.reshape(FRAMES, PATCHES, HEADS, HEAD_DIM).transpose(1, 2, 0, 3)
    adjoint_items = adjoint_items.reshape(PATCHES * HEADS, FRAMES, HEAD_DIM)
    adjoint_stack = attention_backward(temporal_stack, adjoint_items, score_bias)
    adjoint_projected = adjoint_stack.reshape(PATCHES, HEADS, FRAMES, 3, HEAD_DIM).transpose(2, 0, 3, 1, 4)
    adjoint_projected = adjoint_projected.reshape(token_count, 3 * D)
    adjoint_rotated = jnp.dot(adjoint_projected, temporal_project.T, preferred_element_type=jnp.float32)
    term_tin = rotation_gradient(normed_two, adjoint_rotated, temporal_inward)
    adjoint_normed = rotate_transposed(adjoint_rotated, temporal_inward)
    adjoint_hidden = adjoint_top + normalize_backward(adjoint_normed, normed_two, inverse_two)
    adjoint_outrot = jnp.dot(adjoint_hidden.astype(jnp.bfloat16), spatial_output.T, preferred_element_type=jnp.float32)
    term_sout = rotation_gradient(attended_wide, adjoint_outrot, spatial_outward)
    adjoint_attended = rotate_transposed(adjoint_outrot, spatial_outward).astype(jnp.bfloat16)
    adjoint_items = adjoint_attended.reshape(FRAMES, PATCHES, HEADS, HEAD_DIM).transpose(0, 2, 1, 3)

    def spatial_back(paired):
        return attention_backward(paired[0], paired[1], zero_bias)
    adjoint_stack = lax.map(spatial_back, (spatial_stack, adjoint_items))
    adjoint_projected = adjoint_stack.transpose(0, 2, 3, 1, 4).reshape(token_count, 3 * D)
    adjoint_rotated = jnp.dot(adjoint_projected, spatial_project.T, preferred_element_type=jnp.float32)
    term_sin = rotation_gradient(normed_one, adjoint_rotated, spatial_inward)
    adjoint_normed = rotate_transposed(adjoint_rotated, spatial_inward)
    video_gradient = (adjoint_hidden + normalize_backward(adjoint_normed, normed_one, inverse_one)).astype(jnp.bfloat16)
    video_gradient = video_gradient.reshape(FRAMES, PATCHES, D)
    scaling = 1.0 / math.sqrt(token_count)
    return (video_gradient, term_sin * scaling, term_sout * scaling, term_tin * scaling, term_tout * scaling)
```

```python
import functools
import math

import jax
import jax.numpy as jnp
from jax import lax
from jax.experimental import pallas as pl
from jax.experimental.pallas import tpu as pltpu
from jax.sharding import PartitionSpec as P

D = 1152
HEADS = 16
HEAD_DIM = 72
BLOCK = 32
LANES = 128
TILE = 16
SPANS = ((0, 640), (640, 512))
CHUNKS = D // LANES
EPSILON = 1e-06
NEGATIVE = -1e30
SCALE = 1.0 / math.sqrt(HEAD_DIM)
F32 = jnp.float32
BF16 = jnp.bfloat16
VMEM = pl.BlockSpec(memory_space=pltpu.VMEM)
SMEM = pl.BlockSpec(memory_space=pltpu.SMEM)
HBM = pl.BlockSpec(memory_space=pltpu.HBM)
MIB = 1024 * 1024


def dot(a, b):
    return jnp.dot(a, b, preferred_element_type=F32)


def dot_nt(a, b):
    return lax.dot_general(a, b, (((1,), (1,)), ((), ())), preferred_element_type=F32)


def dot_tn(a, b):
    return lax.dot_general(a, b, (((0,), (0,)), ((), ())), preferred_element_type=F32)


def normalize(rows):
    average = jnp.mean(rows, axis=-1, keepdims=True)
    centered = rows - average
    variance = jnp.mean(centered * centered, axis=-1, keepdims=True)
    inverse = lax.rsqrt(variance + EPSILON)
    return centered * inverse, inverse


def normalize_backward(adjoint, normed, inverse):
    grad_mean = jnp.mean(adjoint, axis=-1, keepdims=True)
    grad_cross = jnp.mean(adjoint * normed, axis=-1, keepdims=True)
    return inverse * (adjoint - grad_mean - normed * grad_cross)


def diagonal_mask():
    row = lax.broadcasted_iota(jnp.int32, (LANES, LANES), 0)
    column = lax.broadcasted_iota(jnp.int32, (LANES, LANES), 1)
    return (row // BLOCK) == (column // BLOCK)


def lanes_of(chunk):
    return slice(chunk * LANES, (chunk + 1) * LANES)


def diagonal_spans(blocks_ref):
    width = blocks_ref.shape[1]
    return [(low, min(width, D - low)) for low in range(0, D, width)]


def rotate(rows, blocks_ref):
    return jnp.concatenate(
        [
            dot(rows[:, low : low + size], blocks_ref[low : low + size, 0:size])
            for low, size in diagonal_spans(blocks_ref)
        ],
        axis=1,
    )


def rotate_transposed(rows, blocks_ref):
    return jnp.concatenate(
        [
            dot_nt(rows[:, low : low + size], blocks_ref[low : low + size, 0:size])
            for low, size in diagonal_spans(blocks_ref)
        ],
        axis=1,
    )


def rotation_gradient(left, right, mask, term_ref, base, width=LANES):
    for low in range(0, D, width):
        span = slice(low, min(low + width, D))
        product = dot_tn(left[:, span], right[:, span])
        for inner in range(0, span.stop - low, LANES):
            tile = slice(inner, inner + LANES)
            full = jnp.where(mask, product[tile, tile], 0.0)
            packed = full[0:BLOCK]
            for i in range(1, LANES // BLOCK):
                packed = packed + full[i * BLOCK : (i + 1) * BLOCK]
            start = (base + (low + inner) // LANES) * BLOCK
            term_ref[start : start + BLOCK, :] = packed


class Arriving:
    def __init__(self, source, target, sem):
        self.target = target
        self.copy = pltpu.make_async_copy(source, target, sem)
        self.waited = False

    def begin(self):
        self.copy.start()

    def __call__(self):
        if not self.waited:
            self.copy.wait()
            self.waited = True
        return self.target


class Leaving:
    def __init__(self, source, target, sems):
        self.ref, self.target, self.sems = source, target, sems
        self.started = []

    def flush(self, *parts):
        for i in parts:
            copy = pltpu.make_async_copy(self.ref.at[i], self.target.at[i], self.sems.at[i])
            copy.start()
            self.started.append(copy)

    def finish(self):
        for copy in self.started:
            copy.wait()


def call(kernel, ins, outs, scratch=(), limit=60, cost=None):
    specs = {"v": VMEM, "s": SMEM, "h": HBM, "l": HBM, "p": HBM, "d": HBM}
    loads = [array for mode, array in ins if mode in "lp"]
    stores = [out for mode, out in outs if mode == "d"]
    staging = [pltpu.VMEM(array.shape, array.dtype) for array in loads + stores]
    staging += [pltpu.SemaphoreType.DMA] * len(loads)
    staging += [pltpu.SemaphoreType.DMA((out.shape[0],)) for out in stores]

    def body(*refs):
        given = list(refs[: len(ins) + len(outs)])
        own = refs[len(given) : len(given) + len(scratch)]
        staged = list(refs[len(given) + len(scratch) :])
        buffers, sems = staged[: len(loads) + len(stores)], staged[len(loads) + len(stores) :]
        leaving = []
        for i, (mode, _) in enumerate(list(ins) + list(outs)):
            if mode in "lp":
                given[i] = Arriving(given[i], buffers.pop(0), sems.pop(0))
                if mode == "l":
                    given[i].begin()
            elif mode == "d":
                given[i] = Leaving(buffers.pop(0), given[i], sems.pop(0))
                leaving.append(given[i])
        kernel(*given, *own)
        for out in leaving:
            out.finish()

    return pl.pallas_call(
        body,
        out_shape=tuple(out for _, out in outs),
        in_specs=[specs[mode] for mode, _ in ins],
        out_specs=tuple(specs[mode] for mode, _ in outs),
        scratch_shapes=list(scratch) + staging,
        compiler_params=pltpu.CompilerParams(vmem_limit_bytes=limit * MIB),
        cost_estimate=cost,
    )(*[array for _, array in ins])


def start_all(pairs, sems):
    copies = [
        pltpu.make_async_copy(source, target, sems.at[i]) for i, (source, target) in enumerate(pairs)
    ]
    for copy in copies:
        copy.start()
    return copies


def wait_all(copies):
    for copy in copies:
        copy.wait()


class Plan:
    def __init__(self, frames_local, patches_local, frame_ways, patch_ways):
        self.frames_local = frames_local
        self.patches_local = patches_local
        self.frame_ways = frame_ways
        self.patch_ways = patch_ways
        self.devices = frame_ways * patch_ways
        self.tokens = frames_local * patches_local
        self.frames = frames_local * frame_ways
        self.patches = patches_local * patch_ways
        self.items = frames_local * HEADS // patch_ways
        self.groups = HEADS // self.items
        self.width = self.items * HEAD_DIM
        self.window = max(
            -(-((g + 1) * self.width - g * self.width // LANES * LANES) // LANES) * LANES
            for g in range(self.groups)
        )
        self.padded = self.items * LANES
        self.own_patches = patches_local // frame_ways
        self.own_rows = frames_local * self.own_patches
        self.rows = self.frames * self.own_patches
        self.part = min(self.patches, 512)
        self.parts = self.patches // self.part
        self.term_blocks = BLOCK // patch_ways
        self.term_rows = 4 * CHUNKS * self.term_blocks
        self.term_tiles = -(-self.term_rows // TILE)

    def window_start(self, group):
        return min(group * self.width // LANES * LANES, D - self.window)

    def own_window(self):
        group = lax.rem(lax.axis_index("patch"), self.groups)
        start = jnp.minimum(group * self.width // LANES * LANES, D - self.window)
        return pl.multiple_of(start, LANES), group * self.width - start

    def peer(self, distance):
        return lax.axis_index("patch") ^ distance

    def frame_of(self, distance):
        return self.peer(distance) // self.groups

    def other_frame(self, shift):
        return lax.rem(lax.axis_index("frame") + shift, self.frame_ways)


def head_selection(plan, offset):
    lane = lax.broadcasted_iota(jnp.int32, (plan.window, plan.padded), 0)
    target = lax.broadcasted_iota(jnp.int32, (plan.window, plan.padded), 1)
    inner = target % LANES
    source = offset + (target // LANES) * HEAD_DIM + inner
    return jnp.where((lane == source) & (inner < HEAD_DIM), 1.0, 0.0).astype(BF16)


def weight_windows(plan, weight_ref, windows, sems):
    start, _ = plan.own_window()
    return [
        pltpu.make_async_copy(
            weight_ref.at[:, pl.ds(pl.multiple_of(s * D + start, LANES), plan.window)],
            windows.at[:, pl.ds(s * plan.window, plan.window)],
            sems.at[s],
        )
        for s in range(3)
    ]


def pack_kernel(plan, video, cotangent, early_ref):
    own = plan.own_patches
    for t, source in enumerate((video(), cotangent())):
        for z in range(plan.frame_ways):
            for f in range(plan.frames_local):
                early_ref[z, t, f * own : (f + 1) * own, :] = source[
                    f, z * own : (z + 1) * own, :
                ]


def blocks_kernel(*refs):
    mask = diagonal_mask()
    for blocks_ref, out in zip(refs[: len(refs) // 2], refs[len(refs) // 2 :]):
        width = out.ref.shape[2]
        for c in range(CHUNKS):
            tiled = jnp.concatenate([blocks_ref[lanes_of(c), :]] * (LANES // BLOCK), axis=1)
            tile = jnp.where(mask, tiled, 0.0).astype(BF16)
            for k in range(width // LANES):
                here = c % (width // LANES) == k
                out.ref[0, lanes_of(c), lanes_of(k)] = tile if here else jnp.zeros_like(tile)
        out.flush(0)


def spatial_forward_kernel(plan, *refs):
    pieces = refs[: plan.patch_ways]
    (
        blocks,
        weight_ref,
        normed_out,
        stack_out,
        weights_out,
        send_ref,
        windows,
        attended,
        sems,
    ) = refs[plan.patch_ways :]
    copies = weight_windows(plan, weight_ref, windows, sems)
    for copy in copies:
        copy.start()
    _, offset = plan.own_window()
    chosen = head_selection(plan, offset)
    size = plan.patches_local
    for r, piece in enumerate(pieces):
        for i in range(0, size, BLOCK):
            normed = normalize(piece[i : i + BLOCK, :].astype(F32))[0].astype(BF16)
            normed_out.ref[0, r * size + i : r * size + i + BLOCK, :] = normed
    normed_out.flush(0)
    rotated = rotate(normed_out.ref[0], blocks().at[0]).astype(BF16)
    stack_ref = stack_out.ref
    wait_all(copies)
    projected = dot(rotated, windows[...]).astype(BF16)
    for s in range(3):
        part = projected[:, s * plan.window : (s + 1) * plan.window]
        stack_ref[s] = dot(part, chosen).astype(BF16)
        stack_out.flush(s)
    for h in range(plan.items):
        queries, keys, values = [stack_ref[s, :, lanes_of(h)] for s in range(3)]
        values_t = values.astype(F32).T.astype(BF16)
        for c in range(plan.parts):
            span = slice(c * plan.part, (c + 1) * plan.part)
            scores = dot_nt(keys, queries[span]) * SCALE
            top = jnp.max(scores, axis=0, keepdims=True)
            raised = jnp.exp(scores - top)
            total = jnp.sum(raised, axis=0, keepdims=True)
            rounded = (raised * (1.0 / total)).astype(BF16)
            weights_out.ref[h * plan.parts + c] = rounded
            weights_out.flush(h * plan.parts + c)
            attended[span, lanes_of(h)] = dot(values_t, rounded).T.astype(BF16)
    own = plan.own_patches
    result = dot_nt(attended[...], chosen).astype(BF16)
    for r in range(plan.patch_ways):
        target = plan.peer(r)
        for z in range(plan.frame_ways):
            start = r * size + z * own
            send_ref[z * plan.patch_ways + target] = result[start : start + own, :]


def order_terms(plan, terms, ordered, first, count):
    share = plan.term_tiles * TILE
    for b in range(BLOCK):
        owner, inner = divmod(b, plan.term_blocks)
        start = owner * share + inner * 4 * CHUNKS + first
        ordered[start : start + count, :] = terms[pl.ds(b, count, stride=BLOCK), :]


def term_kernel(plan, prepared_ref, factors, out, outrot, terms, sems):
    copies = start_all([(prepared_ref.at[1], outrot)], sems)
    mask = diagonal_mask()
    parts = factors()
    rotation_gradient(parts[1], parts[2], mask, terms, CHUNKS)
    rotation_gradient(parts[3], parts[4], mask, terms, 2 * CHUNKS)
    wait_all(copies)
    rotation_gradient(parts[0], outrot[...], mask, terms, 0)
    ordered = out.ref.at[0]
    ordered[...] = jnp.zeros_like(ordered)
    order_terms(plan, terms, ordered, 0, 3 * CHUNKS)
    out.flush(0)


def spatial_backward_kernel(
    plan,
    adjoint_ref,
    stack,
    weights,
    blocks,
    normed,
    term,
    weight_ref,
    even_ref,
    odd_ref,
    windows,
    adjoint,
    grads,
    projected,
    terms,
    sems,
):
    copies = weight_windows(plan, weight_ref, windows, sems)
    for copy in copies:
        copy.start()
    own = plan.own_patches
    for r in range(plan.patch_ways):
        source = plan.peer(r)
        for z in range(plan.frame_ways):
            start = r * plan.patches_local + z * own
            adjoint[start : start + own, :] = adjoint_ref[z * plan.patch_ways + source]
    _, offset = plan.own_window()
    chosen = head_selection(plan, offset)
    upstream_all = dot(adjoint[...], chosen).astype(BF16)
    stack_ref, weights_ref = stack(), weights()
    for h in range(plan.items):
        queries, keys, values = [stack_ref[s, :, lanes_of(h)] for s in range(3)]
        upstream = upstream_all[:, lanes_of(h)]
        keys_t = keys.astype(F32).T.astype(BF16)
        grad_keys = None
        grad_values = None
        for c in range(plan.parts):
            span = slice(c * plan.part, (c + 1) * plan.part)
            rounded = weights_ref[h * plan.parts + c]
            probability = rounded.astype(F32)
            grad_weights = dot_nt(values, upstream[span])
            delta = jnp.sum(probability * grad_weights, axis=0, keepdims=True)
            grad_scores = (probability * (grad_weights - delta)).astype(BF16)
            value_part = dot(rounded, upstream[span])
            key_part = dot(grad_scores, queries[span])
            grad_values = value_part if grad_values is None else grad_values + value_part
            grad_keys = key_part if grad_keys is None else grad_keys + key_part
            grads[0, span, lanes_of(h)] = (dot(keys_t, grad_scores).T * SCALE).astype(BF16)
        grads[1, :, lanes_of(h)] = (grad_keys * SCALE).astype(BF16)
        grads[2, :, lanes_of(h)] = grad_values.astype(BF16)
    for s, copy in enumerate(copies):
        projected[:, s * plan.window : (s + 1) * plan.window] = dot_nt(grads[s], chosen).astype(
            BF16
        )
        copy.wait()
    rotated = dot_nt(projected[...], windows[...]).astype(BF16)
    size = plan.patches_local
    share = plan.term_tiles * TILE
    back = rotate_transposed(rotated, blocks().at[0]).astype(BF16)
    rotation_gradient(normed()[0], rotated, diagonal_mask(), terms, 0, 2 * LANES)
    ordered = term().at[0]
    order_terms(plan, terms, ordered, 3 * CHUNKS, CHUNKS)
    for r in range(plan.patch_ways):
        out_ref = (even_ref, odd_ref)[r % 2].at[r // 2]
        out_ref[0:size, :] = back[r * size : (r + 1) * size, :]
        owned = ordered[pl.ds(pl.multiple_of(plan.peer(r) * share, TILE), share), :].astype(BF16)
        for k in range(CHUNKS):
            if k < plan.term_tiles:
                tile = owned[k * TILE : (k + 1) * TILE, :]
            else:
                tile = jnp.zeros((TILE, LANES), BF16)
            out_ref[size : size + TILE, lanes_of(k)] = tile


def pair_kernel(plan, even_ref, other_ref, *out_refs):
    for s, out_ref in enumerate(out_refs):
        out_ref[...] = (even_ref[s].astype(F32) + other_ref[s].astype(F32)).astype(BF16)


def frame_column(plan, mask_ref):
    frame = lax.broadcasted_iota(jnp.int32, (plan.rows, 1), 0) // plan.own_patches
    valid = jnp.zeros((plan.rows, 1), jnp.int32)
    for f in range(plan.frames):
        valid = jnp.where(frame == f, mask_ref[f], valid)
    return valid


def collect_rows(plan, early_ref, which, target):
    return [
        (early_ref.at[z, which], target.at[pl.ds(z * plan.own_rows, plan.own_rows), :])
        for z in range(plan.frame_ways)
    ]


def top_kernel(plan, early_ref, mask_ref, weight, blocks, out, rows, sems):
    copies = start_all(collect_rows(plan, early_ref, 1, rows), sems)
    valid = frame_column(plan, mask_ref).astype(F32)
    wait_all(copies)
    top = (rows[...].astype(F32) * valid).astype(BF16)
    out.ref[0] = top
    out.flush(0)
    outrot = dot_nt(top, weight()[...]).astype(BF16)
    out.ref[1] = outrot
    out.flush(1)
    out.ref[2] = rotate_transposed(outrot, blocks().at[0]).astype(BF16)
    out.flush(2)


def head_window(h):
    low = h * HEAD_DIM // LANES * LANES
    high = -(-(h + 1) * HEAD_DIM // LANES) * LANES
    return low, high


def head_lanes(h, low, high):
    lane = low + lax.broadcasted_iota(jnp.int32, (1, high - low), 1)
    inside = (lane >= h * HEAD_DIM) & (lane < (h + 1) * HEAD_DIM)
    return jnp.where(inside, 1.0, 0.0).astype(BF16)


def temporal_kernel(plan, *refs):
    (
        early_ref,
        arrived_ref,
        mask_ref,
        outward,
        spatial_output,
        inward,
        project_ref,
        prepared,
        send_ref,
        factors,
    ) = refs[:10]
    leaving = refs[10 : 10 + plan.frame_ways]
    (
        project_weight,
        weight_sems,
        inputs,
        projected,
        weights,
        slopes,
        grads,
        piece_sems,
    ) = refs[10 + plan.frame_ways :]
    piece_copies = start_all(collect_rows(plan, early_ref, 0, inputs), piece_sems)
    weight_copies = start_all(
        [(project_ref.at[pl.ds(*span), :], project_weight.at[pl.ds(*span), :]) for span in SPANS],
        weight_sems,
    )
    own = plan.own_patches
    attended_one = factors.ref.at[3]
    for f in range(plan.frames):
        z, inner = divmod(f, plan.frames_local)
        base = z * plan.patch_ways + inner * plan.groups
        for c in range(CHUNKS):
            tile = None
            for g in range(plan.groups):
                low = c * LANES - plan.window_start(g)
                if 0 <= low < plan.window:
                    part = arrived_ref[base + g, :, low : low + LANES]
                    tile = part if tile is None else tile + part
            attended_one[f * own : (f + 1) * own, lanes_of(c)] = tile
    factors.flush(3)
    outrot_one = rotate(attended_one[...], outward().at[0]).astype(BF16)
    out_weight = spatial_output()
    wait_all(piece_copies)
    hidden = (inputs[...].astype(F32) + dot(outrot_one, out_weight[...])).astype(BF16)
    normed, inverse = normalize(hidden.astype(F32))
    normed_low = normed.astype(BF16)
    factors.ref[1] = normed_low
    factors.flush(1)
    rotated = rotate(normed_low, inward().at[0]).astype(BF16)
    total = None
    for (start, size), copy in zip(SPANS, weight_copies):
        copy.wait()
        span = slice(start, start + size)
        if start == 0:
            prepared.begin()
        part = dot(rotated[:, span], project_weight[span, :])
        total = part if total is None else total + part
    projected[...] = total.astype(BF16)

    key_valid = frame_column(plan, mask_ref) == 1
    shape = (plan.rows, plan.rows)
    key_row = lax.broadcasted_iota(jnp.int32, shape, 0)
    query_row = lax.broadcasted_iota(jnp.int32, shape, 1)
    allowed = (key_row == query_row) | (((key_row % own) == (query_row % own)) & key_valid)
    early = prepared()
    rows = plan.rows
    for h in range(HEADS):
        low, high = head_window(h)
        chosen = head_lanes(h, low, high)
        queries = projected[:, low:high] * chosen
        keys = projected[:, D + low : D + high]
        values = projected[:, 2 * D + low : 2 * D + high]
        upstream = early[2, :, low:high] * chosen
        scores = jnp.where(allowed, dot_nt(keys, queries) * SCALE, NEGATIVE)
        peak = jnp.max(scores, axis=0, keepdims=True)
        raised = jnp.exp(scores - peak)
        total = jnp.sum(raised, axis=0, keepdims=True)
        probability = raised * (1.0 / total)
        weights[h * rows : (h + 1) * rows, :] = probability.astype(BF16)
        grad_weights = dot_nt(values, upstream)
        delta = jnp.sum(probability * grad_weights, axis=0, keepdims=True)
        slope = probability * (grad_weights - delta) * SCALE
        slopes[h * rows : (h + 1) * rows, :] = slope.astype(BF16)

    for c in range(CHUNKS):
        low, high = c * LANES, (c + 1) * LANES
        first, last = low // HEAD_DIM, (high - 1) // HEAD_DIM
        span = slice(first * rows, (last + 1) * rows)
        heads = range(first, last + 1)

        def stacked(tile):
            return jnp.concatenate([tile * head_lanes(h, low, high) for h in heads], axis=0)

        def beside(ref):
            return jnp.concatenate([ref[h * rows : (h + 1) * rows, :] for h in heads], axis=1)

        factors.ref[0, :, low:high] = dot_tn(
            weights[span, :], stacked(projected[:, 2 * D + low : 2 * D + high])
        ).astype(BF16)
        grads[:, low:high] = dot_tn(
            slopes[span, :], stacked(projected[:, D + low : D + high])
        ).astype(BF16)
        grads[:, D + low : D + high] = dot(
            beside(slopes), stacked(projected[:, low:high])
        ).astype(BF16)
        grads[:, 2 * D + low : 2 * D + high] = dot(
            beside(weights), stacked(early[2, :, low:high])
        ).astype(BF16)

    factors.flush(0)
    adjoint_rotated = dot_nt(grads[...], project_weight[...]).astype(BF16)
    factors.ref[2] = adjoint_rotated
    factors.flush(2)
    adjoint_normed = rotate_transposed(adjoint_rotated, inward().at[0])
    adjoint_hidden = early[0].astype(F32) + normalize_backward(adjoint_normed, normed, inverse)
    adjoint_hidden = adjoint_hidden.astype(BF16)
    inputs[...] = adjoint_hidden
    pairs = []
    for shift, piece in enumerate(leaving):
        start = pl.multiple_of(plan.other_frame(shift) * plan.own_rows, plan.own_rows)
        pairs.append((inputs.at[pl.ds(start, plan.own_rows), :], piece))
    piece_copies = start_all(pairs, piece_sems)
    outrot_adjoint = dot_nt(adjoint_hidden, out_weight[...]).astype(BF16)
    factors.ref[4] = outrot_adjoint
    factors.flush(4)
    adjoint_attended = rotate_transposed(outrot_adjoint, outward().at[0]).astype(BF16)
    for f in range(plan.frames):
        z, inner = divmod(f, plan.frames_local)
        base = z * plan.patch_ways + inner * plan.groups
        for g in range(plan.groups):
            start = plan.window_start(g)
            send_ref[base + g] = adjoint_attended[
                f * own : (f + 1) * own, start : start + plan.window
            ]
    wait_all(piece_copies)


def final_kernel(plan, *refs):
    pieces = refs[: plan.frame_ways]
    sums = refs[plan.frame_ways : plan.frame_ways + plan.patch_ways // 2]
    video_ref, video_gradient_ref, hidden = refs[plan.frame_ways + len(sums) :]
    size = plan.patches_local
    own = plan.own_patches
    for shift, piece in enumerate(pieces):
        source = plan.other_frame(plan.frame_ways - shift)
        start = pl.multiple_of(source * own, own)
        for f in range(plan.frames_local):
            hidden[f, pl.ds(start, own), :] = piece[f * own : (f + 1) * own, :]
    each = len(sums) // plan.frames_local
    for i in range(plan.frames_local):
        f = plan.frame_of(2 * i * each)
        normed, inverse = normalize(video_ref[f].astype(F32))
        adjoint = sums[i * each][0:size, :].astype(F32)
        for part in sums[i * each + 1 : (i + 1) * each]:
            adjoint = adjoint + part[0:size, :].astype(F32)
        video_gradient_ref[f] = (
            hidden[f].astype(F32) + normalize_backward(adjoint, normed, inverse)
        ).astype(BF16)


def share_kernel(plan, *refs):
    sums, out_ref = refs[:-1], refs[-1]
    size = plan.patches_local
    added = sums[0][size:, :].astype(F32)
    for part in sums[1:]:
        added = added + part[size:, :].astype(F32)
    out_ref[...] = added.astype(BF16)


def sum_kernel(plan, *refs):
    parts, (out_ref, total, turned) = refs[: plan.frame_ways], refs[plan.frame_ways :]
    added = parts[0][...].astype(F32)
    for part in parts[1:]:
        added = added + part[...].astype(F32)
    for k in range(plan.term_tiles):
        total[k * TILE : (k + 1) * TILE, :] = added[:, lanes_of(k)]
    turned[...] = jnp.zeros_like(turned)
    for b in range(plan.term_blocks):
        base = b * 4 * CHUNKS
        for i in range(LANES // BLOCK):
            turned[base + i * CHUNKS : base + (i + 1) * CHUNKS, :] = jnp.concatenate(
                [
                    total[
                        base + t * CHUNKS : base + (t + 1) * CHUNKS, i * BLOCK : (i + 1) * BLOCK
                    ]
                    for t in range(4)
                ],
                axis=1,
            )
    out_ref[...] = turned[...].astype(BF16)


def unpack_kernel(plan, scaling, *refs):
    pieces = refs[: plan.patch_ways]
    out_refs, wide = refs[plan.patch_ways : plan.patch_ways + 4], refs[plan.patch_ways + 4]
    blocks = 4 * CHUNKS
    row = lax.broadcasted_iota(jnp.int32, (blocks, blocks), 0)
    column = lax.broadcasted_iota(jnp.int32, (blocks, blocks), 1)
    order = (row % CHUNKS) * (LANES // BLOCK) + row // CHUNKS
    chosen = jnp.where(order == column, 1.0, 0.0).astype(BF16)
    for r, piece in enumerate(pieces):
        wide[r] = piece[...].astype(F32)
        for inner in range(plan.term_blocks):
            rows = wide[r, inner * blocks : (inner + 1) * blocks, :].astype(BF16)
            turned = dot_tn(rows, chosen) * scaling
            b = plan.peer(r) * plan.term_blocks + inner
            for t, out_ref in enumerate(out_refs):
                out_ref[b] = turned[t * BLOCK : (t + 1) * BLOCK, :]


def estimate(flops, moved):
    return pl.CostEstimate(flops=int(flops), bytes_accessed=int(moved), transcendentals=0)


def per_device(
    video,
    cotangent,
    frame_mask,
    spatial_project,
    spatial_output,
    temporal_project,
    temporal_output,
    spatial_inward,
    spatial_outward,
    temporal_inward,
    temporal_outward,
):
    plan = Plan(video.shape[0], video.shape[1], lax.axis_size("frame"), lax.axis_size("patch"))
    shape = jax.ShapeDtypeStruct
    both = ("frame", "patch")
    dma = pltpu.SemaphoreType.DMA
    exchange = lambda rows, axis: lax.all_to_all(rows, axis, 0, 0, tiled=True)
    mode = lambda kind, arrays: [(kind, array) for array in arrays]

    def shifted(pieces):
        ways = plan.frame_ways
        return [pieces[0]] + [
            lax.ppermute(pieces[s], "frame", [(i, (i + s) % ways) for i in range(ways)])
            for s in range(1, ways)
        ]

    half = plan.patch_ways // 2
    part_shape = shape((plan.patches_local + TILE, D), BF16)
    item_shape = shape((plan.devices, plan.own_patches, plan.window), BF16)

    def swap(rows, distance):
        pairs = [(p, p ^ distance) for p in range(plan.patch_ways)]
        return lax.ppermute(rows, "patch", pairs)

    own, *chips = [
        lax.dynamic_index_in_dim(video, plan.frame_of(distance), 0, keepdims=False)
        for distance in range(0, plan.patch_ways, 2)
    ]
    chips = [swap(rows, 2 * s) for s, rows in enumerate(chips, 1)]
    (early,) = call(
        functools.partial(pack_kernel, plan),
        mode("l", [video, cotangent]),
        [("v", shape((plan.frame_ways, 2, plan.own_rows, D), BF16))],
        limit=16,
    )
    def diagonals(width, *stacks):
        return call(
            blocks_kernel,
            mode("v", [blocks.reshape(D, BLOCK) for blocks in stacks]),
            mode("d", [shape((1, D, width), BF16)] * len(stacks)),
            limit=60,
        )

    (spatial_inward,) = diagonals(2 * LANES, spatial_inward)
    early = exchange(early, "frame")
    chips, spatial_inward = lax.optimization_barrier((chips, spatial_inward))
    gathered = [rows for piece in [own] + chips for rows in (piece, swap(piece, 1))]

    normed, stack, weights, send = call(
        functools.partial(spatial_forward_kernel, plan),
        mode("v", gathered) + [("l", spatial_inward), ("h", spatial_project)],
        [
            ("d", shape((1, plan.patches, D), BF16)),
            ("d", shape((3, plan.patches, plan.padded), BF16)),
            ("d", shape((plan.items * plan.parts, plan.patches, plan.part), BF16)),
            ("v", item_shape),
        ],
        [
            pltpu.VMEM((D, 3 * plan.window), BF16),
            pltpu.VMEM((plan.patches, plan.padded), BF16),
            dma((3,)),
        ],
        cost=estimate(8 * plan.items * plan.patches**2 * LANES, 8e6),
    )
    send, early, *stacks = lax.optimization_barrier(
        (send, early, spatial_outward, temporal_inward, temporal_outward)
    )
    arrived = exchange(send, both)
    spatial_outward, temporal_inward, temporal_outward = diagonals(LANES, *stacks)

    (prepared,) = call(
        functools.partial(top_kernel, plan),
        [("h", early), ("s", frame_mask), ("l", temporal_output), ("l", temporal_outward)],
        [("d", shape((3, plan.rows, D), BF16))],
        [pltpu.VMEM((plan.rows, D), BF16), dma((plan.frame_ways,))],
        cost=estimate(2 * plan.rows * D * D, 4e6),
    )

    send, factors, *leaving = call(
        functools.partial(temporal_kernel, plan),
        [
            ("h", early),
            ("v", arrived),
            ("s", frame_mask),
            ("l", spatial_outward),
            ("l", spatial_output),
            ("l", temporal_inward),
            ("h", temporal_project),
            ("p", prepared),
        ],
        [("v", item_shape), ("d", shape((5, plan.rows, D), BF16))]
        + mode("h", [shape((plan.own_rows, D), BF16)] * plan.frame_ways),
        [
            pltpu.VMEM((D, 3 * D), BF16),
            dma((len(SPANS),)),
            pltpu.VMEM((plan.rows, D), BF16),
            pltpu.VMEM((plan.rows, 3 * D), BF16),
            pltpu.VMEM((HEADS * plan.rows, plan.rows), BF16),
            pltpu.VMEM((HEADS * plan.rows, plan.rows), BF16),
            pltpu.VMEM((plan.rows, 3 * D), BF16),
            dma((plan.frame_ways,)),
        ],
        cost=estimate(16 * plan.rows * D * D, 12e6),
    )
    adjoint_items = exchange(send, both)
    ordered_shape = shape((plan.patch_ways * plan.term_tiles * TILE, LANES), F32)
    (terms,) = call(
        functools.partial(term_kernel, plan),
        [("h", prepared), ("l", factors)],
        [("d", shape((1,) + ordered_shape.shape, F32))],
        [
            pltpu.VMEM((plan.rows, D), BF16),
            pltpu.VMEM((3 * CHUNKS * BLOCK, LANES), F32),
            dma((1,)),
        ],
        cost=estimate(1e9, 4e6),
    )

    adjoint_items, terms = lax.optimization_barrier((adjoint_items, terms))
    even, odd = call(
        functools.partial(spatial_backward_kernel, plan),
        [
            ("v", adjoint_items),
            ("l", stack),
            ("l", weights),
            ("l", spatial_inward),
            ("l", normed),
            ("l", terms),
            ("h", spatial_project),
        ],
        mode("v", [shape((half,) + part_shape.shape, BF16)] * 2),
        [
            pltpu.VMEM((D, 3 * plan.window), BF16),
            pltpu.VMEM((plan.patches, plan.window), BF16),
            pltpu.VMEM((3, plan.patches, plan.padded), BF16),
            pltpu.VMEM((plan.patches, 3 * plan.window), BF16),
            pltpu.VMEM((CHUNKS * BLOCK, LANES), F32),
            dma((3,)),
        ],
        limit=52,
        cost=estimate(1e10, 8e6),
    )
    other = swap(odd, 1)
    sums = call(
        functools.partial(pair_kernel, plan),
        mode("v", [even, other]),
        mode("v", [part_shape] * half),
        limit=16,
    )
    sums = [swap(part, 2 * s) if s else part for s, part in enumerate(sums)]
    sums[1], leaving = lax.optimization_barrier((sums[1], leaving))
    leaving = shifted(leaving)
    (share,) = call(
        functools.partial(share_kernel, plan),
        mode("v", sums),
        [("v", shape((TILE, D), BF16))],
        limit=16,
    )
    shares = shifted([share] * plan.frame_ways)

    (video_gradient,) = call(
        functools.partial(final_kernel, plan),
        mode("v", leaving) + mode("v", sums) + [("v", video)],
        [("v", shape(video.shape, BF16))],
        [pltpu.VMEM(video.shape, BF16)],
        limit=16,
        cost=estimate(2e9, 3e6),
    )

    shares, video_gradient = lax.optimization_barrier((shares, video_gradient))
    share_shape = shape((plan.term_tiles * TILE, LANES), BF16)
    (send,) = call(
        functools.partial(sum_kernel, plan),
        mode("v", shares),
        [("v", share_shape)],
        [pltpu.VMEM(share_shape.shape, F32)] * 2,
        limit=16,
    )
    shared = [swap(send, r) if r else send for r in range(0, plan.patch_ways, 2)]
    shared = [rows for piece in shared for rows in (piece, swap(piece, 1))]
    scaling = 1.0 / math.sqrt(plan.tokens * plan.devices)
    block_shape = shape((BLOCK, BLOCK, D // BLOCK), F32)
    tout, tin, sout, sin = [
        blocks.transpose(2, 0, 1)
        for blocks in call(
            functools.partial(unpack_kernel, plan, scaling),
            mode("v", shared),
            mode("v", [block_shape] * 4),
            [pltpu.VMEM((plan.patch_ways,) + share_shape.shape, F32)],
            limit=16,
        )
    ]
    return (video_gradient, sin, sout, tin, tout)


def solution(mesh):
    in_specs = (P("frame", "patch", None), P("frame", "patch", None)) + (P(),) * 9
    out_specs = (P("frame", "patch", None), P(), P(), P(), P())
    return jax.shard_map(
        per_device, mesh=mesh, in_specs=in_specs, out_specs=out_specs, check_vma=False
    )
```

```python
import functools
import math

import jax
import jax.numpy as jnp
from jax import lax
from jax.experimental import pallas as pl
from jax.experimental.pallas import tpu as pltpu
from jax.sharding import PartitionSpec as P

D = 1152
HEADS = 16
HEAD_DIM = 72
BLOCK = 32
LANES = 128
TILE = 16
SPANS = ((0, 640), (640, 512))
CHUNKS = D // LANES
EPSILON = 1e-06
NEGATIVE = -1e30
SCALE = 1.0 / math.sqrt(HEAD_DIM)
F32 = jnp.float32
BF16 = jnp.bfloat16
VMEM = pl.BlockSpec(memory_space=pltpu.VMEM)
SMEM = pl.BlockSpec(memory_space=pltpu.SMEM)
HBM = pl.BlockSpec(memory_space=pltpu.HBM)
MIB = 1024 * 1024


def dot(a, b):
    return jnp.dot(a, b, preferred_element_type=F32)


def dot_nt(a, b):
    return lax.dot_general(a, b, (((1,), (1,)), ((), ())), preferred_element_type=F32)


def dot_tn(a, b):
    return lax.dot_general(a, b, (((0,), (0,)), ((), ())), preferred_element_type=F32)


def normalize(rows):
    average = jnp.mean(rows, axis=-1, keepdims=True)
    centered = rows - average
    variance = jnp.mean(centered * centered, axis=-1, keepdims=True)
    inverse = lax.rsqrt(variance + EPSILON)
    return centered * inverse, inverse


def normalize_backward(adjoint, normed, inverse):
    grad_mean = jnp.mean(adjoint, axis=-1, keepdims=True)
    grad_cross = jnp.mean(adjoint * normed, axis=-1, keepdims=True)
    return inverse * (adjoint - grad_mean - normed * grad_cross)


def diagonal_mask():
    row = lax.broadcasted_iota(jnp.int32, (LANES, LANES), 0)
    column = lax.broadcasted_iota(jnp.int32, (LANES, LANES), 1)
    return (row // BLOCK) == (column // BLOCK)


def lanes_of(chunk):
    return slice(chunk * LANES, (chunk + 1) * LANES)


def rotate(rows, blocks_ref):
    return jnp.concatenate(
        [dot(rows[:, lanes_of(c)], blocks_ref[lanes_of(c), :]) for c in range(CHUNKS)], axis=1
    )


def rotate_transposed(rows, blocks_ref):
    return jnp.concatenate(
        [dot_nt(rows[:, lanes_of(c)], blocks_ref[lanes_of(c), :]) for c in range(CHUNKS)], axis=1
    )


def rotation_gradient(left, right, mask, term_ref, base):
    for c in range(CHUNKS):
        full = jnp.where(mask, dot_tn(left[:, lanes_of(c)], right[:, lanes_of(c)]), 0.0)
        packed = full[0:BLOCK]
        for i in range(1, LANES // BLOCK):
            packed = packed + full[i * BLOCK : (i + 1) * BLOCK]
        term_ref[(base + c) * BLOCK : (base + c + 1) * BLOCK, :] = packed


class Arriving:
    def __init__(self, source, target, sem):
        self.target = target
        self.copy = pltpu.make_async_copy(source, target, sem)
        self.waited = False

    def begin(self):
        self.copy.start()

    def __call__(self):
        if not self.waited:
            self.copy.wait()
            self.waited = True
        return self.target


class Leaving:
    def __init__(self, source, target, sems):
        self.ref, self.target, self.sems = source, target, sems
        self.started = []

    def flush(self, *parts):
        for i in parts:
            copy = pltpu.make_async_copy(self.ref.at[i], self.target.at[i], self.sems.at[i])
            copy.start()
            self.started.append(copy)

    def finish(self):
        for copy in self.started:
            copy.wait()


def call(kernel, ins, outs, scratch=(), limit=60, cost=None):
    specs = {"v": VMEM, "s": SMEM, "h": HBM, "l": HBM, "p": HBM, "d": HBM}
    loads = [array for mode, array in ins if mode in "lp"]
    stores = [out for mode, out in outs if mode == "d"]
    staging = [pltpu.VMEM(array.shape, array.dtype) for array in loads + stores]
    staging += [pltpu.SemaphoreType.DMA] * len(loads)
    staging += [pltpu.SemaphoreType.DMA((out.shape[0],)) for out in stores]

    def body(*refs):
        given = list(refs[: len(ins) + len(outs)])
        own = refs[len(given) : len(given) + len(scratch)]
        staged = list(refs[len(given) + len(scratch) :])
        buffers, sems = staged[: len(loads) + len(stores)], staged[len(loads) + len(stores) :]
        leaving = []
        for i, (mode, _) in enumerate(list(ins) + list(outs)):
            if mode in "lp":
                given[i] = Arriving(given[i], buffers.pop(0), sems.pop(0))
                if mode == "l":
                    given[i].begin()
            elif mode == "d":
                given[i] = Leaving(buffers.pop(0), given[i], sems.pop(0))
                leaving.append(given[i])
        kernel(*given, *own)
        for out in leaving:
            out.finish()

    return pl.pallas_call(
        body,
        out_shape=tuple(out for _, out in outs),
        in_specs=[specs[mode] for mode, _ in ins],
        out_specs=tuple(specs[mode] for mode, _ in outs),
        scratch_shapes=list(scratch) + staging,
        compiler_params=pltpu.CompilerParams(vmem_limit_bytes=limit * MIB),
        cost_estimate=cost,
    )(*[array for _, array in ins])


def start_all(pairs, sems):
    copies = [
        pltpu.make_async_copy(source, target, sems.at[i]) for i, (source, target) in enumerate(pairs)
    ]
    for copy in copies:
        copy.start()
    return copies


def wait_all(copies):
    for copy in copies:
        copy.wait()


class Plan:
    def __init__(self, frames_local, patches_local, frame_ways, patch_ways):
        self.frames_local = frames_local
        self.patches_local = patches_local
        self.frame_ways = frame_ways
        self.patch_ways = patch_ways
        self.devices = frame_ways * patch_ways
        self.tokens = frames_local * patches_local
        self.frames = frames_local * frame_ways
        self.patches = patches_local * patch_ways
        self.items = frames_local * HEADS // patch_ways
        self.groups = HEADS // self.items
        self.width = self.items * HEAD_DIM
        self.window = max(
            -(-((g + 1) * self.width - g * self.width // LANES * LANES) // LANES) * LANES
            for g in range(self.groups)
        )
        self.padded = self.items * LANES
        self.own_patches = patches_local // frame_ways
        self.own_rows = frames_local * self.own_patches
        self.rows = self.frames * self.own_patches
        self.part = min(self.patches, 512)
        self.parts = self.patches // self.part
        self.term_blocks = BLOCK // patch_ways
        self.term_rows = 4 * CHUNKS * self.term_blocks
        self.term_tiles = -(-self.term_rows // TILE)

    def window_start(self, group):
        return min(group * self.width // LANES * LANES, D - self.window)

    def own_window(self):
        group = lax.rem(lax.axis_index("patch"), self.groups)
        start = jnp.minimum(group * self.width // LANES * LANES, D - self.window)
        return pl.multiple_of(start, LANES), group * self.width - start

    def peer(self, distance):
        return lax.axis_index("patch") ^ distance

    def frame_of(self, distance):
        return self.peer(distance) // self.groups

    def other_frame(self, shift):
        return lax.rem(lax.axis_index("frame") + shift, self.frame_ways)


def head_selection(plan, offset):
    lane = lax.broadcasted_iota(jnp.int32, (plan.window, plan.padded), 0)
    target = lax.broadcasted_iota(jnp.int32, (plan.window, plan.padded), 1)
    inner = target % LANES
    source = offset + (target // LANES) * HEAD_DIM + inner
    return jnp.where((lane == source) & (inner < HEAD_DIM), 1.0, 0.0).astype(BF16)


def weight_windows(plan, weight_ref, windows, sems):
    start, _ = plan.own_window()
    return [
        pltpu.make_async_copy(
            weight_ref.at[:, pl.ds(pl.multiple_of(s * D + start, LANES), plan.window)],
            windows.at[:, pl.ds(s * plan.window, plan.window)],
            sems.at[s],
        )
        for s in range(3)
    ]


def pack_kernel(plan, video, cotangent, early_ref):
    own = plan.own_patches
    for t, source in enumerate((video(), cotangent())):
        for z in range(plan.frame_ways):
            for f in range(plan.frames_local):
                early_ref[z, t, f * own : (f + 1) * own, :] = source[
                    f, z * own : (z + 1) * own, :
                ]


def blocks_kernel(*refs):
    mask = diagonal_mask()
    for blocks_ref, out in zip(refs[: len(refs) // 2], refs[len(refs) // 2 :]):
        for c in range(CHUNKS):
            tiled = jnp.concatenate([blocks_ref[lanes_of(c), :]] * (LANES // BLOCK), axis=1)
            out.ref[0, lanes_of(c), :] = jnp.where(mask, tiled, 0.0).astype(BF16)
        out.flush(0)


def spatial_forward_kernel(plan, *refs):
    pieces = refs[: plan.patch_ways]
    (
        blocks,
        weight_ref,
        normed_out,
        stack_out,
        weights_out,
        inverse_out,
        attended_out,
        send_ref,
        windows,
        sems,
    ) = refs[plan.patch_ways :]
    attended = attended_out.ref.at[0]
    copies = weight_windows(plan, weight_ref, windows, sems)
    for copy in copies:
        copy.start()
    _, offset = plan.own_window()
    chosen = head_selection(plan, offset)
    size = plan.patches_local
    for r, piece in enumerate(pieces):
        for i in range(0, size, BLOCK):
            normed = normalize(piece[i : i + BLOCK, :].astype(F32))[0].astype(BF16)
            normed_out.ref[0, r * size + i : r * size + i + BLOCK, :] = normed
    normed_out.flush(0)
    rotated = rotate(normed_out.ref[0], blocks().at[0]).astype(BF16)
    stack_ref = stack_out.ref
    wait_all(copies)
    projected = dot(rotated, windows[...]).astype(BF16)
    for s in range(3):
        part = projected[:, s * plan.window : (s + 1) * plan.window]
        stack_ref[s] = dot(part, chosen).astype(BF16)
        stack_out.flush(s)
    for h in range(plan.items):
        queries, keys, values = [stack_ref[s, :, lanes_of(h)] for s in range(3)]
        values_t = values.astype(F32).T.astype(BF16)
        for c in range(plan.parts):
            span = slice(c * plan.part, (c + 1) * plan.part)
            scores = dot_nt(keys, queries[span]) * SCALE
            top = jnp.max(scores, axis=0, keepdims=True)
            raised = jnp.exp(scores - top)
            inverse = 1.0 / jnp.sum(raised, axis=0, keepdims=True)
            rounded = raised.astype(BF16)
            weights_out.ref[h * plan.parts + c] = rounded
            weights_out.flush(h * plan.parts + c)
            inverse_out.ref[h * plan.parts + c] = jnp.broadcast_to(inverse, (8, plan.part))
            attended[span, lanes_of(h)] = (dot(values_t, rounded) * inverse).T.astype(BF16)
    inverse_out.flush(*range(plan.items * plan.parts))
    attended_out.flush(0)
    own = plan.own_patches
    result = dot_nt(attended[...], chosen).astype(BF16)
    for r in range(plan.patch_ways):
        target = plan.peer(r)
        for z in range(plan.frame_ways):
            start = r * size + z * own
            send_ref[z * plan.patch_ways + target] = result[start : start + own, :]


def order_terms(plan, terms, ordered, first, count):
    share = plan.term_tiles * TILE
    for b in range(BLOCK):
        owner, inner = divmod(b, plan.term_blocks)
        start = owner * share + inner * 4 * CHUNKS + first
        ordered[start : start + count, :] = terms[pl.ds(b, count, stride=BLOCK), :]


def term_kernel(plan, prepared_ref, factors, out, outrot, terms, sems):
    copies = start_all([(prepared_ref.at[1], outrot)], sems)
    mask = diagonal_mask()
    parts = factors()
    rotation_gradient(parts[1], parts[2], mask, terms, CHUNKS)
    rotation_gradient(parts[3], parts[4], mask, terms, 2 * CHUNKS)
    wait_all(copies)
    rotation_gradient(parts[0], outrot[...], mask, terms, 0)
    ordered = out.ref.at[0]
    ordered[...] = jnp.zeros_like(ordered)
    order_terms(plan, terms, ordered, 0, 3 * CHUNKS)
    out.flush(0)


def spatial_backward_kernel(
    plan,
    adjoint_items,
    stack,
    inverses,
    attended,
    weights,
    blocks,
    normed,
    term,
    weight_ref,
    even_ref,
    odd_ref,
    windows,
    adjoint,
    grads,
    projected,
    terms,
    sems,
):
    copies = weight_windows(plan, weight_ref, windows, sems)
    for copy in copies:
        copy.start()
    own = plan.own_patches
    adjoint_ref = adjoint_items()
    for r in range(plan.patch_ways):
        source = plan.peer(r)
        for z in range(plan.frame_ways):
            start = r * plan.patches_local + z * own
            adjoint[start : start + own, :] = adjoint_ref[z * plan.patch_ways + source]
    _, offset = plan.own_window()
    chosen = head_selection(plan, offset)
    upstream_all = dot(adjoint[...], chosen).astype(BF16)
    stack_ref, inverse_ref, attended_ref = stack(), inverses(), attended()
    weights_ref = weights()
    for h in range(plan.items):
        queries, keys, values = [stack_ref[s, :, lanes_of(h)] for s in range(3)]
        upstream = upstream_all[:, lanes_of(h)]
        keys_t = keys.astype(F32).T.astype(BF16)
        grad_keys = None
        grad_values = None
        for c in range(plan.parts):
            span = slice(c * plan.part, (c + 1) * plan.part)
            rounded = weights_ref[h * plan.parts + c]
            inverse = inverse_ref[h * plan.parts + c]
            wide = upstream[span].astype(F32)
            scaled = (wide * inverse.T[:, 0:1]).astype(BF16)
            overlap = (wide * attended_ref[0, span, lanes_of(h)].astype(F32)).T
            delta = jnp.sum(overlap, axis=0, keepdims=True) * inverse[0:1]
            grad_weights = dot_nt(values, scaled)
            grad_scores = (rounded.astype(F32) * (grad_weights - delta)).astype(BF16)
            value_part = dot(rounded, scaled)
            key_part = dot(grad_scores, queries[span])
            grad_values = value_part if grad_values is None else grad_values + value_part
            grad_keys = key_part if grad_keys is None else grad_keys + key_part
            grads[0, span, lanes_of(h)] = (dot(keys_t, grad_scores).T * SCALE).astype(BF16)
        grads[1, :, lanes_of(h)] = (grad_keys * SCALE).astype(BF16)
        grads[2, :, lanes_of(h)] = grad_values.astype(BF16)
    for s, copy in enumerate(copies):
        projected[:, s * plan.window : (s + 1) * plan.window] = dot_nt(grads[s], chosen).astype(
            BF16
        )
        copy.wait()
    rotated = dot_nt(projected[...], windows[...]).astype(BF16)
    size = plan.patches_local
    share = plan.term_tiles * TILE
    back = rotate_transposed(rotated, blocks().at[0]).astype(BF16)
    rotation_gradient(normed()[0], rotated, diagonal_mask(), terms, 0)
    ordered = term().at[0]
    order_terms(plan, terms, ordered, 3 * CHUNKS, CHUNKS)
    for r in range(plan.patch_ways):
        out_ref = (even_ref, odd_ref)[r % 2].at[r // 2]
        out_ref[0:size, :] = back[r * size : (r + 1) * size, :]
        owned = ordered[pl.ds(pl.multiple_of(plan.peer(r) * share, TILE), share), :].astype(BF16)
        for k in range(CHUNKS):
            if k < plan.term_tiles:
                tile = owned[k * TILE : (k + 1) * TILE, :]
            else:
                tile = jnp.zeros((TILE, LANES), BF16)
            out_ref[size : size + TILE, lanes_of(k)] = tile


def pair_kernel(plan, even_ref, other_ref, *out_refs):
    for s, out_ref in enumerate(out_refs):
        out_ref[...] = (even_ref[s].astype(F32) + other_ref[s].astype(F32)).astype(BF16)


def frame_column(plan, mask_ref):
    frame = lax.broadcasted_iota(jnp.int32, (plan.rows, 1), 0) // plan.own_patches
    valid = jnp.zeros((plan.rows, 1), jnp.int32)
    for f in range(plan.frames):
        valid = jnp.where(frame == f, mask_ref[f], valid)
    return valid


def collect_rows(plan, early_ref, which, target):
    return [
        (early_ref.at[z, which], target.at[pl.ds(z * plan.own_rows, plan.own_rows), :])
        for z in range(plan.frame_ways)
    ]


def top_kernel(plan, early_ref, mask_ref, weight, blocks, out, rows, sems):
    copies = start_all(collect_rows(plan, early_ref, 1, rows), sems)
    valid = frame_column(plan, mask_ref).astype(F32)
    wait_all(copies)
    top = (rows[...].astype(F32) * valid).astype(BF16)
    out.ref[0] = top
    out.flush(0)
    outrot = dot_nt(top, weight()[...]).astype(BF16)
    out.ref[1] = outrot
    out.flush(1)
    out.ref[2] = rotate_transposed(outrot, blocks().at[0]).astype(BF16)
    out.flush(2)


def head_window(h):
    low = h * HEAD_DIM // LANES * LANES
    high = -(-(h + 1) * HEAD_DIM // LANES) * LANES
    return low, high


def head_lanes(h, low, high):
    lane = low + lax.broadcasted_iota(jnp.int32, (1, high - low), 1)
    inside = (lane >= h * HEAD_DIM) & (lane < (h + 1) * HEAD_DIM)
    return jnp.where(inside, 1.0, 0.0).astype(BF16)


def temporal_kernel(plan, *refs):
    (
        early_ref,
        arrived,
        mask_ref,
        outward,
        spatial_output,
        inward,
        project_ref,
        prepared,
        send_ref,
        factors,
    ) = refs[:10]
    leaving = refs[10 : 10 + plan.frame_ways]
    (
        project_weight,
        weight_sems,
        inputs,
        projected,
        weights,
        slopes,
        grads,
        piece_sems,
    ) = refs[10 + plan.frame_ways :]
    piece_copies = start_all(collect_rows(plan, early_ref, 0, inputs), piece_sems)
    weight_copies = start_all(
        [(project_ref.at[pl.ds(*span), :], project_weight.at[pl.ds(*span), :]) for span in SPANS],
        weight_sems,
    )
    prepared.begin()
    own = plan.own_patches
    attended_one = factors.ref.at[3]
    arrived_ref = arrived()
    for f in range(plan.frames):
        z, inner = divmod(f, plan.frames_local)
        base = z * plan.patch_ways + inner * plan.groups
        for c in range(CHUNKS):
            tile = None
            for g in range(plan.groups):
                low = c * LANES - plan.window_start(g)
                if 0 <= low < plan.window:
                    part = arrived_ref[base + g, :, low : low + LANES]
                    tile = part if tile is None else tile + part
            attended_one[f * own : (f + 1) * own, lanes_of(c)] = tile
    factors.flush(3)
    outrot_one = rotate(attended_one[...], outward().at[0]).astype(BF16)
    out_weight = spatial_output()
    wait_all(piece_copies)
    hidden = (inputs[...].astype(F32) + dot(outrot_one, out_weight[...])).astype(BF16)
    normed, inverse = normalize(hidden.astype(F32))
    normed_low = normed.astype(BF16)
    factors.ref[1] = normed_low
    factors.flush(1)
    rotated = rotate(normed_low, inward().at[0]).astype(BF16)
    total = None
    for (start, size), copy in zip(SPANS, weight_copies):
        copy.wait()
        span = slice(start, start + size)
        part = dot(rotated[:, span], project_weight[span, :])
        total = part if total is None else total + part
    projected[...] = total.astype(BF16)

    key_valid = frame_column(plan, mask_ref) == 1
    shape = (plan.rows, plan.rows)
    key_row = lax.broadcasted_iota(jnp.int32, shape, 0)
    query_row = lax.broadcasted_iota(jnp.int32, shape, 1)
    allowed = (key_row == query_row) | (((key_row % own) == (query_row % own)) & key_valid)
    early = prepared()
    rows = plan.rows
    for h in range(HEADS):
        low, high = head_window(h)
        chosen = head_lanes(h, low, high)
        queries = projected[:, low:high] * chosen
        keys = projected[:, D + low : D + high]
        values = projected[:, 2 * D + low : 2 * D + high]
        upstream = early[2, :, low:high] * chosen
        scores = jnp.where(allowed, dot_nt(keys, queries) * SCALE, NEGATIVE)
        peak = jnp.max(scores, axis=0, keepdims=True)
        raised = jnp.exp(scores - peak)
        total = jnp.sum(raised, axis=0, keepdims=True)
        probability = raised * (1.0 / total)
        weights[h * rows : (h + 1) * rows, :] = probability.astype(BF16)
        grad_weights = dot_nt(values, upstream)
        delta = jnp.sum(probability * grad_weights, axis=0, keepdims=True)
        slope = probability * (grad_weights - delta) * SCALE
        slopes[h * rows : (h + 1) * rows, :] = slope.astype(BF16)

    for c in range(CHUNKS):
        low, high = c * LANES, (c + 1) * LANES
        first, last = low // HEAD_DIM, (high - 1) // HEAD_DIM
        span = slice(first * rows, (last + 1) * rows)
        heads = range(first, last + 1)

        def stacked(tile):
            return jnp.concatenate([tile * head_lanes(h, low, high) for h in heads], axis=0)

        def beside(ref):
            return jnp.concatenate([ref[h * rows : (h + 1) * rows, :] for h in heads], axis=1)

        factors.ref[0, :, low:high] = dot_tn(
            weights[span, :], stacked(projected[:, 2 * D + low : 2 * D + high])
        ).astype(BF16)
        grads[:, low:high] = dot_tn(
            slopes[span, :], stacked(projected[:, D + low : D + high])
        ).astype(BF16)
        grads[:, D + low : D + high] = dot(
            beside(slopes), stacked(projected[:, low:high])
        ).astype(BF16)
        grads[:, 2 * D + low : 2 * D + high] = dot(
            beside(weights), stacked(early[2, :, low:high])
        ).astype(BF16)

    factors.flush(0)
    adjoint_rotated = dot_nt(grads[...], project_weight[...]).astype(BF16)
    factors.ref[2] = adjoint_rotated
    factors.flush(2)
    adjoint_normed = rotate_transposed(adjoint_rotated, inward().at[0])
    adjoint_hidden = early[0].astype(F32) + normalize_backward(adjoint_normed, normed, inverse)
    adjoint_hidden = adjoint_hidden.astype(BF16)
    inputs[...] = adjoint_hidden
    pairs = []
    for shift, piece in enumerate(leaving):
        start = pl.multiple_of(plan.other_frame(shift) * plan.own_rows, plan.own_rows)
        pairs.append((inputs.at[pl.ds(start, plan.own_rows), :], piece))
    piece_copies = start_all(pairs, piece_sems)
    outrot_adjoint = dot_nt(adjoint_hidden, out_weight[...]).astype(BF16)
    factors.ref[4] = outrot_adjoint
    factors.flush(4)
    adjoint_attended = rotate_transposed(outrot_adjoint, outward().at[0]).astype(BF16)
    for f in range(plan.frames):
        z, inner = divmod(f, plan.frames_local)
        base = z * plan.patch_ways + inner * plan.groups
        for g in range(plan.groups):
            start = plan.window_start(g)
            send_ref[base + g] = adjoint_attended[
                f * own : (f + 1) * own, start : start + plan.window
            ]
    wait_all(piece_copies)


def final_kernel(plan, *refs):
    pieces = refs[: plan.frame_ways]
    sums = refs[plan.frame_ways : plan.frame_ways + plan.patch_ways // 2]
    video_ref, video_gradient_ref, hidden = refs[plan.frame_ways + len(sums) :]
    size = plan.patches_local
    own = plan.own_patches
    for shift, piece in enumerate(pieces):
        source = plan.other_frame(plan.frame_ways - shift)
        start = pl.multiple_of(source * own, own)
        for f in range(plan.frames_local):
            hidden[f, pl.ds(start, own), :] = piece[f * own : (f + 1) * own, :]
    each = len(sums) // plan.frames_local
    for i in range(plan.frames_local):
        f = plan.frame_of(2 * i * each)
        normed, inverse = normalize(video_ref[f].astype(F32))
        adjoint = sums[i * each][0:size, :].astype(F32)
        for part in sums[i * each + 1 : (i + 1) * each]:
            adjoint = adjoint + part[0:size, :].astype(F32)
        video_gradient_ref[f] = (
            hidden[f].astype(F32) + normalize_backward(adjoint, normed, inverse)
        ).astype(BF16)


def share_kernel(plan, *refs):
    sums, out_ref = refs[:-1], refs[-1]
    size = plan.patches_local
    added = sums[0][size:, :].astype(F32)
    for part in sums[1:]:
        added = added + part[size:, :].astype(F32)
    out_ref[...] = added.astype(BF16)


def sum_kernel(plan, *refs):
    parts, (out_ref, total, turned) = refs[: plan.frame_ways], refs[plan.frame_ways :]
    added = parts[0][...].astype(F32)
    for part in parts[1:]:
        added = added + part[...].astype(F32)
    for k in range(plan.term_tiles):
        total[k * TILE : (k + 1) * TILE, :] = added[:, lanes_of(k)]
    turned[...] = jnp.zeros_like(turned)
    for b in range(plan.term_blocks):
        base = b * 4 * CHUNKS
        for i in range(LANES // BLOCK):
            turned[base + i * CHUNKS : base + (i + 1) * CHUNKS, :] = jnp.concatenate(
                [
                    total[
                        base + t * CHUNKS : base + (t + 1) * CHUNKS, i * BLOCK : (i + 1) * BLOCK
                    ]
                    for t in range(4)
                ],
                axis=1,
            )
    out_ref[...] = turned[...].astype(BF16)


def unpack_kernel(plan, scaling, *refs):
    pieces = refs[: plan.patch_ways]
    out_refs, wide = refs[plan.patch_ways : plan.patch_ways + 4], refs[plan.patch_ways + 4]
    blocks = 4 * CHUNKS
    row = lax.broadcasted_iota(jnp.int32, (blocks, blocks), 0)
    column = lax.broadcasted_iota(jnp.int32, (blocks, blocks), 1)
    order = (row % CHUNKS) * (LANES // BLOCK) + row // CHUNKS
    chosen = jnp.where(order == column, 1.0, 0.0).astype(BF16)
    for r, piece in enumerate(pieces):
        wide[r] = piece[...].astype(F32)
        for inner in range(plan.term_blocks):
            rows = wide[r, inner * blocks : (inner + 1) * blocks, :].astype(BF16)
            turned = dot_tn(rows, chosen) * scaling
            b = plan.peer(r) * plan.term_blocks + inner
            for t, out_ref in enumerate(out_refs):
                out_ref[b] = turned[t * BLOCK : (t + 1) * BLOCK, :]


def estimate(flops, moved):
    return pl.CostEstimate(flops=int(flops), bytes_accessed=int(moved), transcendentals=0)


def per_device(
    video,
    cotangent,
    frame_mask,
    spatial_project,
    spatial_output,
    temporal_project,
    temporal_output,
    spatial_inward,
    spatial_outward,
    temporal_inward,
    temporal_outward,
):
    plan = Plan(video.shape[0], video.shape[1], lax.axis_size("frame"), lax.axis_size("patch"))
    shape = jax.ShapeDtypeStruct
    both = ("frame", "patch")
    dma = pltpu.SemaphoreType.DMA
    exchange = lambda rows, axis: lax.all_to_all(rows, axis, 0, 0, tiled=True)
    mode = lambda kind, arrays: [(kind, array) for array in arrays]

    def shifted(pieces):
        ways = plan.frame_ways
        return [pieces[0]] + [
            lax.ppermute(pieces[s], "frame", [(i, (i + s) % ways) for i in range(ways)])
            for s in range(1, ways)
        ]

    half = plan.patch_ways // 2
    part_shape = shape((plan.patches_local + TILE, D), BF16)
    item_shape = shape((plan.devices, plan.own_patches, plan.window), BF16)

    def swap(rows, distance):
        pairs = [(p, p ^ distance) for p in range(plan.patch_ways)]
        return lax.ppermute(rows, "patch", pairs)

    own, *chips = [
        lax.dynamic_index_in_dim(video, plan.frame_of(distance), 0, keepdims=False)
        for distance in range(0, plan.patch_ways, 2)
    ]
    chips = [swap(rows, 2 * s) for s, rows in enumerate(chips, 1)]
    (early,) = call(
        functools.partial(pack_kernel, plan),
        mode("l", [video, cotangent]),
        [("v", shape((plan.frame_ways, 2, plan.own_rows, D), BF16))],
        limit=62,
    )
    def diagonals(*stacks):
        return call(
            blocks_kernel,
            mode("v", [blocks.reshape(D, BLOCK) for blocks in stacks]),
            mode("d", [shape((1, D, LANES), BF16)] * len(stacks)),
            limit=16,
        )

    (spatial_inward,) = diagonals(spatial_inward)
    early = exchange(early, "frame")
    chips, spatial_inward = lax.optimization_barrier((chips, spatial_inward))
    gathered = [rows for piece in [own] + chips for rows in (piece, swap(piece, 1))]

    normed, stack, weights, inverses, attended, send = call(
        functools.partial(spatial_forward_kernel, plan),
        mode("v", gathered) + [("l", spatial_inward), ("h", spatial_project)],
        [
            ("d", shape((1, plan.patches, D), BF16)),
            ("d", shape((3, plan.patches, plan.padded), BF16)),
            ("d", shape((plan.items * plan.parts, plan.patches, plan.part), BF16)),
            ("d", shape((plan.items * plan.parts, 8, plan.part), F32)),
            ("d", shape((1, plan.patches, plan.padded), BF16)),
            ("v", item_shape),
        ],
        [
            pltpu.VMEM((D, 3 * plan.window), BF16),
            dma((3,)),
        ],
        cost=estimate(8 * plan.items * plan.patches**2 * LANES, 8e6),
    )
    send, early, *stacks = lax.optimization_barrier(
        (send, early, spatial_outward, temporal_inward, temporal_outward)
    )
    arrived = exchange(send, both)
    spatial_outward, temporal_inward, temporal_outward = diagonals(*stacks)

    (prepared,) = call(
        functools.partial(top_kernel, plan),
        [("h", early), ("s", frame_mask), ("l", temporal_output), ("l", temporal_outward)],
        [("d", shape((3, plan.rows, D), BF16))],
        [pltpu.VMEM((plan.rows, D), BF16), dma((plan.frame_ways,))],
        cost=estimate(2 * plan.rows * D * D, 4e6),
    )

    send, factors, *leaving = call(
        functools.partial(temporal_kernel, plan),
        [
            ("h", early),
            ("l", arrived),
            ("s", frame_mask),
            ("l", spatial_outward),
            ("l", spatial_output),
            ("l", temporal_inward),
            ("h", temporal_project),
            ("p", prepared),
        ],
        [("v", item_shape), ("d", shape((5, plan.rows, D), BF16))]
        + mode("h", [shape((plan.own_rows, D), BF16)] * plan.frame_ways),
        [
            pltpu.VMEM((D, 3 * D), BF16),
            dma((len(SPANS),)),
            pltpu.VMEM((plan.rows, D), BF16),
            pltpu.VMEM((plan.rows, 3 * D), BF16),
            pltpu.VMEM((HEADS * plan.rows, plan.rows), BF16),
            pltpu.VMEM((HEADS * plan.rows, plan.rows), BF16),
            pltpu.VMEM((plan.rows, 3 * D), BF16),
            dma((plan.frame_ways,)),
        ],
        cost=estimate(16 * plan.rows * D * D, 12e6),
    )
    adjoint_items = exchange(send, both)
    ordered_shape = shape((plan.patch_ways * plan.term_tiles * TILE, LANES), F32)
    (terms,) = call(
        functools.partial(term_kernel, plan),
        [("h", prepared), ("l", factors)],
        [("d", shape((1,) + ordered_shape.shape, F32))],
        [
            pltpu.VMEM((plan.rows, D), BF16),
            pltpu.VMEM((3 * CHUNKS * BLOCK, LANES), F32),
            dma((1,)),
        ],
        cost=estimate(1e9, 4e6),
    )

    adjoint_items, terms = lax.optimization_barrier((adjoint_items, terms))
    even, odd = call(
        functools.partial(spatial_backward_kernel, plan),
        [
            ("l", adjoint_items),
            ("l", stack),
            ("l", inverses),
            ("l", attended),
            ("l", weights),
            ("l", spatial_inward),
            ("l", normed),
            ("l", terms),
            ("h", spatial_project),
        ],
        mode("v", [shape((half,) + part_shape.shape, BF16)] * 2),
        [
            pltpu.VMEM((D, 3 * plan.window), BF16),
            pltpu.VMEM((plan.patches, plan.window), BF16),
            pltpu.VMEM((3, plan.patches, plan.padded), BF16),
            pltpu.VMEM((plan.patches, 3 * plan.window), BF16),
            pltpu.VMEM((CHUNKS * BLOCK, LANES), F32),
            dma((3,)),
        ],
        limit=52,
        cost=estimate(1e10, 8e6),
    )
    other = swap(odd, 1)
    sums = call(
        functools.partial(pair_kernel, plan),
        mode("v", [even, other]),
        mode("v", [part_shape] * half),
        limit=16,
    )
    sums = [swap(part, 2 * s) if s else part for s, part in enumerate(sums)]
    sums[1], leaving = lax.optimization_barrier((sums[1], leaving))
    leaving = shifted(leaving)
    (share,) = call(
        functools.partial(share_kernel, plan),
        mode("v", sums),
        [("v", shape((TILE, D), BF16))],
        limit=16,
    )
    shares = shifted([share] * plan.frame_ways)

    (video_gradient,) = call(
        functools.partial(final_kernel, plan),
        mode("v", leaving) + mode("v", sums) + [("v", video)],
        [("v", shape(video.shape, BF16))],
        [pltpu.VMEM(video.shape, BF16)],
        limit=16,
        cost=estimate(2e9, 3e6),
    )

    shares, video_gradient = lax.optimization_barrier((shares, video_gradient))
    share_shape = shape((plan.term_tiles * TILE, LANES), BF16)
    (send,) = call(
        functools.partial(sum_kernel, plan),
        mode("v", shares),
        [("v", share_shape)],
        [pltpu.VMEM(share_shape.shape, F32)] * 2,
        limit=16,
    )
    shared = [swap(send, r) if r else send for r in range(0, plan.patch_ways, 2)]
    shared = [rows for piece in shared for rows in (piece, swap(piece, 1))]
    scaling = 1.0 / math.sqrt(plan.tokens * plan.devices)
    block_shape = shape((BLOCK, BLOCK, D // BLOCK), F32)
    tout, tin, sout, sin = [
        blocks.transpose(2, 0, 1)
        for blocks in call(
            functools.partial(unpack_kernel, plan, scaling),
            mode("v", shared),
            mode("v", [block_shape] * 4),
            [pltpu.VMEM((plan.patch_ways,) + share_shape.shape, F32)],
            limit=16,
        )
    ]
    return (video_gradient, sin, sout, tin, tout)


def solution(mesh):
    in_specs = (P("frame", "patch", None), P("frame", "patch", None)) + (P(),) * 9
    out_specs = (P("frame", "patch", None), P(), P(), P(), P())
    return jax.shard_map(
        per_device, mesh=mesh, in_specs=in_specs, out_specs=out_specs, check_vma=False
    )
```

```python
import functools
import math

import jax
import jax.numpy as jnp
from jax import lax
from jax.experimental import pallas as pl
from jax.experimental.pallas import tpu as pltpu
from jax.sharding import PartitionSpec as P

D = 1152
HEADS = 16
HEAD_DIM = 72
BLOCK = 32
LANES = 128
TILE = 16
SPANS = ((0, 640), (640, 512))
CHUNKS = D // LANES
EPSILON = 1e-06
NEGATIVE = -1e30
SCALE = 1.0 / math.sqrt(HEAD_DIM)
F32 = jnp.float32
BF16 = jnp.bfloat16
VMEM = pl.BlockSpec(memory_space=pltpu.VMEM)
SMEM = pl.BlockSpec(memory_space=pltpu.SMEM)
HBM = pl.BlockSpec(memory_space=pltpu.HBM)
MIB = 1024 * 1024


def dot(a, b):
    return jnp.dot(a, b, preferred_element_type=F32)


def dot_nt(a, b):
    return lax.dot_general(a, b, (((1,), (1,)), ((), ())), preferred_element_type=F32)


def dot_tn(a, b):
    return lax.dot_general(a, b, (((0,), (0,)), ((), ())), preferred_element_type=F32)


def normalize(rows):
    average = jnp.mean(rows, axis=-1, keepdims=True)
    centered = rows - average
    variance = jnp.mean(centered * centered, axis=-1, keepdims=True)
    inverse = lax.rsqrt(variance + EPSILON)
    return centered * inverse, inverse


def normalize_backward(adjoint, normed, inverse):
    grad_mean = jnp.mean(adjoint, axis=-1, keepdims=True)
    grad_cross = jnp.mean(adjoint * normed, axis=-1, keepdims=True)
    return inverse * (adjoint - grad_mean - normed * grad_cross)


def diagonal_mask():
    row = lax.broadcasted_iota(jnp.int32, (LANES, LANES), 0)
    column = lax.broadcasted_iota(jnp.int32, (LANES, LANES), 1)
    return (row // BLOCK) == (column // BLOCK)


def lanes_of(chunk):
    return slice(chunk * LANES, (chunk + 1) * LANES)


def rotate(rows, blocks_ref):
    return jnp.concatenate(
        [dot(rows[:, lanes_of(c)], blocks_ref[lanes_of(c), :]) for c in range(CHUNKS)], axis=1
    )


def rotate_transposed(rows, blocks_ref):
    return jnp.concatenate(
        [dot_nt(rows[:, lanes_of(c)], blocks_ref[lanes_of(c), :]) for c in range(CHUNKS)], axis=1
    )


def rotation_gradient(left, right, mask, term_ref, base):
    for c in range(CHUNKS):
        full = jnp.where(mask, dot_tn(left[:, lanes_of(c)], right[:, lanes_of(c)]), 0.0)
        packed = full[0:BLOCK]
        for i in range(1, LANES // BLOCK):
            packed = packed + full[i * BLOCK : (i + 1) * BLOCK]
        term_ref[(base + c) * BLOCK : (base + c + 1) * BLOCK, :] = packed


class Arriving:
    def __init__(self, source, target, sem):
        self.target = target
        self.copy = pltpu.make_async_copy(source, target, sem)
        self.waited = False

    def begin(self):
        self.copy.start()

    def __call__(self):
        if not self.waited:
            self.copy.wait()
            self.waited = True
        return self.target


class Leaving:
    def __init__(self, source, target, sems):
        self.ref, self.target, self.sems = source, target, sems
        self.started = []

    def flush(self, *parts):
        for i in parts:
            copy = pltpu.make_async_copy(self.ref.at[i], self.target.at[i], self.sems.at[i])
            copy.start()
            self.started.append(copy)

    def finish(self):
        for copy in self.started:
            copy.wait()


def call(kernel, ins, outs, scratch=(), limit=60, cost=None):
    specs = {"v": VMEM, "s": SMEM, "h": HBM, "l": HBM, "p": HBM, "d": HBM}
    loads = [array for mode, array in ins if mode in "lp"]
    stores = [out for mode, out in outs if mode == "d"]
    staging = [pltpu.VMEM(array.shape, array.dtype) for array in loads + stores]
    staging += [pltpu.SemaphoreType.DMA] * len(loads)
    staging += [pltpu.SemaphoreType.DMA((out.shape[0],)) for out in stores]

    def body(*refs):
        given = list(refs[: len(ins) + len(outs)])
        own = refs[len(given) : len(given) + len(scratch)]
        staged = list(refs[len(given) + len(scratch) :])
        buffers, sems = staged[: len(loads) + len(stores)], staged[len(loads) + len(stores) :]
        leaving = []
        for i, (mode, _) in enumerate(list(ins) + list(outs)):
            if mode in "lp":
                given[i] = Arriving(given[i], buffers.pop(0), sems.pop(0))
                if mode == "l":
                    given[i].begin()
            elif mode == "d":
                given[i] = Leaving(buffers.pop(0), given[i], sems.pop(0))
                leaving.append(given[i])
        kernel(*given, *own)
        for out in leaving:
            out.finish()

    return pl.pallas_call(
        body,
        out_shape=tuple(out for _, out in outs),
        in_specs=[specs[mode] for mode, _ in ins],
        out_specs=tuple(specs[mode] for mode, _ in outs),
        scratch_shapes=list(scratch) + staging,
        compiler_params=pltpu.CompilerParams(vmem_limit_bytes=limit * MIB),
        cost_estimate=cost,
    )(*[array for _, array in ins])


def start_all(pairs, sems):
    copies = [
        pltpu.make_async_copy(source, target, sems.at[i]) for i, (source, target) in enumerate(pairs)
    ]
    for copy in copies:
        copy.start()
    return copies


def wait_all(copies):
    for copy in copies:
        copy.wait()


class Plan:
    def __init__(self, frames_local, patches_local, frame_ways, patch_ways):
        self.frames_local = frames_local
        self.patches_local = patches_local
        self.frame_ways = frame_ways
        self.patch_ways = patch_ways
        self.devices = frame_ways * patch_ways
        self.tokens = frames_local * patches_local
        self.frames = frames_local * frame_ways
        self.patches = patches_local * patch_ways
        self.items = frames_local * HEADS // patch_ways
        self.groups = HEADS // self.items
        self.width = self.items * HEAD_DIM
        self.window = max(
            -(-((g + 1) * self.width - g * self.width // LANES * LANES) // LANES) * LANES
            for g in range(self.groups)
        )
        self.padded = self.items * LANES
        self.own_patches = patches_local // frame_ways
        self.own_rows = frames_local * self.own_patches
        self.rows = self.frames * self.own_patches
        self.part = min(self.patches, 512)
        self.parts = self.patches // self.part
        self.term_blocks = BLOCK // patch_ways
        self.term_rows = 4 * CHUNKS * self.term_blocks
        self.term_tiles = -(-self.term_rows // TILE)

    def window_start(self, group):
        return min(group * self.width // LANES * LANES, D - self.window)

    def own_window(self):
        group = lax.rem(lax.axis_index("patch"), self.groups)
        start = jnp.minimum(group * self.width // LANES * LANES, D - self.window)
        return pl.multiple_of(start, LANES), group * self.width - start

    def peer(self, distance):
        return lax.axis_index("patch") ^ distance

    def frame_of(self, distance):
        return self.peer(distance) // self.groups

    def other_frame(self, shift):
        return lax.rem(lax.axis_index("frame") + shift, self.frame_ways)


def head_selection(plan, offset):
    lane = lax.broadcasted_iota(jnp.int32, (plan.window, plan.padded), 0)
    target = lax.broadcasted_iota(jnp.int32, (plan.window, plan.padded), 1)
    inner = target % LANES
    source = offset + (target // LANES) * HEAD_DIM + inner
    return jnp.where((lane == source) & (inner < HEAD_DIM), 1.0, 0.0).astype(BF16)


def weight_windows(plan, weight_ref, windows, sems):
    start, _ = plan.own_window()
    return [
        pltpu.make_async_copy(
            weight_ref.at[:, pl.ds(pl.multiple_of(s * D + start, LANES), plan.window)],
            windows.at[:, pl.ds(s * plan.window, plan.window)],
            sems.at[s],
        )
        for s in range(3)
    ]


def pack_kernel(plan, video, cotangent, early_ref):
    own = plan.own_patches
    for t, source in enumerate((video(), cotangent())):
        for z in range(plan.frame_ways):
            for f in range(plan.frames_local):
                early_ref[z, t, f * own : (f + 1) * own, :] = source[
                    f, z * own : (z + 1) * own, :
                ]


def blocks_kernel(*refs):
    mask = diagonal_mask()
    for blocks_ref, out in zip(refs[: len(refs) // 2], refs[len(refs) // 2 :]):
        for c in range(CHUNKS):
            tiled = jnp.concatenate([blocks_ref[lanes_of(c), :]] * (LANES // BLOCK), axis=1)
            out.ref[0, lanes_of(c), :] = jnp.where(mask, tiled, 0.0).astype(BF16)
        out.flush(0)


def spatial_forward_kernel(plan, *refs):
    pieces = refs[: plan.patch_ways]
    (
        blocks,
        weight_ref,
        normed_out,
        stack_out,
        weights_out,
        send_ref,
        windows,
        attended,
        sems,
    ) = refs[plan.patch_ways :]
    copies = weight_windows(plan, weight_ref, windows, sems)
    for copy in copies:
        copy.start()
    _, offset = plan.own_window()
    chosen = head_selection(plan, offset)
    size = plan.patches_local
    for r, piece in enumerate(pieces):
        rows = piece()
        for i in range(0, size, BLOCK):
            normed = normalize(rows[i : i + BLOCK, :].astype(F32))[0].astype(BF16)
            normed_out.ref[0, r * size + i : r * size + i + BLOCK, :] = normed
    normed_out.flush(0)
    rotated = rotate(normed_out.ref[0], blocks().at[0]).astype(BF16)
    stack_ref = stack_out.ref
    wait_all(copies)
    projected = dot(rotated, windows[...]).astype(BF16)
    for s in range(3):
        part = projected[:, s * plan.window : (s + 1) * plan.window]
        stack_ref[s] = dot(part, chosen).astype(BF16)
        stack_out.flush(s)
    for h in range(plan.items):
        queries, keys, values = [stack_ref[s, :, lanes_of(h)] for s in range(3)]
        values_t = values.astype(F32).T.astype(BF16)
        for c in range(plan.parts):
            span = slice(c * plan.part, (c + 1) * plan.part)
            scores = dot_nt(keys, queries[span]) * SCALE
            top = jnp.max(scores, axis=0, keepdims=True)
            raised = jnp.exp(scores - top)
            total = jnp.sum(raised, axis=0, keepdims=True)
            rounded = (raised * (1.0 / total)).astype(BF16)
            weights_out.ref[h * plan.parts + c] = rounded
            weights_out.flush(h * plan.parts + c)
            attended[span, lanes_of(h)] = dot(values_t, rounded).T.astype(BF16)
    own = plan.own_patches
    result = dot_nt(attended[...], chosen).astype(BF16)
    for r in range(plan.patch_ways):
        target = plan.peer(r)
        for z in range(plan.frame_ways):
            start = r * size + z * own
            send_ref[z * plan.patch_ways + target] = result[start : start + own, :]


def order_terms(plan, terms, ordered, first, count):
    share = plan.term_tiles * TILE
    for b in range(BLOCK):
        owner, inner = divmod(b, plan.term_blocks)
        start = owner * share + inner * 4 * CHUNKS + first
        ordered[start : start + count, :] = terms[pl.ds(b, count, stride=BLOCK), :]


def term_kernel(plan, prepared_ref, factors, out, outrot, terms, sems):
    copies = start_all([(prepared_ref.at[1], outrot)], sems)
    mask = diagonal_mask()
    parts = factors()
    rotation_gradient(parts[1], parts[2], mask, terms, CHUNKS)
    rotation_gradient(parts[3], parts[4], mask, terms, 2 * CHUNKS)
    wait_all(copies)
    rotation_gradient(parts[0], outrot[...], mask, terms, 0)
    ordered = out.ref.at[0]
    ordered[...] = jnp.zeros_like(ordered)
    order_terms(plan, terms, ordered, 0, 3 * CHUNKS)
    out.flush(0)


def spatial_backward_kernel(
    plan,
    adjoint_items,
    stack,
    weights,
    blocks,
    normed,
    term,
    weight_ref,
    even_out,
    odd_out,
    windows,
    adjoint,
    grads,
    projected,
    terms,
    sems,
):
    copies = weight_windows(plan, weight_ref, windows, sems)
    for copy in copies:
        copy.start()
    own = plan.own_patches
    adjoint_ref = adjoint_items()
    for r in range(plan.patch_ways):
        source = plan.peer(r)
        for z in range(plan.frame_ways):
            start = r * plan.patches_local + z * own
            adjoint[start : start + own, :] = adjoint_ref[z * plan.patch_ways + source]
    _, offset = plan.own_window()
    chosen = head_selection(plan, offset)
    upstream_all = dot(adjoint[...], chosen).astype(BF16)
    stack_ref, weights_ref = stack(), weights()
    for h in range(plan.items):
        queries, keys, values = [stack_ref[s, :, lanes_of(h)] for s in range(3)]
        upstream = upstream_all[:, lanes_of(h)]
        keys_t = keys.astype(F32).T.astype(BF16)
        grad_keys = None
        grad_values = None
        for c in range(plan.parts):
            span = slice(c * plan.part, (c + 1) * plan.part)
            rounded = weights_ref[h * plan.parts + c]
            probability = rounded.astype(F32)
            grad_weights = dot_nt(values, upstream[span])
            delta = jnp.sum(probability * grad_weights, axis=0, keepdims=True)
            grad_scores = (probability * (grad_weights - delta)).astype(BF16)
            value_part = dot(rounded, upstream[span])
            key_part = dot(grad_scores, queries[span])
            grad_values = value_part if grad_values is None else grad_values + value_part
            grad_keys = key_part if grad_keys is None else grad_keys + key_part
            grads[0, span, lanes_of(h)] = (dot(keys_t, grad_scores).T * SCALE).astype(BF16)
        grads[1, :, lanes_of(h)] = (grad_keys * SCALE).astype(BF16)
        grads[2, :, lanes_of(h)] = grad_values.astype(BF16)
    for s, copy in enumerate(copies):
        projected[:, s * plan.window : (s + 1) * plan.window] = dot_nt(grads[s], chosen).astype(
            BF16
        )
        copy.wait()
    rotated = dot_nt(projected[...], windows[...]).astype(BF16)
    size = plan.patches_local
    share = plan.term_tiles * TILE
    rotation_gradient(normed()[0], rotated, diagonal_mask(), terms, 0)
    ordered = term().at[0]
    order_terms(plan, terms, ordered, 3 * CHUNKS, CHUNKS)
    back = rotate_transposed(rotated, blocks().at[0]).astype(BF16)
    for r in list(range(1, plan.patch_ways, 2)) + list(range(0, plan.patch_ways, 2)):
        out = (even_out, odd_out)[r % 2]
        out_ref = out.ref.at[r // 2]
        out_ref[0:size, :] = back[r * size : (r + 1) * size, :]
        owned = ordered[pl.ds(pl.multiple_of(plan.peer(r) * share, TILE), share), :].astype(BF16)
        for k in range(CHUNKS):
            if k < plan.term_tiles:
                tile = owned[k * TILE : (k + 1) * TILE, :]
            else:
                tile = jnp.zeros((TILE, LANES), BF16)
            out_ref[size : size + TILE, lanes_of(k)] = tile
        out.flush(r // 2)


def pair_kernel(plan, even_ref, other_ref, *out_refs):
    for s, out_ref in enumerate(out_refs):
        out_ref[...] = (even_ref[s].astype(F32) + other_ref[s].astype(F32)).astype(BF16)


def frame_column(plan, mask_ref):
    frame = lax.broadcasted_iota(jnp.int32, (plan.rows, 1), 0) // plan.own_patches
    valid = jnp.zeros((plan.rows, 1), jnp.int32)
    for f in range(plan.frames):
        valid = jnp.where(frame == f, mask_ref[f], valid)
    return valid


def collect_rows(plan, early_ref, which, target):
    return [
        (early_ref.at[z, which], target.at[pl.ds(z * plan.own_rows, plan.own_rows), :])
        for z in range(plan.frame_ways)
    ]


def top_kernel(plan, early_ref, mask_ref, weight, blocks, out, rows, sems):
    copies = start_all(collect_rows(plan, early_ref, 1, rows), sems)
    valid = frame_column(plan, mask_ref).astype(F32)
    wait_all(copies)
    top = (rows[...].astype(F32) * valid).astype(BF16)
    out.ref[0] = top
    out.flush(0)
    outrot = dot_nt(top, weight()[...]).astype(BF16)
    out.ref[1] = outrot
    out.flush(1)
    out.ref[2] = rotate_transposed(outrot, blocks().at[0]).astype(BF16)
    out.flush(2)


def head_window(h):
    low = h * HEAD_DIM // LANES * LANES
    high = -(-(h + 1) * HEAD_DIM // LANES) * LANES
    return low, high


def head_lanes(h, low, high):
    lane = low + lax.broadcasted_iota(jnp.int32, (1, high - low), 1)
    inside = (lane >= h * HEAD_DIM) & (lane < (h + 1) * HEAD_DIM)
    return jnp.where(inside, 1.0, 0.0).astype(BF16)


def temporal_kernel(plan, *refs):
    (
        early_ref,
        arrived,
        mask_ref,
        outward,
        spatial_output,
        inward,
        project_ref,
        prepared,
        send_ref,
        factors,
    ) = refs[:10]
    leaving = refs[10 : 10 + plan.frame_ways]
    (
        project_weight,
        weight_sems,
        inputs,
        projected,
        weights,
        slopes,
        grads,
        piece_sems,
    ) = refs[10 + plan.frame_ways :]
    piece_copies = start_all(collect_rows(plan, early_ref, 0, inputs), piece_sems)
    weight_copies = start_all(
        [(project_ref.at[pl.ds(*span), :], project_weight.at[pl.ds(*span), :]) for span in SPANS],
        weight_sems,
    )
    own = plan.own_patches
    attended_one = factors.ref.at[3]
    arrived_ref = arrived()
    for f in range(plan.frames):
        z, inner = divmod(f, plan.frames_local)
        base = z * plan.patch_ways + inner * plan.groups
        for c in range(CHUNKS):
            tile = None
            for g in range(plan.groups):
                low = c * LANES - plan.window_start(g)
                if 0 <= low < plan.window:
                    part = arrived_ref[base + g, :, low : low + LANES]
                    tile = part if tile is None else tile + part
            attended_one[f * own : (f + 1) * own, lanes_of(c)] = tile
    factors.flush(3)
    outrot_one = rotate(attended_one[...], outward().at[0]).astype(BF16)
    out_weight = spatial_output()
    wait_all(piece_copies)
    hidden = (inputs[...].astype(F32) + dot(outrot_one, out_weight[...])).astype(BF16)
    normed, inverse = normalize(hidden.astype(F32))
    normed_low = normed.astype(BF16)
    factors.ref[1] = normed_low
    factors.flush(1)
    rotated = rotate(normed_low, inward().at[0]).astype(BF16)
    total = None
    for (start, size), copy in zip(SPANS, weight_copies):
        copy.wait()
        span = slice(start, start + size)
        if start == 0:
            prepared.begin()
        part = dot(rotated[:, span], project_weight[span, :])
        total = part if total is None else total + part
    projected[...] = total.astype(BF16)

    key_valid = frame_column(plan, mask_ref) == 1
    shape = (plan.rows, plan.rows)
    key_row = lax.broadcasted_iota(jnp.int32, shape, 0)
    query_row = lax.broadcasted_iota(jnp.int32, shape, 1)
    allowed = (key_row == query_row) | (((key_row % own) == (query_row % own)) & key_valid)
    early = prepared()
    rows = plan.rows
    for h in range(HEADS):
        low, high = head_window(h)
        chosen = head_lanes(h, low, high)
        queries = projected[:, low:high] * chosen
        keys = projected[:, D + low : D + high]
        values = projected[:, 2 * D + low : 2 * D + high]
        upstream = early[2, :, low:high] * chosen
        scores = jnp.where(allowed, dot_nt(keys, queries) * SCALE, NEGATIVE)
        peak = jnp.max(scores, axis=0, keepdims=True)
        raised = jnp.exp(scores - peak)
        total = jnp.sum(raised, axis=0, keepdims=True)
        probability = raised * (1.0 / total)
        weights[h * rows : (h + 1) * rows, :] = probability.astype(BF16)
        grad_weights = dot_nt(values, upstream)
        delta = jnp.sum(probability * grad_weights, axis=0, keepdims=True)
        slope = probability * (grad_weights - delta) * SCALE
        slopes[h * rows : (h + 1) * rows, :] = slope.astype(BF16)

    for c in range(CHUNKS):
        low, high = c * LANES, (c + 1) * LANES
        first, last = low // HEAD_DIM, (high - 1) // HEAD_DIM
        span = slice(first * rows, (last + 1) * rows)
        heads = range(first, last + 1)

        def stacked(tile):
            return jnp.concatenate([tile * head_lanes(h, low, high) for h in heads], axis=0)

        def beside(ref):
            return jnp.concatenate([ref[h * rows : (h + 1) * rows, :] for h in heads], axis=1)

        factors.ref[0, :, low:high] = dot_tn(
            weights[span, :], stacked(projected[:, 2 * D + low : 2 * D + high])
        ).astype(BF16)
        grads[:, low:high] = dot_tn(
            slopes[span, :], stacked(projected[:, D + low : D + high])
        ).astype(BF16)
        grads[:, D + low : D + high] = dot(
            beside(slopes), stacked(projected[:, low:high])
        ).astype(BF16)
        grads[:, 2 * D + low : 2 * D + high] = dot(
            beside(weights), stacked(early[2, :, low:high])
        ).astype(BF16)

    factors.flush(0)
    adjoint_rotated = dot_nt(grads[...], project_weight[...]).astype(BF16)
    factors.ref[2] = adjoint_rotated
    factors.flush(2)
    adjoint_normed = rotate_transposed(adjoint_rotated, inward().at[0])
    adjoint_hidden = early[0].astype(F32) + normalize_backward(adjoint_normed, normed, inverse)
    adjoint_hidden = adjoint_hidden.astype(BF16)
    inputs[...] = adjoint_hidden
    pairs = []
    for shift, piece in enumerate(leaving):
        start = pl.multiple_of(plan.other_frame(shift) * plan.own_rows, plan.own_rows)
        pairs.append((inputs.at[pl.ds(start, plan.own_rows), :], piece))
    piece_copies = start_all(pairs, piece_sems)
    outrot_adjoint = dot_nt(adjoint_hidden, out_weight[...]).astype(BF16)
    factors.ref[4] = outrot_adjoint
    factors.flush(4)
    adjoint_attended = rotate_transposed(outrot_adjoint, outward().at[0]).astype(BF16)
    for f in range(plan.frames):
        z, inner = divmod(f, plan.frames_local)
        base = z * plan.patch_ways + inner * plan.groups
        for g in range(plan.groups):
            start = plan.window_start(g)
            send_ref[base + g] = adjoint_attended[
                f * own : (f + 1) * own, start : start + plan.window
            ]
    wait_all(piece_copies)


def final_kernel(plan, *refs):
    pieces = refs[: plan.frame_ways]
    sums = refs[plan.frame_ways : plan.frame_ways + plan.patch_ways // 2]
    video_ref, video_gradient_ref, hidden = refs[plan.frame_ways + len(sums) :]
    size = plan.patches_local
    own = plan.own_patches
    for shift, piece in enumerate(pieces):
        source = plan.other_frame(plan.frame_ways - shift)
        start = pl.multiple_of(source * own, own)
        for f in range(plan.frames_local):
            hidden[f, pl.ds(start, own), :] = piece[f * own : (f + 1) * own, :]
    each = len(sums) // plan.frames_local
    for i in range(plan.frames_local):
        f = plan.frame_of(2 * i * each)
        normed, inverse = normalize(video_ref[f].astype(F32))
        adjoint = sums[i * each][0:size, :].astype(F32)
        for part in sums[i * each + 1 : (i + 1) * each]:
            adjoint = adjoint + part[0:size, :].astype(F32)
        video_gradient_ref[f] = (
            hidden[f].astype(F32) + normalize_backward(adjoint, normed, inverse)
        ).astype(BF16)


def share_kernel(plan, *refs):
    sums, out_ref = refs[:-1], refs[-1]
    size = plan.patches_local
    added = sums[0][size:, :].astype(F32)
    for part in sums[1:]:
        added = added + part[size:, :].astype(F32)
    out_ref[...] = added.astype(BF16)


def sum_kernel(plan, *refs):
    parts, (out_ref, total, turned) = refs[: plan.frame_ways], refs[plan.frame_ways :]
    added = parts[0][...].astype(F32)
    for part in parts[1:]:
        added = added + part[...].astype(F32)
    for k in range(plan.term_tiles):
        total[k * TILE : (k + 1) * TILE, :] = added[:, lanes_of(k)]
    turned[...] = jnp.zeros_like(turned)
    for b in range(plan.term_blocks):
        base = b * 4 * CHUNKS
        for i in range(LANES // BLOCK):
            turned[base + i * CHUNKS : base + (i + 1) * CHUNKS, :] = jnp.concatenate(
                [
                    total[
                        base + t * CHUNKS : base + (t + 1) * CHUNKS, i * BLOCK : (i + 1) * BLOCK
                    ]
                    for t in range(4)
                ],
                axis=1,
            )
    out_ref[...] = turned[...].astype(BF16)


def unpack_kernel(plan, scaling, *refs):
    pieces = refs[: plan.patch_ways]
    out_refs, wide = refs[plan.patch_ways : plan.patch_ways + 4], refs[plan.patch_ways + 4]
    blocks = 4 * CHUNKS
    row = lax.broadcasted_iota(jnp.int32, (blocks, blocks), 0)
    column = lax.broadcasted_iota(jnp.int32, (blocks, blocks), 1)
    order = (row % CHUNKS) * (LANES // BLOCK) + row // CHUNKS
    chosen = jnp.where(order == column, 1.0, 0.0).astype(BF16)
    for r, piece in enumerate(pieces):
        wide[r] = piece[...].astype(F32)
        for inner in range(plan.term_blocks):
            rows = wide[r, inner * blocks : (inner + 1) * blocks, :].astype(BF16)
            turned = dot_tn(rows, chosen) * scaling
            b = plan.peer(r) * plan.term_blocks + inner
            for t, out_ref in enumerate(out_refs):
                out_ref[b] = turned[t * BLOCK : (t + 1) * BLOCK, :]


def estimate(flops, moved):
    return pl.CostEstimate(flops=int(flops), bytes_accessed=int(moved), transcendentals=0)


def per_device(
    video,
    cotangent,
    frame_mask,
    spatial_project,
    spatial_output,
    temporal_project,
    temporal_output,
    spatial_inward,
    spatial_outward,
    temporal_inward,
    temporal_outward,
):
    plan = Plan(video.shape[0], video.shape[1], lax.axis_size("frame"), lax.axis_size("patch"))
    shape = jax.ShapeDtypeStruct
    both = ("frame", "patch")
    dma = pltpu.SemaphoreType.DMA
    exchange = lambda rows, axis: lax.all_to_all(rows, axis, 0, 0, tiled=True)
    mode = lambda kind, arrays: [(kind, array) for array in arrays]

    def shifted(pieces):
        ways = plan.frame_ways
        return [pieces[0]] + [
            lax.ppermute(pieces[s], "frame", [(i, (i + s) % ways) for i in range(ways)])
            for s in range(1, ways)
        ]

    half = plan.patch_ways // 2
    part_shape = shape((plan.patches_local + TILE, D), BF16)
    item_shape = shape((plan.devices, plan.own_patches, plan.window), BF16)

    def swap(rows, distance):
        pairs = [(p, p ^ distance) for p in range(plan.patch_ways)]
        return lax.ppermute(rows, "patch", pairs)

    own, *chips = [
        lax.dynamic_index_in_dim(video, plan.frame_of(distance), 0, keepdims=False)
        for distance in range(0, plan.patch_ways, 2)
    ]
    chips = [swap(rows, 2 * s) for s, rows in enumerate(chips, 1)]
    (early,) = call(
        functools.partial(pack_kernel, plan),
        mode("l", [video, cotangent]),
        [("v", shape((plan.frame_ways, 2, plan.own_rows, D), BF16))],
        limit=62,
    )
    def diagonals(*stacks):
        return call(
            blocks_kernel,
            mode("v", [blocks.reshape(D, BLOCK) for blocks in stacks]),
            mode("d", [shape((1, D, LANES), BF16)] * len(stacks)),
            limit=16,
        )

    (spatial_inward,) = diagonals(spatial_inward)
    early = exchange(early, "frame")
    chips, spatial_inward = lax.optimization_barrier((chips, spatial_inward))
    gathered = [rows for piece in [own] + chips for rows in (piece, swap(piece, 1))]

    normed, stack, weights, send = call(
        functools.partial(spatial_forward_kernel, plan),
        mode("l", gathered) + [("l", spatial_inward), ("h", spatial_project)],
        [
            ("d", shape((1, plan.patches, D), BF16)),
            ("d", shape((3, plan.patches, plan.padded), BF16)),
            ("d", shape((plan.items * plan.parts, plan.patches, plan.part), BF16)),
            ("v", item_shape),
        ],
        [
            pltpu.VMEM((D, 3 * plan.window), BF16),
            pltpu.VMEM((plan.patches, plan.padded), BF16),
            dma((3,)),
        ],
        cost=estimate(8 * plan.items * plan.patches**2 * LANES, 8e6),
    )
    send, early, *stacks = lax.optimization_barrier(
        (send, early, spatial_outward, temporal_inward, temporal_outward)
    )
    arrived = exchange(send, both)
    spatial_outward, temporal_inward, temporal_outward = diagonals(*stacks)

    (prepared,) = call(
        functools.partial(top_kernel, plan),
        [("h", early), ("s", frame_mask), ("l", temporal_output), ("l", temporal_outward)],
        [("d", shape((3, plan.rows, D), BF16))],
        [pltpu.VMEM((plan.rows, D), BF16), dma((plan.frame_ways,))],
        cost=estimate(2 * plan.rows * D * D, 4e6),
    )

    send, factors, *leaving = call(
        functools.partial(temporal_kernel, plan),
        [
            ("h", early),
            ("l", arrived),
            ("s", frame_mask),
            ("l", spatial_outward),
            ("l", spatial_output),
            ("l", temporal_inward),
            ("h", temporal_project),
            ("p", prepared),
        ],
        [("v", item_shape), ("d", shape((5, plan.rows, D), BF16))]
        + mode("h", [shape((plan.own_rows, D), BF16)] * plan.frame_ways),
        [
            pltpu.VMEM((D, 3 * D), BF16),
            dma((len(SPANS),)),
            pltpu.VMEM((plan.rows, D), BF16),
            pltpu.VMEM((plan.rows, 3 * D), BF16),
            pltpu.VMEM((HEADS * plan.rows, plan.rows), BF16),
            pltpu.VMEM((HEADS * plan.rows, plan.rows), BF16),
            pltpu.VMEM((plan.rows, 3 * D), BF16),
            dma((plan.frame_ways,)),
        ],
        cost=estimate(16 * plan.rows * D * D, 12e6),
    )
    adjoint_items = exchange(send, both)
    ordered_shape = shape((plan.patch_ways * plan.term_tiles * TILE, LANES), F32)
    (terms,) = call(
        functools.partial(term_kernel, plan),
        [("h", prepared), ("l", factors)],
        [("d", shape((1,) + ordered_shape.shape, F32))],
        [
            pltpu.VMEM((plan.rows, D), BF16),
            pltpu.VMEM((3 * CHUNKS * BLOCK, LANES), F32),
            dma((1,)),
        ],
        cost=estimate(1e9, 4e6),
    )

    adjoint_items, terms = lax.optimization_barrier((adjoint_items, terms))
    even, odd = call(
        functools.partial(spatial_backward_kernel, plan),
        [
            ("l", adjoint_items),
            ("l", stack),
            ("l", weights),
            ("l", spatial_inward),
            ("l", normed),
            ("l", terms),
            ("h", spatial_project),
        ],
        mode("d", [shape((half,) + part_shape.shape, BF16)] * 2),
        [
            pltpu.VMEM((D, 3 * plan.window), BF16),
            pltpu.VMEM((plan.patches, plan.window), BF16),
            pltpu.VMEM((3, plan.patches, plan.padded), BF16),
            pltpu.VMEM((plan.patches, 3 * plan.window), BF16),
            pltpu.VMEM((CHUNKS * BLOCK, LANES), F32),
            dma((3,)),
        ],
        limit=52,
        cost=estimate(1e10, 8e6),
    )
    other = swap(odd, 1)
    sums = call(
        functools.partial(pair_kernel, plan),
        mode("v", [even, other]),
        mode("v", [part_shape] * half),
        limit=16,
    )
    sums = [swap(part, 2 * s) if s else part for s, part in enumerate(sums)]
    sums[1], leaving = lax.optimization_barrier((sums[1], leaving))
    leaving = shifted(leaving)
    (share,) = call(
        functools.partial(share_kernel, plan),
        mode("v", sums),
        [("v", shape((TILE, D), BF16))],
        limit=16,
    )
    shares = shifted([share] * plan.frame_ways)

    (video_gradient,) = call(
        functools.partial(final_kernel, plan),
        mode("v", leaving) + mode("v", sums) + [("v", video)],
        [("v", shape(video.shape, BF16))],
        [pltpu.VMEM(video.shape, BF16)],
        limit=16,
        cost=estimate(2e9, 3e6),
    )

    shares, video_gradient = lax.optimization_barrier((shares, video_gradient))
    share_shape = shape((plan.term_tiles * TILE, LANES), BF16)
    (send,) = call(
        functools.partial(sum_kernel, plan),
        mode("v", shares),
        [("v", share_shape)],
        [pltpu.VMEM(share_shape.shape, F32)] * 2,
        limit=16,
    )
    shared = [swap(send, r) if r else send for r in range(0, plan.patch_ways, 2)]
    shared = [rows for piece in shared for rows in (piece, swap(piece, 1))]
    scaling = 1.0 / math.sqrt(plan.tokens * plan.devices)
    block_shape = shape((BLOCK, BLOCK, D // BLOCK), F32)
    tout, tin, sout, sin = [
        blocks.transpose(2, 0, 1)
        for blocks in call(
            functools.partial(unpack_kernel, plan, scaling),
            mode("v", shared),
            mode("v", [block_shape] * 4),
            [pltpu.VMEM((plan.patch_ways,) + share_shape.shape, F32)],
            limit=16,
        )
    ]
    return (video_gradient, sin, sout, tin, tout)


def solution(mesh):
    in_specs = (P("frame", "patch", None), P("frame", "patch", None)) + (P(),) * 9
    out_specs = (P("frame", "patch", None), P(), P(), P(), P())
    return jax.shard_map(
        per_device, mesh=mesh, in_specs=in_specs, out_specs=out_specs, check_vma=False
    )
```

```python
import functools
import math

import jax
import jax.numpy as jnp
from jax import lax
from jax.experimental import pallas as pl
from jax.experimental.pallas import tpu as pltpu
from jax.sharding import PartitionSpec as P

D = 1152
HEADS = 16
HEAD_DIM = 72
BLOCK = 32
LANES = 128
TILE = 16
SPANS = ((0, 640), (640, 512))
CHUNKS = D // LANES
EPSILON = 1e-06
NEGATIVE = -1e30
SCALE = 1.0 / math.sqrt(HEAD_DIM)
F32 = jnp.float32
BF16 = jnp.bfloat16
VMEM = pl.BlockSpec(memory_space=pltpu.VMEM)
SMEM = pl.BlockSpec(memory_space=pltpu.SMEM)
HBM = pl.BlockSpec(memory_space=pltpu.HBM)
MIB = 1024 * 1024


def dot(a, b):
    return jnp.dot(a, b, preferred_element_type=F32)


def dot_nt(a, b):
    return lax.dot_general(a, b, (((1,), (1,)), ((), ())), preferred_element_type=F32)


def dot_tn(a, b):
    return lax.dot_general(a, b, (((0,), (0,)), ((), ())), preferred_element_type=F32)


def normalize(rows):
    average = jnp.mean(rows, axis=-1, keepdims=True)
    centered = rows - average
    variance = jnp.mean(centered * centered, axis=-1, keepdims=True)
    inverse = lax.rsqrt(variance + EPSILON)
    return centered * inverse, inverse


def normalize_backward(adjoint, normed, inverse):
    grad_mean = jnp.mean(adjoint, axis=-1, keepdims=True)
    grad_cross = jnp.mean(adjoint * normed, axis=-1, keepdims=True)
    return inverse * (adjoint - grad_mean - normed * grad_cross)


def diagonal_mask():
    row = lax.broadcasted_iota(jnp.int32, (LANES, LANES), 0)
    column = lax.broadcasted_iota(jnp.int32, (LANES, LANES), 1)
    return (row // BLOCK) == (column // BLOCK)


def lanes_of(chunk):
    return slice(chunk * LANES, (chunk + 1) * LANES)


def rotate(rows, blocks_ref):
    return jnp.concatenate(
        [dot(rows[:, lanes_of(c)], blocks_ref[lanes_of(c), :]) for c in range(CHUNKS)], axis=1
    )


def rotate_transposed(rows, blocks_ref):
    return jnp.concatenate(
        [dot_nt(rows[:, lanes_of(c)], blocks_ref[lanes_of(c), :]) for c in range(CHUNKS)], axis=1
    )


def rotation_gradient(left, right, mask, term_ref, base):
    for c in range(CHUNKS):
        full = jnp.where(mask, dot_tn(left[:, lanes_of(c)], right[:, lanes_of(c)]), 0.0)
        packed = full[0:BLOCK]
        for i in range(1, LANES // BLOCK):
            packed = packed + full[i * BLOCK : (i + 1) * BLOCK]
        term_ref[(base + c) * BLOCK : (base + c + 1) * BLOCK, :] = packed


class Arriving:
    def __init__(self, source, target, sem):
        self.target = target
        self.copy = pltpu.make_async_copy(source, target, sem)
        self.waited = False

    def begin(self):
        self.copy.start()

    def __call__(self):
        if not self.waited:
            self.copy.wait()
            self.waited = True
        return self.target


class Leaving:
    def __init__(self, source, target, sems):
        self.ref, self.target, self.sems = source, target, sems
        self.started = []

    def flush(self, *parts):
        for i in parts:
            copy = pltpu.make_async_copy(self.ref.at[i], self.target.at[i], self.sems.at[i])
            copy.start()
            self.started.append(copy)

    def flush_span(self, start, size, i):
        span = pl.ds(start, size)
        copy = pltpu.make_async_copy(self.ref.at[span], self.target.at[span], self.sems.at[i])
        copy.start()
        self.started.append(copy)

    def finish(self):
        for copy in self.started:
            copy.wait()


def call(kernel, ins, outs, scratch=(), limit=60, cost=None):
    specs = {"v": VMEM, "s": SMEM, "h": HBM, "l": HBM, "p": HBM, "d": HBM}
    loads = [array for mode, array in ins if mode in "lp"]
    stores = [out for mode, out in outs if mode == "d"]
    staging = [pltpu.VMEM(array.shape, array.dtype) for array in loads + stores]
    staging += [pltpu.SemaphoreType.DMA] * len(loads)
    staging += [pltpu.SemaphoreType.DMA((out.shape[0],)) for out in stores]

    def body(*refs):
        given = list(refs[: len(ins) + len(outs)])
        own = refs[len(given) : len(given) + len(scratch)]
        staged = list(refs[len(given) + len(scratch) :])
        buffers, sems = staged[: len(loads) + len(stores)], staged[len(loads) + len(stores) :]
        leaving = []
        for i, (mode, _) in enumerate(list(ins) + list(outs)):
            if mode in "lp":
                given[i] = Arriving(given[i], buffers.pop(0), sems.pop(0))
                if mode == "l":
                    given[i].begin()
            elif mode == "d":
                given[i] = Leaving(buffers.pop(0), given[i], sems.pop(0))
                leaving.append(given[i])
        kernel(*given, *own)
        for out in leaving:
            out.finish()

    return pl.pallas_call(
        body,
        out_shape=tuple(out for _, out in outs),
        in_specs=[specs[mode] for mode, _ in ins],
        out_specs=tuple(specs[mode] for mode, _ in outs),
        scratch_shapes=list(scratch) + staging,
        compiler_params=pltpu.CompilerParams(vmem_limit_bytes=limit * MIB),
        cost_estimate=cost,
    )(*[array for _, array in ins])


def start_all(pairs, sems):
    copies = [
        pltpu.make_async_copy(source, target, sems.at[i]) for i, (source, target) in enumerate(pairs)
    ]
    for copy in copies:
        copy.start()
    return copies


def wait_all(copies):
    for copy in copies:
        copy.wait()


class Plan:
    def __init__(self, frames_local, patches_local, frame_ways, patch_ways):
        self.frames_local = frames_local
        self.patches_local = patches_local
        self.frame_ways = frame_ways
        self.patch_ways = patch_ways
        self.devices = frame_ways * patch_ways
        self.tokens = frames_local * patches_local
        self.frames = frames_local * frame_ways
        self.patches = patches_local * patch_ways
        self.items = frames_local * HEADS // patch_ways
        self.groups = HEADS // self.items
        self.width = self.items * HEAD_DIM
        self.window = max(
            -(-((g + 1) * self.width - g * self.width // LANES * LANES) // LANES) * LANES
            for g in range(self.groups)
        )
        self.padded = self.items * LANES
        self.own_patches = patches_local // frame_ways
        self.own_rows = frames_local * self.own_patches
        self.rows = self.frames * self.own_patches
        self.part = min(self.patches, 512)
        self.parts = self.patches // self.part
        self.term_blocks = BLOCK // patch_ways
        self.term_rows = 4 * CHUNKS * self.term_blocks
        self.term_tiles = -(-self.term_rows // TILE)

    def window_start(self, group):
        return min(group * self.width // LANES * LANES, D - self.window)

    def own_window(self):
        group = lax.rem(lax.axis_index("patch"), self.groups)
        start = jnp.minimum(group * self.width // LANES * LANES, D - self.window)
        return pl.multiple_of(start, LANES), group * self.width - start

    def peer(self, distance):
        return lax.axis_index("patch") ^ distance

    def frame_of(self, distance):
        return self.peer(distance) // self.groups

    def other_frame(self, shift):
        return lax.rem(lax.axis_index("frame") + shift, self.frame_ways)


def head_selection(plan, offset):
    lane = lax.broadcasted_iota(jnp.int32, (plan.window, plan.padded), 0)
    target = lax.broadcasted_iota(jnp.int32, (plan.window, plan.padded), 1)
    inner = target % LANES
    source = offset + (target // LANES) * HEAD_DIM + inner
    return jnp.where((lane == source) & (inner < HEAD_DIM), 1.0, 0.0).astype(BF16)


def weight_windows(plan, weight_ref, windows, sems):
    start, _ = plan.own_window()
    return [
        pltpu.make_async_copy(
            weight_ref.at[:, pl.ds(pl.multiple_of(s * D + start, LANES), plan.window)],
            windows.at[:, pl.ds(s * plan.window, plan.window)],
            sems.at[s],
        )
        for s in range(3)
    ]


def pack_kernel(plan, video, cotangent, early_ref):
    own = plan.own_patches
    for t, source in enumerate((video(), cotangent())):
        for z in range(plan.frame_ways):
            for f in range(plan.frames_local):
                early_ref[z, t, f * own : (f + 1) * own, :] = source[
                    f, z * own : (z + 1) * own, :
                ]


def blocks_kernel(*refs):
    mask = diagonal_mask()
    for blocks_ref, out in zip(refs[: len(refs) // 2], refs[len(refs) // 2 :]):
        for c in range(CHUNKS):
            tiled = jnp.concatenate([blocks_ref[lanes_of(c), :]] * (LANES // BLOCK), axis=1)
            out.ref[0, lanes_of(c), :] = jnp.where(mask, tiled, 0.0).astype(BF16)
        out.flush(0)


def spatial_forward_kernel(plan, *refs):
    pieces = refs[: plan.patch_ways]
    (
        blocks,
        weight_ref,
        normed_out,
        stack_out,
        weights_out,
        send_ref,
        windows,
        attended,
        sems,
    ) = refs[plan.patch_ways :]
    copies = weight_windows(plan, weight_ref, windows, sems)
    for copy in copies:
        copy.start()
    _, offset = plan.own_window()
    chosen = head_selection(plan, offset)
    size = plan.patches_local
    for r, piece in enumerate(pieces):
        rows = piece()
        for i in range(0, size, BLOCK):
            normed = normalize(rows[i : i + BLOCK, :].astype(F32))[0].astype(BF16)
            normed_out.ref[0, r * size + i : r * size + i + BLOCK, :] = normed
    normed_out.flush(0)
    rotated = rotate(normed_out.ref[0], blocks().at[0]).astype(BF16)
    stack_ref = stack_out.ref
    wait_all(copies)
    projected = dot(rotated, windows[...]).astype(BF16)
    for s in range(3):
        part = projected[:, s * plan.window : (s + 1) * plan.window]
        stack_ref[s] = dot(part, chosen).astype(BF16)
        stack_out.flush(s)
    for h in range(plan.items):
        queries, keys, values = [stack_ref[s, :, lanes_of(h)] for s in range(3)]
        values_t = values.astype(F32).T.astype(BF16)
        for c in range(plan.parts):
            span = slice(c * plan.part, (c + 1) * plan.part)
            scores = dot_nt(keys, queries[span]) * SCALE
            top = jnp.max(scores, axis=0, keepdims=True)
            raised = jnp.exp(scores - top)
            total = jnp.sum(raised, axis=0, keepdims=True)
            rounded = (raised * (1.0 / total)).astype(BF16)
            weights_out.ref[h * plan.parts + c] = rounded
            weights_out.flush(h * plan.parts + c)
            attended[span, lanes_of(h)] = dot(values_t, rounded).T.astype(BF16)
    own = plan.own_patches
    result = dot_nt(attended[...], chosen).astype(BF16)
    for r in range(plan.patch_ways):
        target = plan.peer(r)
        for z in range(plan.frame_ways):
            start = r * size + z * own
            send_ref[z * plan.patch_ways + target] = result[start : start + own, :]


def order_terms(plan, terms, ordered, first, count):
    share = plan.term_tiles * TILE
    for b in range(BLOCK):
        owner, inner = divmod(b, plan.term_blocks)
        start = owner * share + inner * 4 * CHUNKS + first
        ordered[start : start + count, :] = terms[pl.ds(b, count, stride=BLOCK), :]


def store_terms(plan, ordered, distance, out_ref):
    share = plan.term_tiles * TILE
    start = pl.multiple_of(plan.peer(distance) * share, TILE)
    owned = ordered[pl.ds(start, share), :].astype(BF16)
    for k in range(CHUNKS):
        if k < plan.term_tiles:
            tile = owned[k * TILE : (k + 1) * TILE, :]
        else:
            tile = jnp.zeros((TILE, LANES), BF16)
        out_ref[:, lanes_of(k)] = tile


def term_kernel(plan, prepared_ref, factors, even_out, odd_out, outrot, terms, ordered, sems):
    copies = start_all([(prepared_ref.at[1], outrot)], sems)
    mask = diagonal_mask()
    parts = factors()
    rotation_gradient(parts[1], parts[2], mask, terms, CHUNKS)
    rotation_gradient(parts[3], parts[4], mask, terms, 2 * CHUNKS)
    wait_all(copies)
    rotation_gradient(parts[0], outrot[...], mask, terms, 0)
    ordered[...] = jnp.zeros_like(ordered)
    order_terms(plan, terms, ordered, 0, 3 * CHUNKS)
    for r in range(plan.patch_ways):
        out = (even_out, odd_out)[r % 2]
        store_terms(plan, ordered, r, out.ref.at[r // 2])
        out.flush(r // 2)


def spatial_backward_kernel(
    plan,
    adjoint_ref,
    stack,
    weights,
    blocks,
    normed,
    weight_ref,
    even_out,
    odd_out,
    windows,
    adjoint,
    grads,
    projected,
    terms,
    ordered,
    sems,
):
    copies = weight_windows(plan, weight_ref, windows, sems)
    for copy in copies:
        copy.start()
    own = plan.own_patches
    for r in range(plan.patch_ways):
        source = plan.peer(r)
        for z in range(plan.frame_ways):
            start = r * plan.patches_local + z * own
            adjoint[start : start + own, :] = adjoint_ref[z * plan.patch_ways + source]
    _, offset = plan.own_window()
    chosen = head_selection(plan, offset)
    upstream_all = dot(adjoint[...], chosen).astype(BF16)
    stack_ref, weights_ref = stack(), weights()
    for h in range(plan.items):
        queries, keys, values = [stack_ref[s, :, lanes_of(h)] for s in range(3)]
        upstream = upstream_all[:, lanes_of(h)]
        keys_t = keys.astype(F32).T.astype(BF16)
        grad_keys = None
        grad_values = None
        for c in range(plan.parts):
            span = slice(c * plan.part, (c + 1) * plan.part)
            rounded = weights_ref[h * plan.parts + c]
            probability = rounded.astype(F32)
            grad_weights = dot_nt(values, upstream[span])
            delta = jnp.sum(probability * grad_weights, axis=0, keepdims=True)
            grad_scores = (probability * (grad_weights - delta)).astype(BF16)
            value_part = dot(rounded, upstream[span])
            key_part = dot(grad_scores, queries[span])
            grad_values = value_part if grad_values is None else grad_values + value_part
            grad_keys = key_part if grad_keys is None else grad_keys + key_part
            grads[0, span, lanes_of(h)] = (dot(keys_t, grad_scores).T * SCALE).astype(BF16)
        grads[1, :, lanes_of(h)] = (grad_keys * SCALE).astype(BF16)
        grads[2, :, lanes_of(h)] = grad_values.astype(BF16)
    for s, copy in enumerate(copies):
        projected[:, s * plan.window : (s + 1) * plan.window] = dot_nt(grads[s], chosen).astype(
            BF16
        )
        copy.wait()
    rotated = dot_nt(projected[...], windows[...]).astype(BF16)
    size = plan.patches_local
    rotation_gradient(normed()[0], rotated, diagonal_mask(), terms, 0)
    ordered[...] = jnp.zeros_like(ordered)
    order_terms(plan, terms, ordered, 3 * CHUNKS, CHUNKS)
    back = rotate_transposed(rotated, blocks().at[0]).astype(BF16)
    for r in list(range(1, plan.patch_ways, 2)) + list(range(0, plan.patch_ways, 2)):
        out = (even_out, odd_out)[r % 2]
        out_ref = out.ref.at[r // 2]
        out_ref[0:size, :] = back[r * size : (r + 1) * size, :]
        store_terms(plan, ordered, r, out_ref.at[size : size + TILE])
        out.flush(r // 2)


def pair_kernel(plan, even_ref, other_ref, even_term_ref, other_term_ref, *out_refs):
    size = plan.patches_local
    for s, out_ref in enumerate(out_refs):
        added = even_ref[s].astype(F32) + other_ref[s].astype(F32)
        early = even_term_ref[s].astype(F32) + other_term_ref[s].astype(F32)
        out_ref[0:size, :] = added[0:size].astype(BF16)
        out_ref[size:, :] = (added[size:] + early).astype(BF16)


def frame_column(plan, mask_ref):
    frame = lax.broadcasted_iota(jnp.int32, (plan.rows, 1), 0) // plan.own_patches
    valid = jnp.zeros((plan.rows, 1), jnp.int32)
    for f in range(plan.frames):
        valid = jnp.where(frame == f, mask_ref[f], valid)
    return valid


def collect_rows(plan, early_ref, which, target):
    return [
        (early_ref.at[z, which], target.at[pl.ds(z * plan.own_rows, plan.own_rows), :])
        for z in range(plan.frame_ways)
    ]


def top_kernel(plan, early_ref, mask_ref, weight, blocks, out, rows, sems):
    copies = start_all(collect_rows(plan, early_ref, 1, rows), sems)
    valid = frame_column(plan, mask_ref).astype(F32)
    wait_all(copies)
    top = (rows[...].astype(F32) * valid).astype(BF16)
    out.ref[0] = top
    out.flush(0)
    outrot = dot_nt(top, weight()[...]).astype(BF16)
    out.ref[1] = outrot
    out.flush(1)
    out.ref[2] = rotate_transposed(outrot, blocks().at[0]).astype(BF16)
    out.flush(2)


def head_window(h):
    low = h * HEAD_DIM // LANES * LANES
    high = -(-(h + 1) * HEAD_DIM // LANES) * LANES
    return low, high


def head_lanes(h, low, high):
    lane = low + lax.broadcasted_iota(jnp.int32, (1, high - low), 1)
    inside = (lane >= h * HEAD_DIM) & (lane < (h + 1) * HEAD_DIM)
    return jnp.where(inside, 1.0, 0.0).astype(BF16)


def temporal_kernel(plan, *refs):
    (
        early_ref,
        arrived,
        mask_ref,
        outward,
        spatial_output,
        inward,
        project_ref,
        prepared,
        send_ref,
        factors,
    ) = refs[:10]
    leaving = refs[10 : 10 + plan.frame_ways]
    (
        project_weight,
        weight_sems,
        inputs,
        projected,
        weights,
        slopes,
        grads,
        piece_sems,
    ) = refs[10 + plan.frame_ways :]
    piece_copies = start_all(collect_rows(plan, early_ref, 0, inputs), piece_sems)
    weight_copies = start_all(
        [(project_ref.at[pl.ds(*span), :], project_weight.at[pl.ds(*span), :]) for span in SPANS],
        weight_sems,
    )
    own = plan.own_patches
    attended_one = factors.ref.at[3]
    arrived_ref = arrived()
    for f in range(plan.frames):
        z, inner = divmod(f, plan.frames_local)
        base = z * plan.patch_ways + inner * plan.groups
        for c in range(CHUNKS):
            tile = None
            for g in range(plan.groups):
                low = c * LANES - plan.window_start(g)
                if 0 <= low < plan.window:
                    part = arrived_ref[base + g, :, low : low + LANES]
                    tile = part if tile is None else tile + part
            attended_one[f * own : (f + 1) * own, lanes_of(c)] = tile
    factors.flush(3)
    outrot_one = rotate(attended_one[...], outward().at[0]).astype(BF16)
    out_weight = spatial_output()
    wait_all(piece_copies)
    hidden = (inputs[...].astype(F32) + dot(outrot_one, out_weight[...])).astype(BF16)
    normed, inverse = normalize(hidden.astype(F32))
    normed_low = normed.astype(BF16)
    factors.ref[1] = normed_low
    factors.flush(1)
    rotated = rotate(normed_low, inward().at[0]).astype(BF16)
    total = None
    for (start, size), copy in zip(SPANS, weight_copies):
        copy.wait()
        span = slice(start, start + size)
        if start == 0:
            prepared.begin()
        part = dot(rotated[:, span], project_weight[span, :])
        total = part if total is None else total + part
    projected[...] = total.astype(BF16)

    key_valid = frame_column(plan, mask_ref) == 1
    shape = (plan.rows, plan.rows)
    key_row = lax.broadcasted_iota(jnp.int32, shape, 0)
    query_row = lax.broadcasted_iota(jnp.int32, shape, 1)
    allowed = (key_row == query_row) | (((key_row % own) == (query_row % own)) & key_valid)
    early = prepared()
    rows = plan.rows
    for h in range(HEADS):
        low, high = head_window(h)
        chosen = head_lanes(h, low, high)
        queries = projected[:, low:high] * chosen
        keys = projected[:, D + low : D + high]
        values = projected[:, 2 * D + low : 2 * D + high]
        upstream = early[2, :, low:high] * chosen
        scores = jnp.where(allowed, dot_nt(keys, queries) * SCALE, NEGATIVE)
        peak = jnp.max(scores, axis=0, keepdims=True)
        raised = jnp.exp(scores - peak)
        total = jnp.sum(raised, axis=0, keepdims=True)
        probability = raised * (1.0 / total)
        weights[h * rows : (h + 1) * rows, :] = probability.astype(BF16)
        grad_weights = dot_nt(values, upstream)
        delta = jnp.sum(probability * grad_weights, axis=0, keepdims=True)
        slope = probability * (grad_weights - delta) * SCALE
        slopes[h * rows : (h + 1) * rows, :] = slope.astype(BF16)

    for c in range(CHUNKS):
        low, high = c * LANES, (c + 1) * LANES
        first, last = low // HEAD_DIM, (high - 1) // HEAD_DIM
        span = slice(first * rows, (last + 1) * rows)
        heads = range(first, last + 1)

        def stacked(tile):
            return jnp.concatenate([tile * head_lanes(h, low, high) for h in heads], axis=0)

        def beside(ref):
            return jnp.concatenate([ref[h * rows : (h + 1) * rows, :] for h in heads], axis=1)

        factors.ref[0, :, low:high] = dot_tn(
            weights[span, :], stacked(projected[:, 2 * D + low : 2 * D + high])
        ).astype(BF16)
        grads[:, low:high] = dot_tn(
            slopes[span, :], stacked(projected[:, D + low : D + high])
        ).astype(BF16)
        grads[:, D + low : D + high] = dot(
            beside(slopes), stacked(projected[:, low:high])
        ).astype(BF16)
        grads[:, 2 * D + low : 2 * D + high] = dot(
            beside(weights), stacked(early[2, :, low:high])
        ).astype(BF16)

    factors.flush(0)
    adjoint_rotated = dot_nt(grads[...], project_weight[...]).astype(BF16)
    factors.ref[2] = adjoint_rotated
    factors.flush(2)
    adjoint_normed = rotate_transposed(adjoint_rotated, inward().at[0])
    adjoint_hidden = early[0].astype(F32) + normalize_backward(adjoint_normed, normed, inverse)
    adjoint_hidden = adjoint_hidden.astype(BF16)
    inputs[...] = adjoint_hidden
    pairs = []
    for shift, piece in enumerate(leaving):
        start = pl.multiple_of(plan.other_frame(shift) * plan.own_rows, plan.own_rows)
        pairs.append((inputs.at[pl.ds(start, plan.own_rows), :], piece))
    piece_copies = start_all(pairs, piece_sems)
    outrot_adjoint = dot_nt(adjoint_hidden, out_weight[...]).astype(BF16)
    factors.ref[4] = outrot_adjoint
    factors.flush(4)
    adjoint_attended = rotate_transposed(outrot_adjoint, outward().at[0]).astype(BF16)
    for f in range(plan.frames):
        z, inner = divmod(f, plan.frames_local)
        base = z * plan.patch_ways + inner * plan.groups
        for g in range(plan.groups):
            start = plan.window_start(g)
            send_ref[base + g] = adjoint_attended[
                f * own : (f + 1) * own, start : start + plan.window
            ]
    wait_all(piece_copies)


def final_kernel(plan, *refs):
    pieces = refs[: plan.frame_ways]
    sums = refs[plan.frame_ways : plan.frame_ways + plan.patch_ways // 2]
    video_ref, video_gradient_ref, hidden = refs[plan.frame_ways + len(sums) :]
    size = plan.patches_local
    own = plan.own_patches
    for shift, piece in enumerate(pieces):
        source = plan.other_frame(plan.frame_ways - shift)
        start = pl.multiple_of(source * own, own)
        for f in range(plan.frames_local):
            hidden[f, pl.ds(start, own), :] = piece[f * own : (f + 1) * own, :]
    each = len(sums) // plan.frames_local
    for i in range(plan.frames_local):
        f = plan.frame_of(2 * i * each)
        normed, inverse = normalize(video_ref[f].astype(F32))
        adjoint = sums[i * each][0:size, :].astype(F32)
        for part in sums[i * each + 1 : (i + 1) * each]:
            adjoint = adjoint + part[0:size, :].astype(F32)
        video_gradient_ref[f] = (
            hidden[f].astype(F32) + normalize_backward(adjoint, normed, inverse)
        ).astype(BF16)


def share_kernel(plan, *refs):
    sums, out_ref = refs[:-1], refs[-1]
    size = plan.patches_local
    added = sums[0][size:, :].astype(F32)
    for part in sums[1:]:
        added = added + part[size:, :].astype(F32)
    out_ref[...] = added.astype(BF16)


def sum_kernel(plan, *refs):
    parts, (out_ref, total, turned) = refs[: plan.frame_ways], refs[plan.frame_ways :]
    added = parts[0][...].astype(F32)
    for part in parts[1:]:
        added = added + part[...].astype(F32)
    for k in range(plan.term_tiles):
        total[k * TILE : (k + 1) * TILE, :] = added[:, lanes_of(k)]
    turned[...] = jnp.zeros_like(turned)
    for b in range(plan.term_blocks):
        base = b * 4 * CHUNKS
        for i in range(LANES // BLOCK):
            turned[base + i * CHUNKS : base + (i + 1) * CHUNKS, :] = jnp.concatenate(
                [
                    total[
                        base + t * CHUNKS : base + (t + 1) * CHUNKS, i * BLOCK : (i + 1) * BLOCK
                    ]
                    for t in range(4)
                ],
                axis=1,
            )
    out_ref[...] = turned[...].astype(BF16)


def unpack_kernel(plan, scaling, *refs):
    pieces = refs[: plan.patch_ways]
    outs, wide = refs[plan.patch_ways : plan.patch_ways + 4], refs[plan.patch_ways + 4]
    blocks = 4 * CHUNKS
    row = lax.broadcasted_iota(jnp.int32, (blocks, blocks), 0)
    column = lax.broadcasted_iota(jnp.int32, (blocks, blocks), 1)
    order = (row % CHUNKS) * (LANES // BLOCK) + row // CHUNKS
    chosen = jnp.where(order == column, 1.0, 0.0).astype(BF16)
    for r, piece in enumerate(pieces):
        wide[r] = piece[...].astype(F32)
        for inner in range(plan.term_blocks):
            rows = wide[r, inner * blocks : (inner + 1) * blocks, :].astype(BF16)
            turned = dot_tn(rows, chosen) * scaling
            b = plan.peer(r) * plan.term_blocks + inner
            for t, out in enumerate(outs):
                out.ref[b] = turned[t * BLOCK : (t + 1) * BLOCK, :]
        for out in outs:
            out.flush_span(plan.peer(r) * plan.term_blocks, plan.term_blocks, r)


def estimate(flops, moved):
    return pl.CostEstimate(flops=int(flops), bytes_accessed=int(moved), transcendentals=0)


def per_device(
    video,
    cotangent,
    frame_mask,
    spatial_project,
    spatial_output,
    temporal_project,
    temporal_output,
    spatial_inward,
    spatial_outward,
    temporal_inward,
    temporal_outward,
):
    plan = Plan(video.shape[0], video.shape[1], lax.axis_size("frame"), lax.axis_size("patch"))
    shape = jax.ShapeDtypeStruct
    both = ("frame", "patch")
    dma = pltpu.SemaphoreType.DMA
    exchange = lambda rows, axis: lax.all_to_all(rows, axis, 0, 0, tiled=True)
    mode = lambda kind, arrays: [(kind, array) for array in arrays]

    def shifted(pieces):
        ways = plan.frame_ways
        return [pieces[0]] + [
            lax.ppermute(pieces[s], "frame", [(i, (i + s) % ways) for i in range(ways)])
            for s in range(1, ways)
        ]

    half = plan.patch_ways // 2
    part_shape = shape((plan.patches_local + TILE, D), BF16)
    item_shape = shape((plan.devices, plan.own_patches, plan.window), BF16)

    def swap(rows, distance):
        pairs = [(p, p ^ distance) for p in range(plan.patch_ways)]
        return lax.ppermute(rows, "patch", pairs)

    own, *chips = [
        lax.dynamic_index_in_dim(video, plan.frame_of(distance), 0, keepdims=False)
        for distance in range(0, plan.patch_ways, 2)
    ]
    chips = [swap(rows, 2 * s) for s, rows in enumerate(chips, 1)]
    (early,) = call(
        functools.partial(pack_kernel, plan),
        mode("l", [video, cotangent]),
        [("v", shape((plan.frame_ways, 2, plan.own_rows, D), BF16))],
        limit=62,
    )
    def diagonals(*stacks):
        return call(
            blocks_kernel,
            mode("v", [blocks.reshape(D, BLOCK) for blocks in stacks]),
            mode("d", [shape((1, D, LANES), BF16)] * len(stacks)),
            limit=16,
        )

    (spatial_inward,) = diagonals(spatial_inward)
    early = exchange(early, "frame")
    chips, spatial_inward = lax.optimization_barrier((chips, spatial_inward))
    gathered = [rows for piece in [own] + chips for rows in (piece, swap(piece, 1))]

    normed, stack, weights, send = call(
        functools.partial(spatial_forward_kernel, plan),
        mode("l", gathered) + [("l", spatial_inward), ("h", spatial_project)],
        [
            ("d", shape((1, plan.patches, D), BF16)),
            ("d", shape((3, plan.patches, plan.padded), BF16)),
            ("d", shape((plan.items * plan.parts, plan.patches, plan.part), BF16)),
            ("v", item_shape),
        ],
        [
            pltpu.VMEM((D, 3 * plan.window), BF16),
            pltpu.VMEM((plan.patches, plan.padded), BF16),
            dma((3,)),
        ],
        cost=estimate(8 * plan.items * plan.patches**2 * LANES, 8e6),
    )
    send, early, *stacks = lax.optimization_barrier(
        (send, early, spatial_outward, temporal_inward, temporal_outward)
    )
    arrived = exchange(send, both)
    spatial_outward, temporal_inward, temporal_outward = diagonals(*stacks)

    (prepared,) = call(
        functools.partial(top_kernel, plan),
        [("h", early), ("s", frame_mask), ("l", temporal_output), ("l", temporal_outward)],
        [("d", shape((3, plan.rows, D), BF16))],
        [pltpu.VMEM((plan.rows, D), BF16), dma((plan.frame_ways,))],
        cost=estimate(2 * plan.rows * D * D, 4e6),
    )

    send, factors, *leaving = call(
        functools.partial(temporal_kernel, plan),
        [
            ("h", early),
            ("l", arrived),
            ("s", frame_mask),
            ("l", spatial_outward),
            ("l", spatial_output),
            ("l", temporal_inward),
            ("h", temporal_project),
            ("p", prepared),
        ],
        [("v", item_shape), ("d", shape((5, plan.rows, D), BF16))]
        + mode("h", [shape((plan.own_rows, D), BF16)] * plan.frame_ways),
        [
            pltpu.VMEM((D, 3 * D), BF16),
            dma((len(SPANS),)),
            pltpu.VMEM((plan.rows, D), BF16),
            pltpu.VMEM((plan.rows, 3 * D), BF16),
            pltpu.VMEM((HEADS * plan.rows, plan.rows), BF16),
            pltpu.VMEM((HEADS * plan.rows, plan.rows), BF16),
            pltpu.VMEM((plan.rows, 3 * D), BF16),
            dma((plan.frame_ways,)),
        ],
        cost=estimate(16 * plan.rows * D * D, 12e6),
    )
    adjoint_items = exchange(send, both)
    ordered_scratch = pltpu.VMEM((plan.patch_ways * plan.term_tiles * TILE, LANES), F32)
    even_terms, odd_terms = call(
        functools.partial(term_kernel, plan),
        [("h", prepared), ("l", factors)],
        mode("d", [shape((half, TILE, D), BF16)] * 2),
        [
            pltpu.VMEM((plan.rows, D), BF16),
            pltpu.VMEM((3 * CHUNKS * BLOCK, LANES), F32),
            ordered_scratch,
            dma((1,)),
        ],
        cost=estimate(1e9, 4e6),
    )
    adjoint_items, even_terms, other_terms = lax.optimization_barrier(
        (adjoint_items, even_terms, swap(odd_terms, 1))
    )
    even, odd = call(
        functools.partial(spatial_backward_kernel, plan),
        [
            ("v", adjoint_items),
            ("l", stack),
            ("l", weights),
            ("l", spatial_inward),
            ("l", normed),
            ("h", spatial_project),
        ],
        mode("d", [shape((half,) + part_shape.shape, BF16)] * 2),
        [
            pltpu.VMEM((D, 3 * plan.window), BF16),
            pltpu.VMEM((plan.patches, plan.window), BF16),
            pltpu.VMEM((3, plan.patches, plan.padded), BF16),
            pltpu.VMEM((plan.patches, 3 * plan.window), BF16),
            pltpu.VMEM((CHUNKS * BLOCK, LANES), F32),
            ordered_scratch,
            dma((3,)),
        ],
        limit=52,
        cost=estimate(1e10, 8e6),
    )
    other = swap(odd, 1)
    sums = call(
        functools.partial(pair_kernel, plan),
        mode("v", [even, other, even_terms, other_terms]),
        mode("v", [part_shape] * half),
        limit=16,
    )
    sums = [swap(part, 2 * s) if s else part for s, part in enumerate(sums)]
    sums[1], leaving = lax.optimization_barrier((sums[1], leaving))
    leaving = shifted(leaving)
    (share,) = call(
        functools.partial(share_kernel, plan),
        mode("v", sums),
        [("v", shape((TILE, D), BF16))],
        limit=16,
    )
    shares = shifted([share] * plan.frame_ways)

    (video_gradient,) = call(
        functools.partial(final_kernel, plan),
        mode("v", leaving) + mode("v", sums) + [("v", video)],
        [("v", shape(video.shape, BF16))],
        [pltpu.VMEM(video.shape, BF16)],
        limit=16,
        cost=estimate(2e9, 3e6),
    )

    shares, video_gradient = lax.optimization_barrier((shares, video_gradient))
    share_shape = shape((plan.term_tiles * TILE, LANES), BF16)
    (send,) = call(
        functools.partial(sum_kernel, plan),
        mode("v", shares),
        [("v", share_shape)],
        [pltpu.VMEM(share_shape.shape, F32)] * 2,
        limit=16,
    )
    shared = [swap(send, r) if r else send for r in range(0, plan.patch_ways, 2)]
    shared = [rows for piece in shared for rows in (piece, swap(piece, 1))]
    scaling = 1.0 / math.sqrt(plan.tokens * plan.devices)
    block_shape = shape((BLOCK, BLOCK, D // BLOCK), F32)
    tout, tin, sout, sin = [
        blocks.transpose(2, 0, 1)
        for blocks in call(
            functools.partial(unpack_kernel, plan, scaling),
            mode("v", shared),
            mode("d", [block_shape] * 4),
            [pltpu.VMEM((plan.patch_ways,) + share_shape.shape, F32)],
            limit=16,
        )
    ]
    return (video_gradient, sin, sout, tin, tout)


def solution(mesh):
    in_specs = (P("frame", "patch", None), P("frame", "patch", None)) + (P(),) * 9
    out_specs = (P("frame", "patch", None), P(), P(), P(), P())
    return jax.shard_map(
        per_device, mesh=mesh, in_specs=in_specs, out_specs=out_specs, check_vma=False
    )
```

```python
import functools
import math

import jax
import jax.numpy as jnp
from jax import lax
from jax.experimental import pallas as pl
from jax.experimental.pallas import tpu as pltpu
from jax.sharding import PartitionSpec as P

D = 1152
HEADS = 16
HEAD_DIM = 72
BLOCK = 32
LANES = 128
TILE = 16
SPANS = ((0, 640), (640, 512))
CHUNKS = D // LANES
EPSILON = 1e-06
NEGATIVE = -1e30
SCALE = 1.0 / math.sqrt(HEAD_DIM)
F32 = jnp.float32
BF16 = jnp.bfloat16
VMEM = pl.BlockSpec(memory_space=pltpu.VMEM)
SMEM = pl.BlockSpec(memory_space=pltpu.SMEM)
HBM = pl.BlockSpec(memory_space=pltpu.HBM)
MIB = 1024 * 1024


def dot(a, b):
    return jnp.dot(a, b, preferred_element_type=F32)


def dot_nt(a, b):
    return lax.dot_general(a, b, (((1,), (1,)), ((), ())), preferred_element_type=F32)


def dot_tn(a, b):
    return lax.dot_general(a, b, (((0,), (0,)), ((), ())), preferred_element_type=F32)


def normalize(rows):
    average = jnp.mean(rows, axis=-1, keepdims=True)
    centered = rows - average
    variance = jnp.mean(centered * centered, axis=-1, keepdims=True)
    inverse = lax.rsqrt(variance + EPSILON)
    return centered * inverse, inverse


def normalize_backward(adjoint, normed, inverse):
    grad_mean = jnp.mean(adjoint, axis=-1, keepdims=True)
    grad_cross = jnp.mean(adjoint * normed, axis=-1, keepdims=True)
    return inverse * (adjoint - grad_mean - normed * grad_cross)


def diagonal_mask():
    row = lax.broadcasted_iota(jnp.int32, (LANES, LANES), 0)
    column = lax.broadcasted_iota(jnp.int32, (LANES, LANES), 1)
    return (row // BLOCK) == (column // BLOCK)


def lanes_of(chunk):
    return slice(chunk * LANES, (chunk + 1) * LANES)


def rotate(rows, blocks_ref):
    return jnp.concatenate(
        [dot(rows[:, lanes_of(c)], blocks_ref[lanes_of(c), :]) for c in range(CHUNKS)], axis=1
    )


def rotate_transposed(rows, blocks_ref):
    return jnp.concatenate(
        [dot_nt(rows[:, lanes_of(c)], blocks_ref[lanes_of(c), :]) for c in range(CHUNKS)], axis=1
    )


def rotation_gradient(left, right, mask, term_ref, base):
    for c in range(CHUNKS):
        full = jnp.where(mask, dot_tn(left[:, lanes_of(c)], right[:, lanes_of(c)]), 0.0)
        packed = full[0:BLOCK]
        for i in range(1, LANES // BLOCK):
            packed = packed + full[i * BLOCK : (i + 1) * BLOCK]
        term_ref[(base + c) * BLOCK : (base + c + 1) * BLOCK, :] = packed


class Arriving:
    def __init__(self, source, target, sem):
        self.target = target
        self.copy = pltpu.make_async_copy(source, target, sem)
        self.waited = False

    def begin(self):
        self.copy.start()

    def __call__(self):
        if not self.waited:
            self.copy.wait()
            self.waited = True
        return self.target


class Leaving:
    def __init__(self, source, target, sems):
        self.ref, self.target, self.sems = source, target, sems
        self.started = []

    def flush(self, *parts):
        for i in parts:
            copy = pltpu.make_async_copy(self.ref.at[i], self.target.at[i], self.sems.at[i])
            copy.start()
            self.started.append(copy)

    def finish(self):
        for copy in self.started:
            copy.wait()


def call(kernel, ins, outs, scratch=(), limit=60, cost=None):
    specs = {"v": VMEM, "s": SMEM, "h": HBM, "l": HBM, "p": HBM, "d": HBM}
    loads = [array for mode, array in ins if mode in "lp"]
    stores = [out for mode, out in outs if mode == "d"]
    staging = [pltpu.VMEM(array.shape, array.dtype) for array in loads + stores]
    staging += [pltpu.SemaphoreType.DMA] * len(loads)
    staging += [pltpu.SemaphoreType.DMA((out.shape[0],)) for out in stores]

    def body(*refs):
        given = list(refs[: len(ins) + len(outs)])
        own = refs[len(given) : len(given) + len(scratch)]
        staged = list(refs[len(given) + len(scratch) :])
        buffers, sems = staged[: len(loads) + len(stores)], staged[len(loads) + len(stores) :]
        leaving = []
        for i, (mode, _) in enumerate(list(ins) + list(outs)):
            if mode in "lp":
                given[i] = Arriving(given[i], buffers.pop(0), sems.pop(0))
                if mode == "l":
                    given[i].begin()
            elif mode == "d":
                given[i] = Leaving(buffers.pop(0), given[i], sems.pop(0))
                leaving.append(given[i])
        kernel(*given, *own)
        for out in leaving:
            out.finish()

    return pl.pallas_call(
        body,
        out_shape=tuple(out for _, out in outs),
        in_specs=[specs[mode] for mode, _ in ins],
        out_specs=tuple(specs[mode] for mode, _ in outs),
        scratch_shapes=list(scratch) + staging,
        compiler_params=pltpu.CompilerParams(vmem_limit_bytes=limit * MIB),
        cost_estimate=cost,
    )(*[array for _, array in ins])


def start_all(pairs, sems):
    copies = [
        pltpu.make_async_copy(source, target, sems.at[i]) for i, (source, target) in enumerate(pairs)
    ]
    for copy in copies:
        copy.start()
    return copies


def wait_all(copies):
    for copy in copies:
        copy.wait()


class Plan:
    def __init__(self, frames_local, patches_local, frame_ways, patch_ways):
        self.frames_local = frames_local
        self.patches_local = patches_local
        self.frame_ways = frame_ways
        self.patch_ways = patch_ways
        self.devices = frame_ways * patch_ways
        self.tokens = frames_local * patches_local
        self.frames = frames_local * frame_ways
        self.patches = patches_local * patch_ways
        self.items = frames_local * HEADS // patch_ways
        self.groups = HEADS // self.items
        self.width = self.items * HEAD_DIM
        self.window = max(
            -(-((g + 1) * self.width - g * self.width // LANES * LANES) // LANES) * LANES
            for g in range(self.groups)
        )
        self.padded = self.items * LANES
        self.own_patches = patches_local // frame_ways
        self.own_rows = frames_local * self.own_patches
        self.rows = self.frames * self.own_patches
        self.part = min(self.patches, 512)
        self.parts = self.patches // self.part
        self.term_blocks = BLOCK // patch_ways
        self.term_rows = 4 * CHUNKS * self.term_blocks
        self.term_tiles = -(-self.term_rows // TILE)

    def window_start(self, group):
        return min(group * self.width // LANES * LANES, D - self.window)

    def own_window(self):
        group = lax.rem(lax.axis_index("patch"), self.groups)
        start = jnp.minimum(group * self.width // LANES * LANES, D - self.window)
        return pl.multiple_of(start, LANES), group * self.width - start

    def peer(self, distance):
        return lax.axis_index("patch") ^ distance

    def frame_of(self, distance):
        return self.peer(distance) // self.groups

    def other_frame(self, shift):
        return lax.rem(lax.axis_index("frame") + shift, self.frame_ways)


def head_selection(plan, offset):
    lane = lax.broadcasted_iota(jnp.int32, (plan.window, plan.padded), 0)
    target = lax.broadcasted_iota(jnp.int32, (plan.window, plan.padded), 1)
    inner = target % LANES
    source = offset + (target // LANES) * HEAD_DIM + inner
    return jnp.where((lane == source) & (inner < HEAD_DIM), 1.0, 0.0).astype(BF16)


def weight_windows(plan, weight_ref, windows, sems):
    start, _ = plan.own_window()
    return [
        pltpu.make_async_copy(
            weight_ref.at[:, pl.ds(pl.multiple_of(s * D + start, LANES), plan.window)],
            windows.at[:, pl.ds(s * plan.window, plan.window)],
            sems.at[s],
        )
        for s in range(3)
    ]


def pack_kernel(plan, video, cotangent, early_ref):
    own = plan.own_patches
    for t, source in enumerate((video(), cotangent())):
        for z in range(plan.frame_ways):
            for f in range(plan.frames_local):
                early_ref[z, t, f * own : (f + 1) * own, :] = source[
                    f, z * own : (z + 1) * own, :
                ]


def blocks_kernel(*refs):
    mask = diagonal_mask()
    for blocks_ref, out in zip(refs[: len(refs) // 2], refs[len(refs) // 2 :]):
        for c in range(CHUNKS):
            tiled = jnp.concatenate([blocks_ref[lanes_of(c), :]] * (LANES // BLOCK), axis=1)
            out.ref[0, lanes_of(c), :] = jnp.where(mask, tiled, 0.0).astype(BF16)
        out.flush(0)


def spatial_forward_kernel(plan, *refs):
    pieces = refs[: plan.patch_ways]
    (
        blocks,
        weight_ref,
        normed_out,
        stack_out,
        weights_out,
        send_ref,
        windows,
        attended,
        sems,
    ) = refs[plan.patch_ways :]
    copies = weight_windows(plan, weight_ref, windows, sems)
    for copy in copies:
        copy.start()
    _, offset = plan.own_window()
    chosen = head_selection(plan, offset)
    size = plan.patches_local
    for r, piece in enumerate(pieces):
        rows = piece()
        for i in range(0, size, BLOCK):
            normed = normalize(rows[i : i + BLOCK, :].astype(F32))[0].astype(BF16)
            normed_out.ref[0, r * size + i : r * size + i + BLOCK, :] = normed
    normed_out.flush(0)
    rotated = rotate(normed_out.ref[0], blocks().at[0]).astype(BF16)
    stack_ref = stack_out.ref
    wait_all(copies)
    projected = dot(rotated, windows[...]).astype(BF16)
    for s in range(3):
        part = projected[:, s * plan.window : (s + 1) * plan.window]
        stack_ref[s] = dot(part, chosen).astype(BF16)
        stack_out.flush(s)
    for h in range(plan.items):
        queries, keys, values = [stack_ref[s, :, lanes_of(h)] for s in range(3)]
        values_t = values.astype(F32).T.astype(BF16)
        for c in range(plan.parts):
            span = slice(c * plan.part, (c + 1) * plan.part)
            scores = dot_nt(keys, queries[span]) * SCALE
            top = jnp.max(scores, axis=0, keepdims=True)
            raised = jnp.exp(scores - top)
            total = jnp.sum(raised, axis=0, keepdims=True)
            rounded = (raised * (1.0 / total)).astype(BF16)
            weights_out.ref[h * plan.parts + c] = rounded
            weights_out.flush(h * plan.parts + c)
            attended[span, lanes_of(h)] = dot(values_t, rounded).T.astype(BF16)
    own = plan.own_patches
    result = dot_nt(attended[...], chosen).astype(BF16)
    for r in range(plan.patch_ways):
        target = plan.peer(r)
        for z in range(plan.frame_ways):
            start = r * size + z * own
            send_ref[z * plan.patch_ways + target] = result[start : start + own, :]


def order_terms(plan, terms, ordered, first, count):
    share = plan.term_tiles * TILE
    for b in range(BLOCK):
        owner, inner = divmod(b, plan.term_blocks)
        start = owner * share + inner * 4 * CHUNKS + first
        ordered[start : start + count, :] = terms[pl.ds(b, count, stride=BLOCK), :]


def store_terms(plan, ordered, distance, out_ref):
    share = plan.term_tiles * TILE
    start = pl.multiple_of(plan.peer(distance) * share, TILE)
    owned = ordered[pl.ds(start, share), :].astype(BF16)
    for k in range(CHUNKS):
        if k < plan.term_tiles:
            tile = owned[k * TILE : (k + 1) * TILE, :]
        else:
            tile = jnp.zeros((TILE, LANES), BF16)
        out_ref[:, lanes_of(k)] = tile


def term_kernel(plan, prepared_ref, factors, even_out, odd_out, outrot, terms, ordered, sems):
    copies = start_all([(prepared_ref.at[1], outrot)], sems)
    mask = diagonal_mask()
    parts = factors()
    rotation_gradient(parts[1], parts[2], mask, terms, CHUNKS)
    rotation_gradient(parts[3], parts[4], mask, terms, 2 * CHUNKS)
    wait_all(copies)
    rotation_gradient(parts[0], outrot[...], mask, terms, 0)
    ordered[...] = jnp.zeros_like(ordered)
    order_terms(plan, terms, ordered, 0, 3 * CHUNKS)
    for r in range(plan.patch_ways):
        out = (even_out, odd_out)[r % 2]
        store_terms(plan, ordered, r, out.ref.at[r // 2])
        out.flush(r // 2)


def spatial_backward_kernel(
    plan,
    adjoint_ref,
    stack,
    weights,
    blocks,
    normed,
    weight_ref,
    even_out,
    odd_out,
    windows,
    adjoint,
    grads,
    projected,
    terms,
    ordered,
    sems,
):
    copies = weight_windows(plan, weight_ref, windows, sems)
    for copy in copies:
        copy.start()
    own = plan.own_patches
    for r in range(plan.patch_ways):
        source = plan.peer(r)
        for z in range(plan.frame_ways):
            start = r * plan.patches_local + z * own
            adjoint[start : start + own, :] = adjoint_ref[z * plan.patch_ways + source]
    _, offset = plan.own_window()
    chosen = head_selection(plan, offset)
    upstream_all = dot(adjoint[...], chosen).astype(BF16)
    stack_ref, weights_ref = stack(), weights()
    for h in range(plan.items):
        queries, keys, values = [stack_ref[s, :, lanes_of(h)] for s in range(3)]
        upstream = upstream_all[:, lanes_of(h)]
        keys_t = keys.astype(F32).T.astype(BF16)
        grad_keys = None
        grad_values = None
        for c in range(plan.parts):
            span = slice(c * plan.part, (c + 1) * plan.part)
            rounded = weights_ref[h * plan.parts + c]
            probability = rounded.astype(F32)
            grad_weights = dot_nt(values, upstream[span])
            delta = jnp.sum(probability * grad_weights, axis=0, keepdims=True)
            grad_scores = (probability * (grad_weights - delta)).astype(BF16)
            value_part = dot(rounded, upstream[span])
            key_part = dot(grad_scores, queries[span])
            grad_values = value_part if grad_values is None else grad_values + value_part
            grad_keys = key_part if grad_keys is None else grad_keys + key_part
            grads[0, span, lanes_of(h)] = (dot(keys_t, grad_scores).T * SCALE).astype(BF16)
        grads[1, :, lanes_of(h)] = (grad_keys * SCALE).astype(BF16)
        grads[2, :, lanes_of(h)] = grad_values.astype(BF16)
    for s, copy in enumerate(copies):
        projected[:, s * plan.window : (s + 1) * plan.window] = dot_nt(grads[s], chosen).astype(
            BF16
        )
        copy.wait()
    rotated = dot_nt(projected[...], windows[...]).astype(BF16)
    size = plan.patches_local
    rotation_gradient(normed()[0], rotated, diagonal_mask(), terms, 0)
    ordered[...] = jnp.zeros_like(ordered)
    order_terms(plan, terms, ordered, 3 * CHUNKS, CHUNKS)
    back = rotate_transposed(rotated, blocks().at[0]).astype(BF16)
    for r in list(range(1, plan.patch_ways, 2)) + list(range(0, plan.patch_ways, 2)):
        out = (even_out, odd_out)[r % 2]
        out_ref = out.ref.at[r // 2]
        out_ref[0:size, :] = back[r * size : (r + 1) * size, :]
        store_terms(plan, ordered, r, out_ref.at[size : size + TILE])
        out.flush(r // 2)


def pair_kernel(plan, even_ref, other_ref, even_term_ref, other_term_ref, *out_refs):
    size = plan.patches_local
    for s, out_ref in enumerate(out_refs):
        added = even_ref[s].astype(F32) + other_ref[s].astype(F32)
        early = even_term_ref[s].astype(F32) + other_term_ref[s].astype(F32)
        out_ref[0:size, :] = added[0:size].astype(BF16)
        out_ref[size:, :] = (added[size:] + early).astype(BF16)


def frame_column(plan, mask_ref):
    frame = lax.broadcasted_iota(jnp.int32, (plan.rows, 1), 0) // plan.own_patches
    valid = jnp.zeros((plan.rows, 1), jnp.int32)
    for f in range(plan.frames):
        valid = jnp.where(frame == f, mask_ref[f], valid)
    return valid


def collect_rows(plan, early_ref, which, target):
    return [
        (early_ref.at[z, which], target.at[pl.ds(z * plan.own_rows, plan.own_rows), :])
        for z in range(plan.frame_ways)
    ]


def top_kernel(plan, early_ref, mask_ref, weight, blocks, out, rows, sems):
    copies = start_all(collect_rows(plan, early_ref, 1, rows), sems)
    valid = frame_column(plan, mask_ref).astype(F32)
    wait_all(copies)
    top = (rows[...].astype(F32) * valid).astype(BF16)
    out.ref[0] = top
    out.flush(0)
    outrot = dot_nt(top, weight()[...]).astype(BF16)
    out.ref[1] = outrot
    out.flush(1)
    out.ref[2] = rotate_transposed(outrot, blocks().at[0]).astype(BF16)
    out.flush(2)


def head_window(h):
    low = h * HEAD_DIM // LANES * LANES
    high = -(-(h + 1) * HEAD_DIM // LANES) * LANES
    return low, high


def head_lanes(h, low, high):
    lane = low + lax.broadcasted_iota(jnp.int32, (1, high - low), 1)
    inside = (lane >= h * HEAD_DIM) & (lane < (h + 1) * HEAD_DIM)
    return jnp.where(inside, 1.0, 0.0).astype(BF16)


def temporal_kernel(plan, *refs):
    (
        early_ref,
        arrived,
        mask_ref,
        outward,
        spatial_output,
        inward,
        project_ref,
        prepared,
        send_ref,
        factors,
    ) = refs[:10]
    leaving = refs[10 : 10 + plan.frame_ways]
    (
        project_weight,
        weight_sems,
        inputs,
        projected,
        weights,
        slopes,
        grads,
        piece_sems,
    ) = refs[10 + plan.frame_ways :]
    piece_copies = start_all(collect_rows(plan, early_ref, 0, inputs), piece_sems)
    weight_copies = start_all(
        [(project_ref.at[pl.ds(*span), :], project_weight.at[pl.ds(*span), :]) for span in SPANS],
        weight_sems,
    )
    own = plan.own_patches
    attended_one = factors.ref.at[3]
    arrived_ref = arrived()
    for f in range(plan.frames):
        z, inner = divmod(f, plan.frames_local)
        base = z * plan.patch_ways + inner * plan.groups
        for c in range(CHUNKS):
            tile = None
            for g in range(plan.groups):
                low = c * LANES - plan.window_start(g)
                if 0 <= low < plan.window:
                    part = arrived_ref[base + g, :, low : low + LANES]
                    tile = part if tile is None else tile + part
            attended_one[f * own : (f + 1) * own, lanes_of(c)] = tile
    factors.flush(3)
    outrot_one = rotate(attended_one[...], outward().at[0]).astype(BF16)
    out_weight = spatial_output()
    wait_all(piece_copies)
    hidden = (inputs[...].astype(F32) + dot(outrot_one, out_weight[...])).astype(BF16)
    normed, inverse = normalize(hidden.astype(F32))
    normed_low = normed.astype(BF16)
    factors.ref[1] = normed_low
    factors.flush(1)
    rotated = rotate(normed_low, inward().at[0]).astype(BF16)
    total = None
    for (start, size), copy in zip(SPANS, weight_copies):
        copy.wait()
        span = slice(start, start + size)
        if start == 0:
            prepared.begin()
        part = dot(rotated[:, span], project_weight[span, :])
        total = part if total is None else total + part
    projected[...] = total.astype(BF16)

    key_valid = frame_column(plan, mask_ref) == 1
    shape = (plan.rows, plan.rows)
    key_row = lax.broadcasted_iota(jnp.int32, shape, 0)
    query_row = lax.broadcasted_iota(jnp.int32, shape, 1)
    allowed = (key_row == query_row) | (((key_row % own) == (query_row % own)) & key_valid)
    early = prepared()
    rows = plan.rows
    for h in range(HEADS):
        low, high = head_window(h)
        chosen = head_lanes(h, low, high)
        queries = projected[:, low:high] * chosen
        keys = projected[:, D + low : D + high]
        values = projected[:, 2 * D + low : 2 * D + high]
        upstream = early[2, :, low:high] * chosen
        scores = jnp.where(allowed, dot_nt(keys, queries) * SCALE, NEGATIVE)
        peak = jnp.max(scores, axis=0, keepdims=True)
        raised = jnp.exp(scores - peak)
        total = jnp.sum(raised, axis=0, keepdims=True)
        probability = raised * (1.0 / total)
        weights[h * rows : (h + 1) * rows, :] = probability.astype(BF16)
        grad_weights = dot_nt(values, upstream)
        delta = jnp.sum(probability * grad_weights, axis=0, keepdims=True)
        slope = probability * (grad_weights - delta) * SCALE
        slopes[h * rows : (h + 1) * rows, :] = slope.astype(BF16)

    for c in range(CHUNKS):
        low, high = c * LANES, (c + 1) * LANES
        first, last = low // HEAD_DIM, (high - 1) // HEAD_DIM
        span = slice(first * rows, (last + 1) * rows)
        heads = range(first, last + 1)

        def stacked(tile):
            return jnp.concatenate([tile * head_lanes(h, low, high) for h in heads], axis=0)

        def beside(ref):
            return jnp.concatenate([ref[h * rows : (h + 1) * rows, :] for h in heads], axis=1)

        factors.ref[0, :, low:high] = dot_tn(
            weights[span, :], stacked(projected[:, 2 * D + low : 2 * D + high])
        ).astype(BF16)
        grads[:, low:high] = dot_tn(
            slopes[span, :], stacked(projected[:, D + low : D + high])
        ).astype(BF16)
        grads[:, D + low : D + high] = dot(
            beside(slopes), stacked(projected[:, low:high])
        ).astype(BF16)
        grads[:, 2 * D + low : 2 * D + high] = dot(
            beside(weights), stacked(early[2, :, low:high])
        ).astype(BF16)

    factors.flush(0)
    adjoint_rotated = dot_nt(grads[...], project_weight[...]).astype(BF16)
    factors.ref[2] = adjoint_rotated
    factors.flush(2)
    adjoint_normed = rotate_transposed(adjoint_rotated, inward().at[0])
    adjoint_hidden = early[0].astype(F32) + normalize_backward(adjoint_normed, normed, inverse)
    adjoint_hidden = adjoint_hidden.astype(BF16)
    inputs[...] = adjoint_hidden
    pairs = []
    for shift, piece in enumerate(leaving):
        start = pl.multiple_of(plan.other_frame(shift) * plan.own_rows, plan.own_rows)
        pairs.append((inputs.at[pl.ds(start, plan.own_rows), :], piece))
    piece_copies = start_all(pairs, piece_sems)
    outrot_adjoint = dot_nt(adjoint_hidden, out_weight[...]).astype(BF16)
    factors.ref[4] = outrot_adjoint
    factors.flush(4)
    adjoint_attended = rotate_transposed(outrot_adjoint, outward().at[0]).astype(BF16)
    for f in range(plan.frames):
        z, inner = divmod(f, plan.frames_local)
        base = z * plan.patch_ways + inner * plan.groups
        for g in range(plan.groups):
            start = plan.window_start(g)
            send_ref[base + g] = adjoint_attended[
                f * own : (f + 1) * own, start : start + plan.window
            ]
    wait_all(piece_copies)


def final_kernel(plan, *refs):
    pieces = refs[: plan.frame_ways]
    sums = refs[plan.frame_ways : plan.frame_ways + plan.patch_ways // 2]
    video_ref, video_gradient_ref, hidden = refs[plan.frame_ways + len(sums) :]
    size = plan.patches_local
    own = plan.own_patches
    for shift, piece in enumerate(pieces):
        source = plan.other_frame(plan.frame_ways - shift)
        start = pl.multiple_of(source * own, own)
        for f in range(plan.frames_local):
            hidden[f, pl.ds(start, own), :] = piece[f * own : (f + 1) * own, :]
    each = len(sums) // plan.frames_local
    for i in range(plan.frames_local):
        f = plan.frame_of(2 * i * each)
        normed, inverse = normalize(video_ref[f].astype(F32))
        adjoint = sums[i * each][0:size, :].astype(F32)
        for part in sums[i * each + 1 : (i + 1) * each]:
            adjoint = adjoint + part[0:size, :].astype(F32)
        video_gradient_ref[f] = (
            hidden[f].astype(F32) + normalize_backward(adjoint, normed, inverse)
        ).astype(BF16)


def share_kernel(plan, *refs):
    sums, out_ref = refs[:-1], refs[-1]
    size = plan.patches_local
    added = sums[0][size:, :].astype(F32)
    for part in sums[1:]:
        added = added + part[size:, :].astype(F32)
    out_ref[...] = added.astype(BF16)


def sum_kernel(plan, *refs):
    parts, (out_ref, total, turned) = refs[: plan.frame_ways], refs[plan.frame_ways :]
    added = parts[0][...].astype(F32)
    for part in parts[1:]:
        added = added + part[...].astype(F32)
    for k in range(plan.term_tiles):
        total[k * TILE : (k + 1) * TILE, :] = added[:, lanes_of(k)]
    turned[...] = jnp.zeros_like(turned)
    for b in range(plan.term_blocks):
        base = b * 4 * CHUNKS
        for i in range(LANES // BLOCK):
            turned[base + i * CHUNKS : base + (i + 1) * CHUNKS, :] = jnp.concatenate(
                [
                    total[
                        base + t * CHUNKS : base + (t + 1) * CHUNKS, i * BLOCK : (i + 1) * BLOCK
                    ]
                    for t in range(4)
                ],
                axis=1,
            )
    out_ref[...] = turned[...].astype(BF16)


def unpack_kernel(plan, scaling, *refs):
    pieces = refs[: plan.patch_ways]
    out_refs, wide = refs[plan.patch_ways : plan.patch_ways + 4], refs[plan.patch_ways + 4]
    blocks = 4 * CHUNKS
    row = lax.broadcasted_iota(jnp.int32, (blocks, blocks), 0)
    column = lax.broadcasted_iota(jnp.int32, (blocks, blocks), 1)
    order = (row % CHUNKS) * (LANES // BLOCK) + row // CHUNKS
    chosen = jnp.where(order == column, 1.0, 0.0).astype(BF16)
    for r, piece in enumerate(pieces):
        wide[r] = piece[...].astype(F32)
        for inner in range(plan.term_blocks):
            rows = wide[r, inner * blocks : (inner + 1) * blocks, :].astype(BF16)
            turned = dot_tn(rows, chosen) * scaling
            b = plan.peer(r) * plan.term_blocks + inner
            for t, out_ref in enumerate(out_refs):
                out_ref[b] = turned[t * BLOCK : (t + 1) * BLOCK, :]


def estimate(flops, moved):
    return pl.CostEstimate(flops=int(flops), bytes_accessed=int(moved), transcendentals=0)


def per_device(
    video,
    cotangent,
    frame_mask,
    spatial_project,
    spatial_output,
    temporal_project,
    temporal_output,
    spatial_inward,
    spatial_outward,
    temporal_inward,
    temporal_outward,
):
    plan = Plan(video.shape[0], video.shape[1], lax.axis_size("frame"), lax.axis_size("patch"))
    shape = jax.ShapeDtypeStruct
    both = ("frame", "patch")
    dma = pltpu.SemaphoreType.DMA
    exchange = lambda rows, axis: lax.all_to_all(rows, axis, 0, 0, tiled=True)
    mode = lambda kind, arrays: [(kind, array) for array in arrays]

    def shifted(pieces):
        ways = plan.frame_ways
        return [pieces[0]] + [
            lax.ppermute(pieces[s], "frame", [(i, (i + s) % ways) for i in range(ways)])
            for s in range(1, ways)
        ]

    half = plan.patch_ways // 2
    part_shape = shape((plan.patches_local + TILE, D), BF16)
    item_shape = shape((plan.devices, plan.own_patches, plan.window), BF16)

    def swap(rows, distance):
        pairs = [(p, p ^ distance) for p in range(plan.patch_ways)]
        return lax.ppermute(rows, "patch", pairs)

    own, *chips = [
        lax.dynamic_index_in_dim(video, plan.frame_of(distance), 0, keepdims=False)
        for distance in range(0, plan.patch_ways, 2)
    ]
    chips = [swap(rows, 2 * s) for s, rows in enumerate(chips, 1)]
    (early,) = call(
        functools.partial(pack_kernel, plan),
        mode("l", [video, cotangent]),
        [("v", shape((plan.frame_ways, 2, plan.own_rows, D), BF16))],
        limit=62,
    )
    def diagonals(*stacks):
        return call(
            blocks_kernel,
            mode("v", [blocks.reshape(D, BLOCK) for blocks in stacks]),
            mode("d", [shape((1, D, LANES), BF16)] * len(stacks)),
            limit=16,
        )

    (spatial_inward,) = diagonals(spatial_inward)
    early = exchange(early, "frame")
    chips, spatial_inward = lax.optimization_barrier((chips, spatial_inward))
    gathered = [rows for piece in [own] + chips for rows in (piece, swap(piece, 1))]

    normed, stack, weights, send = call(
        functools.partial(spatial_forward_kernel, plan),
        mode("l", gathered) + [("l", spatial_inward), ("h", spatial_project)],
        [
            ("d", shape((1, plan.patches, D), BF16)),
            ("d", shape((3, plan.patches, plan.padded), BF16)),
            ("d", shape((plan.items * plan.parts, plan.patches, plan.part), BF16)),
            ("v", item_shape),
        ],
        [
            pltpu.VMEM((D, 3 * plan.window), BF16),
            pltpu.VMEM((plan.patches, plan.padded), BF16),
            dma((3,)),
        ],
        cost=estimate(8 * plan.items * plan.patches**2 * LANES, 8e6),
    )
    send, early, *stacks = lax.optimization_barrier(
        (send, early, spatial_outward, temporal_inward, temporal_outward)
    )
    arrived = exchange(send, both)
    spatial_outward, temporal_inward, temporal_outward = diagonals(*stacks)

    (prepared,) = call(
        functools.partial(top_kernel, plan),
        [("h", early), ("s", frame_mask), ("l", temporal_output), ("l", temporal_outward)],
        [("d", shape((3, plan.rows, D), BF16))],
        [pltpu.VMEM((plan.rows, D), BF16), dma((plan.frame_ways,))],
        cost=estimate(2 * plan.rows * D * D, 4e6),
    )

    send, factors, *leaving = call(
        functools.partial(temporal_kernel, plan),
        [
            ("h", early),
            ("l", arrived),
            ("s", frame_mask),
            ("l", spatial_outward),
            ("l", spatial_output),
            ("l", temporal_inward),
            ("h", temporal_project),
            ("p", prepared),
        ],
        [("v", item_shape), ("d", shape((5, plan.rows, D), BF16))]
        + mode("h", [shape((plan.own_rows, D), BF16)] * plan.frame_ways),
        [
            pltpu.VMEM((D, 3 * D), BF16),
            dma((len(SPANS),)),
            pltpu.VMEM((plan.rows, D), BF16),
            pltpu.VMEM((plan.rows, 3 * D), BF16),
            pltpu.VMEM((HEADS * plan.rows, plan.rows), BF16),
            pltpu.VMEM((HEADS * plan.rows, plan.rows), BF16),
            pltpu.VMEM((plan.rows, 3 * D), BF16),
            dma((plan.frame_ways,)),
        ],
        cost=estimate(16 * plan.rows * D * D, 12e6),
    )
    adjoint_items = exchange(send, both)
    ordered_scratch = pltpu.VMEM((plan.patch_ways * plan.term_tiles * TILE, LANES), F32)
    even_terms, odd_terms = call(
        functools.partial(term_kernel, plan),
        [("h", prepared), ("l", factors)],
        mode("d", [shape((half, TILE, D), BF16)] * 2),
        [
            pltpu.VMEM((plan.rows, D), BF16),
            pltpu.VMEM((3 * CHUNKS * BLOCK, LANES), F32),
            ordered_scratch,
            dma((1,)),
        ],
        cost=estimate(1e9, 4e6),
    )
    adjoint_items, even_terms, other_terms = lax.optimization_barrier(
        (adjoint_items, even_terms, swap(odd_terms, 1))
    )
    even, odd = call(
        functools.partial(spatial_backward_kernel, plan),
        [
            ("v", adjoint_items),
            ("l", stack),
            ("l", weights),
            ("l", spatial_inward),
            ("l", normed),
            ("h", spatial_project),
        ],
        mode("d", [shape((half,) + part_shape.shape, BF16)] * 2),
        [
            pltpu.VMEM((D, 3 * plan.window), BF16),
            pltpu.VMEM((plan.patches, plan.window), BF16),
            pltpu.VMEM((3, plan.patches, plan.padded), BF16),
            pltpu.VMEM((plan.patches, 3 * plan.window), BF16),
            pltpu.VMEM((CHUNKS * BLOCK, LANES), F32),
            ordered_scratch,
            dma((3,)),
        ],
        limit=52,
        cost=estimate(1e10, 8e6),
    )
    other = swap(odd, 1)
    sums = call(
        functools.partial(pair_kernel, plan),
        mode("v", [even, other, even_terms, other_terms]),
        mode("v", [part_shape] * half),
        limit=16,
    )
    sums = [swap(part, 2 * s) if s else part for s, part in enumerate(sums)]
    sums[1], leaving = lax.optimization_barrier((sums[1], leaving))
    leaving = shifted(leaving)
    (share,) = call(
        functools.partial(share_kernel, plan),
        mode("v", sums),
        [("v", shape((TILE, D), BF16))],
        limit=16,
    )
    shares = shifted([share] * plan.frame_ways)

    (video_gradient,) = call(
        functools.partial(final_kernel, plan),
        mode("v", leaving) + mode("v", sums) + [("v", video)],
        [("v", shape(video.shape, BF16))],
        [pltpu.VMEM(video.shape, BF16)],
        limit=16,
        cost=estimate(2e9, 3e6),
    )

    shares, video_gradient = lax.optimization_barrier((shares, video_gradient))
    share_shape = shape((plan.term_tiles * TILE, LANES), BF16)
    (send,) = call(
        functools.partial(sum_kernel, plan),
        mode("v", shares),
        [("v", share_shape)],
        [pltpu.VMEM(share_shape.shape, F32)] * 2,
        limit=16,
    )
    shared = [swap(send, r) if r else send for r in range(0, plan.patch_ways, 2)]
    shared = [rows for piece in shared for rows in (piece, swap(piece, 1))]
    scaling = 1.0 / math.sqrt(plan.tokens * plan.devices)
    block_shape = shape((BLOCK, BLOCK, D // BLOCK), F32)
    tout, tin, sout, sin = [
        blocks.transpose(2, 0, 1)
        for blocks in call(
            functools.partial(unpack_kernel, plan, scaling),
            mode("v", shared),
            mode("v", [block_shape] * 4),
            [pltpu.VMEM((plan.patch_ways,) + share_shape.shape, F32)],
            limit=16,
        )
    ]
    return (video_gradient, sin, sout, tin, tout)


def solution(mesh):
    in_specs = (P("frame", "patch", None), P("frame", "patch", None)) + (P(),) * 9
    out_specs = (P("frame", "patch", None), P(), P(), P(), P())
    return jax.shard_map(
        per_device, mesh=mesh, in_specs=in_specs, out_specs=out_specs, check_vma=False
    )
```

```python
import functools
import math

import jax
import jax.numpy as jnp
from jax import lax
from jax.experimental import pallas as pl
from jax.experimental.pallas import tpu as pltpu
from jax.sharding import PartitionSpec as P

D = 1152
HEADS = 16
HEAD_DIM = 72
BLOCK = 32
LANES = 128
TILE = 16
SPANS = ((0, 640), (640, 512))
CHUNKS = D // LANES
EPSILON = 1e-06
NEGATIVE = -1e30
SCALE = 1.0 / math.sqrt(HEAD_DIM)
F32 = jnp.float32
BF16 = jnp.bfloat16
VMEM = pl.BlockSpec(memory_space=pltpu.VMEM)
SMEM = pl.BlockSpec(memory_space=pltpu.SMEM)
HBM = pl.BlockSpec(memory_space=pltpu.HBM)
MIB = 1024 * 1024


def dot(a, b):
    return jnp.dot(a, b, preferred_element_type=F32)


def dot_nt(a, b):
    return lax.dot_general(a, b, (((1,), (1,)), ((), ())), preferred_element_type=F32)


def dot_tn(a, b):
    return lax.dot_general(a, b, (((0,), (0,)), ((), ())), preferred_element_type=F32)


def normalize(rows):
    average = jnp.mean(rows, axis=-1, keepdims=True)
    centered = rows - average
    variance = jnp.mean(centered * centered, axis=-1, keepdims=True)
    inverse = lax.rsqrt(variance + EPSILON)
    return centered * inverse, inverse


def normalize_backward(adjoint, normed, inverse):
    grad_mean = jnp.mean(adjoint, axis=-1, keepdims=True)
    grad_cross = jnp.mean(adjoint * normed, axis=-1, keepdims=True)
    return inverse * (adjoint - grad_mean - normed * grad_cross)


def diagonal_mask():
    row = lax.broadcasted_iota(jnp.int32, (LANES, LANES), 0)
    column = lax.broadcasted_iota(jnp.int32, (LANES, LANES), 1)
    return (row // BLOCK) == (column // BLOCK)


def lanes_of(chunk):
    return slice(chunk * LANES, (chunk + 1) * LANES)


def rotate(rows, blocks_ref):
    return jnp.concatenate(
        [
            dot(rows[:, lanes_of(c)], blocks_ref[lanes_of(c), :]).astype(BF16)
            for c in range(CHUNKS)
        ],
        axis=1,
    )


def rotate_transposed(rows, blocks_ref, dtype=BF16):
    return jnp.concatenate(
        [
            dot_nt(rows[:, lanes_of(c)], blocks_ref[lanes_of(c), :]).astype(dtype)
            for c in range(CHUNKS)
        ],
        axis=1,
    )


def rotation_gradient(left, right, mask, term_ref, base):
    for c in range(CHUNKS):
        full = jnp.where(mask, dot_tn(left[:, lanes_of(c)], right[:, lanes_of(c)]), 0.0)
        packed = full[0:BLOCK]
        for i in range(1, LANES // BLOCK):
            packed = packed + full[i * BLOCK : (i + 1) * BLOCK]
        term_ref[(base + c) * BLOCK : (base + c + 1) * BLOCK, :] = packed


class Arriving:
    def __init__(self, source, target, sem):
        self.target = target
        self.copy = pltpu.make_async_copy(source, target, sem)
        self.waited = False

    def begin(self):
        self.copy.start()

    def __call__(self):
        if not self.waited:
            self.copy.wait()
            self.waited = True
        return self.target


class Leaving:
    def __init__(self, source, target, sems):
        self.ref, self.target, self.sems = source, target, sems
        self.started = []

    def flush(self, *parts):
        for i in parts:
            copy = pltpu.make_async_copy(self.ref.at[i], self.target.at[i], self.sems.at[i])
            copy.start()
            self.started.append(copy)

    def finish(self):
        for copy in self.started:
            copy.wait()


def call(kernel, ins, outs, scratch=(), limit=60, cost=None):
    specs = {"v": VMEM, "s": SMEM, "h": HBM, "l": HBM, "p": HBM, "d": HBM}
    loads = [array for mode, array in ins if mode in "lp"]
    stores = [out for mode, out in outs if mode == "d"]
    staging = [pltpu.VMEM(array.shape, array.dtype) for array in loads + stores]
    staging += [pltpu.SemaphoreType.DMA] * len(loads)
    staging += [pltpu.SemaphoreType.DMA((out.shape[0],)) for out in stores]

    def body(*refs):
        given = list(refs[: len(ins) + len(outs)])
        own = refs[len(given) : len(given) + len(scratch)]
        staged = list(refs[len(given) + len(scratch) :])
        buffers, sems = staged[: len(loads) + len(stores)], staged[len(loads) + len(stores) :]
        leaving = []
        for i, (mode, _) in enumerate(list(ins) + list(outs)):
            if mode in "lp":
                given[i] = Arriving(given[i], buffers.pop(0), sems.pop(0))
                if mode == "l":
                    given[i].begin()
            elif mode == "d":
                given[i] = Leaving(buffers.pop(0), given[i], sems.pop(0))
                leaving.append(given[i])
        kernel(*given, *own)
        for out in leaving:
            out.finish()

    return pl.pallas_call(
        body,
        out_shape=tuple(out for _, out in outs),
        in_specs=[specs[mode] for mode, _ in ins],
        out_specs=tuple(specs[mode] for mode, _ in outs),
        scratch_shapes=list(scratch) + staging,
        compiler_params=pltpu.CompilerParams(vmem_limit_bytes=limit * MIB),
        cost_estimate=cost,
    )(*[array for _, array in ins])


def start_all(pairs, sems):
    copies = [
        pltpu.make_async_copy(source, target, sems.at[i]) for i, (source, target) in enumerate(pairs)
    ]
    for copy in copies:
        copy.start()
    return copies


def wait_all(copies):
    for copy in copies:
        copy.wait()


class Plan:
    def __init__(self, frames_local, patches_local, frame_ways, patch_ways):
        self.frames_local = frames_local
        self.patches_local = patches_local
        self.frame_ways = frame_ways
        self.patch_ways = patch_ways
        self.devices = frame_ways * patch_ways
        self.tokens = frames_local * patches_local
        self.frames = frames_local * frame_ways
        self.patches = patches_local * patch_ways
        self.items = frames_local * HEADS // patch_ways
        self.groups = HEADS // self.items
        self.width = self.items * HEAD_DIM
        self.window = max(
            -(-((g + 1) * self.width - g * self.width // LANES * LANES) // LANES) * LANES
            for g in range(self.groups)
        )
        self.padded = self.items * LANES
        self.own_patches = patches_local // frame_ways
        self.own_rows = frames_local * self.own_patches
        self.rows = self.frames * self.own_patches
        self.part = min(self.patches, 512)
        self.parts = self.patches // self.part
        self.term_blocks = BLOCK // patch_ways
        self.term_rows = 4 * CHUNKS * self.term_blocks
        self.term_tiles = -(-self.term_rows // TILE)

    def window_start(self, group):
        return min(group * self.width // LANES * LANES, D - self.window)

    def own_window(self):
        group = lax.rem(lax.axis_index("patch"), self.groups)
        start = jnp.minimum(group * self.width // LANES * LANES, D - self.window)
        return pl.multiple_of(start, LANES), group * self.width - start

    def peer(self, distance):
        return lax.axis_index("patch") ^ distance

    def frame_of(self, distance):
        return self.peer(distance) // self.groups

    def other_frame(self, shift):
        return lax.rem(lax.axis_index("frame") + shift, self.frame_ways)


def head_selection(plan, offset):
    lane = lax.broadcasted_iota(jnp.int32, (plan.window, plan.padded), 0)
    target = lax.broadcasted_iota(jnp.int32, (plan.window, plan.padded), 1)
    inner = target % LANES
    source = offset + (target // LANES) * HEAD_DIM + inner
    return jnp.where((lane == source) & (inner < HEAD_DIM), 1.0, 0.0).astype(BF16)


def weight_windows(plan, weight_ref, windows, sems):
    start, _ = plan.own_window()
    return [
        pltpu.make_async_copy(
            weight_ref.at[:, pl.ds(pl.multiple_of(s * D + start, LANES), plan.window)],
            windows.at[:, pl.ds(s * plan.window, plan.window)],
            sems.at[s],
        )
        for s in range(3)
    ]


def pack_kernel(plan, video, cotangent, early_ref):
    own = plan.own_patches
    for t, source in enumerate((video(), cotangent())):
        for z in range(plan.frame_ways):
            for f in range(plan.frames_local):
                early_ref[z, t, f * own : (f + 1) * own, :] = source[
                    f, z * own : (z + 1) * own, :
                ]


def blocks_kernel(*refs):
    mask = diagonal_mask()
    for blocks_ref, out in zip(refs[: len(refs) // 2], refs[len(refs) // 2 :]):
        for c in range(CHUNKS):
            tiled = jnp.concatenate([blocks_ref[lanes_of(c), :]] * (LANES // BLOCK), axis=1)
            out.ref[0, lanes_of(c), :] = jnp.where(mask, tiled, 0.0).astype(BF16)
        out.flush(0)


def spatial_forward_kernel(plan, *refs):
    pieces = refs[: plan.patch_ways]
    (
        blocks,
        weight_ref,
        normed_out,
        stack_out,
        weights_out,
        send_ref,
        windows,
        attended,
        sems,
    ) = refs[plan.patch_ways :]
    copies = weight_windows(plan, weight_ref, windows, sems)
    for copy in copies:
        copy.start()
    _, offset = plan.own_window()
    chosen = head_selection(plan, offset)
    size = plan.patches_local
    for r, piece in enumerate(pieces):
        rows = piece()
        for i in range(0, size, BLOCK):
            normed = normalize(rows[i : i + BLOCK, :].astype(F32))[0].astype(BF16)
            normed_out.ref[0, r * size + i : r * size + i + BLOCK, :] = normed
    normed_out.flush(0)
    rotated = rotate(normed_out.ref[0], blocks().at[0])
    stack_ref = stack_out.ref
    wait_all(copies)
    projected = dot(rotated, windows[...]).astype(BF16)
    for s in range(3):
        part = projected[:, s * plan.window : (s + 1) * plan.window]
        stack_ref[s] = dot(part, chosen).astype(BF16)
        stack_out.flush(s)
    for h in range(plan.items):
        queries, keys, values = [stack_ref[s, :, lanes_of(h)] for s in range(3)]
        values_t = values.astype(F32).T.astype(BF16)
        for c in range(plan.parts):
            span = slice(c * plan.part, (c + 1) * plan.part)
            scores = dot_nt(keys, queries[span]) * SCALE
            top = jnp.max(scores, axis=0, keepdims=True)
            raised = jnp.exp(scores - top)
            total = jnp.sum(raised, axis=0, keepdims=True)
            rounded = (raised * (1.0 / total)).astype(BF16)
            weights_out.ref[h * plan.parts + c] = rounded
            weights_out.flush(h * plan.parts + c)
            attended[span, lanes_of(h)] = dot(values_t, rounded).T.astype(BF16)
    own = plan.own_patches
    result = dot_nt(attended[...], chosen).astype(BF16)
    for r in range(plan.patch_ways):
        target = plan.peer(r)
        for z in range(plan.frame_ways):
            start = r * size + z * own
            send_ref[z * plan.patch_ways + target] = result[start : start + own, :]


def order_terms(plan, terms, ordered, first, count):
    share = plan.term_tiles * TILE
    for b in range(BLOCK):
        owner, inner = divmod(b, plan.term_blocks)
        start = owner * share + inner * 4 * CHUNKS + first
        ordered[start : start + count, :] = terms[pl.ds(b, count, stride=BLOCK), :]


def store_terms(plan, ordered, distance, out_ref):
    share = plan.term_tiles * TILE
    start = pl.multiple_of(plan.peer(distance) * share, TILE)
    owned = ordered[pl.ds(start, share), :].astype(BF16)
    for k in range(CHUNKS):
        if k < plan.term_tiles:
            tile = owned[k * TILE : (k + 1) * TILE, :]
        else:
            tile = jnp.zeros((TILE, LANES), BF16)
        out_ref[:, lanes_of(k)] = tile


def term_kernel(plan, prepared_ref, factors, even_out, odd_out, outrot, terms, ordered, sems):
    copies = start_all([(prepared_ref.at[1], outrot)], sems)
    mask = diagonal_mask()
    parts = factors()
    rotation_gradient(parts[1], parts[2], mask, terms, CHUNKS)
    rotation_gradient(parts[3], parts[4], mask, terms, 2 * CHUNKS)
    wait_all(copies)
    rotation_gradient(parts[0], outrot[...], mask, terms, 0)
    ordered[...] = jnp.zeros_like(ordered)
    order_terms(plan, terms, ordered, 0, 3 * CHUNKS)
    for r in range(plan.patch_ways):
        out = (even_out, odd_out)[r % 2]
        store_terms(plan, ordered, r, out.ref.at[r // 2])
        out.flush(r // 2)


def spatial_backward_kernel(
    plan,
    adjoint_ref,
    stack,
    weights,
    blocks,
    normed,
    weight_ref,
    even_out,
    odd_out,
    windows,
    adjoint,
    grads,
    projected,
    terms,
    ordered,
    sems,
):
    copies = weight_windows(plan, weight_ref, windows, sems)
    for copy in copies:
        copy.start()
    own = plan.own_patches
    for r in range(plan.patch_ways):
        source = plan.peer(r)
        for z in range(plan.frame_ways):
            start = r * plan.patches_local + z * own
            adjoint[start : start + own, :] = adjoint_ref[z * plan.patch_ways + source]
    _, offset = plan.own_window()
    chosen = head_selection(plan, offset)
    upstream_all = dot(adjoint[...], chosen).astype(BF16)
    stack_ref, weights_ref = stack(), weights()
    for h in range(plan.items):
        queries, keys, values = [stack_ref[s, :, lanes_of(h)] for s in range(3)]
        upstream = upstream_all[:, lanes_of(h)]
        keys_t = keys.astype(F32).T.astype(BF16)
        grad_keys = None
        grad_values = None
        for c in range(plan.parts):
            span = slice(c * plan.part, (c + 1) * plan.part)
            rounded = weights_ref[h * plan.parts + c]
            probability = rounded.astype(F32)
            grad_weights = dot_nt(values, upstream[span])
            delta = jnp.sum(probability * grad_weights, axis=0, keepdims=True)
            grad_scores = (probability * (grad_weights - delta)).astype(BF16)
            value_part = dot(rounded, upstream[span])
            key_part = dot(grad_scores, queries[span])
            grad_values = value_part if grad_values is None else grad_values + value_part
            grad_keys = key_part if grad_keys is None else grad_keys + key_part
            grads[0, span, lanes_of(h)] = (dot(keys_t, grad_scores).T * SCALE).astype(BF16)
        grads[1, :, lanes_of(h)] = (grad_keys * SCALE).astype(BF16)
        grads[2, :, lanes_of(h)] = grad_values.astype(BF16)
    for s, copy in enumerate(copies):
        projected[:, s * plan.window : (s + 1) * plan.window] = dot_nt(grads[s], chosen).astype(
            BF16
        )
        copy.wait()
    rotated = dot_nt(projected[...], windows[...]).astype(BF16)
    size = plan.patches_local
    rotation_gradient(normed()[0], rotated, diagonal_mask(), terms, 0)
    ordered[...] = jnp.zeros_like(ordered)
    order_terms(plan, terms, ordered, 3 * CHUNKS, CHUNKS)
    back = rotate_transposed(rotated, blocks().at[0])
    for r in list(range(1, plan.patch_ways, 2)) + list(range(0, plan.patch_ways, 2)):
        out = (even_out, odd_out)[r % 2]
        out_ref = out.ref.at[r // 2]
        out_ref[0:size, :] = back[r * size : (r + 1) * size, :]
        store_terms(plan, ordered, r, out_ref.at[size : size + TILE])
        out.flush(r // 2)


def pair_kernel(plan, even_ref, other_ref, even_term_ref, other_term_ref, *out_refs):
    size = plan.patches_local
    for s, out_ref in enumerate(out_refs):
        added = even_ref[s].astype(F32) + other_ref[s].astype(F32)
        early = even_term_ref[s].astype(F32) + other_term_ref[s].astype(F32)
        out_ref[0:size, :] = added[0:size].astype(BF16)
        out_ref[size:, :] = (added[size:] + early).astype(BF16)


def frame_column(plan, mask_ref):
    frame = lax.broadcasted_iota(jnp.int32, (plan.rows, 1), 0) // plan.own_patches
    valid = jnp.zeros((plan.rows, 1), jnp.int32)
    for f in range(plan.frames):
        valid = jnp.where(frame == f, mask_ref[f], valid)
    return valid


def collect_rows(plan, early_ref, which, target):
    return [
        (early_ref.at[z, which], target.at[pl.ds(z * plan.own_rows, plan.own_rows), :])
        for z in range(plan.frame_ways)
    ]


def top_kernel(plan, early_ref, mask_ref, weight, blocks, out, rows, sems):
    copies = start_all(collect_rows(plan, early_ref, 1, rows), sems)
    valid = frame_column(plan, mask_ref).astype(F32)
    wait_all(copies)
    top = (rows[...].astype(F32) * valid).astype(BF16)
    out.ref[0] = top
    out.flush(0)
    outrot = dot_nt(top, weight()[...]).astype(BF16)
    out.ref[1] = outrot
    out.flush(1)
    out.ref[2] = rotate_transposed(outrot, blocks().at[0])
    out.flush(2)


def head_window(h):
    low = h * HEAD_DIM // LANES * LANES
    high = -(-(h + 1) * HEAD_DIM // LANES) * LANES
    return low, high


def head_lanes(h, low, high):
    lane = low + lax.broadcasted_iota(jnp.int32, (1, high - low), 1)
    inside = (lane >= h * HEAD_DIM) & (lane < (h + 1) * HEAD_DIM)
    return jnp.where(inside, 1.0, 0.0).astype(BF16)


def temporal_kernel(plan, *refs):
    (
        early_ref,
        arrived,
        mask_ref,
        outward,
        spatial_output,
        inward,
        project_ref,
        prepared,
        send_ref,
        factors,
    ) = refs[:10]
    leaving = refs[10 : 10 + plan.frame_ways]
    (
        project_weight,
        weight_sems,
        inputs,
        projected,
        weights,
        slopes,
        grads,
        piece_sems,
    ) = refs[10 + plan.frame_ways :]
    piece_copies = start_all(collect_rows(plan, early_ref, 0, inputs), piece_sems)
    weight_copies = start_all(
        [(project_ref.at[pl.ds(*span), :], project_weight.at[pl.ds(*span), :]) for span in SPANS],
        weight_sems,
    )
    own = plan.own_patches
    attended_one = factors.ref.at[3]
    arrived_ref = arrived()
    for f in range(plan.frames):
        z, inner = divmod(f, plan.frames_local)
        base = z * plan.patch_ways + inner * plan.groups
        for c in range(CHUNKS):
            tile = None
            for g in range(plan.groups):
                low = c * LANES - plan.window_start(g)
                if 0 <= low < plan.window:
                    part = arrived_ref[base + g, :, low : low + LANES]
                    tile = part if tile is None else tile + part
            attended_one[f * own : (f + 1) * own, lanes_of(c)] = tile
    factors.flush(3)
    outrot_one = rotate(attended_one[...], outward().at[0])
    out_weight = spatial_output()
    wait_all(piece_copies)
    hidden = (inputs[...].astype(F32) + dot(outrot_one, out_weight[...])).astype(BF16)
    normed, inverse = normalize(hidden.astype(F32))
    normed_low = normed.astype(BF16)
    factors.ref[1] = normed_low
    factors.flush(1)
    rotated = rotate(normed_low, inward().at[0])
    total = None
    for (start, size), copy in zip(SPANS, weight_copies):
        copy.wait()
        span = slice(start, start + size)
        if start == 0:
            prepared.begin()
        part = dot(rotated[:, span], project_weight[span, :])
        total = part if total is None else total + part
    projected[...] = total.astype(BF16)

    key_valid = frame_column(plan, mask_ref) == 1
    shape = (plan.rows, plan.rows)
    key_row = lax.broadcasted_iota(jnp.int32, shape, 0)
    query_row = lax.broadcasted_iota(jnp.int32, shape, 1)
    allowed = (key_row == query_row) | (((key_row % own) == (query_row % own)) & key_valid)
    early = prepared()
    rows = plan.rows
    for h in range(HEADS):
        low, high = head_window(h)
        chosen = head_lanes(h, low, high)
        queries = projected[:, low:high] * chosen
        keys = projected[:, D + low : D + high]
        values = projected[:, 2 * D + low : 2 * D + high]
        upstream = early[2, :, low:high] * chosen
        scores = jnp.where(allowed, dot_nt(keys, queries) * SCALE, NEGATIVE)
        peak = jnp.max(scores, axis=0, keepdims=True)
        raised = jnp.exp(scores - peak)
        total = jnp.sum(raised, axis=0, keepdims=True)
        probability = raised * (1.0 / total)
        weights[h * rows : (h + 1) * rows, :] = probability.astype(BF16)
        grad_weights = dot_nt(values, upstream)
        delta = jnp.sum(probability * grad_weights, axis=0, keepdims=True)
        slope = probability * (grad_weights - delta) * SCALE
        slopes[h * rows : (h + 1) * rows, :] = slope.astype(BF16)

    for c in range(CHUNKS):
        low, high = c * LANES, (c + 1) * LANES
        first, last = low // HEAD_DIM, (high - 1) // HEAD_DIM
        span = slice(first * rows, (last + 1) * rows)
        heads = range(first, last + 1)

        def stacked(tile):
            return jnp.concatenate([tile * head_lanes(h, low, high) for h in heads], axis=0)

        def beside(ref):
            return jnp.concatenate([ref[h * rows : (h + 1) * rows, :] for h in heads], axis=1)

        factors.ref[0, :, low:high] = dot_tn(
            weights[span, :], stacked(projected[:, 2 * D + low : 2 * D + high])
        ).astype(BF16)
        grads[:, low:high] = dot_tn(
            slopes[span, :], stacked(projected[:, D + low : D + high])
        ).astype(BF16)
        grads[:, D + low : D + high] = dot(
            beside(slopes), stacked(projected[:, low:high])
        ).astype(BF16)
        grads[:, 2 * D + low : 2 * D + high] = dot(
            beside(weights), stacked(early[2, :, low:high])
        ).astype(BF16)

    factors.flush(0)
    adjoint_rotated = dot_nt(grads[...], project_weight[...]).astype(BF16)
    factors.ref[2] = adjoint_rotated
    factors.flush(2)
    adjoint_normed = rotate_transposed(adjoint_rotated, inward().at[0], F32)
    adjoint_hidden = early[0].astype(F32) + normalize_backward(adjoint_normed, normed, inverse)
    adjoint_hidden = adjoint_hidden.astype(BF16)
    inputs[...] = adjoint_hidden
    pairs = []
    for shift, piece in enumerate(leaving):
        start = pl.multiple_of(plan.other_frame(shift) * plan.own_rows, plan.own_rows)
        pairs.append((inputs.at[pl.ds(start, plan.own_rows), :], piece))
    piece_copies = start_all(pairs, piece_sems)
    outrot_adjoint = dot_nt(adjoint_hidden, out_weight[...]).astype(BF16)
    factors.ref[4] = outrot_adjoint
    factors.flush(4)
    adjoint_attended = rotate_transposed(outrot_adjoint, outward().at[0])
    for f in range(plan.frames):
        z, inner = divmod(f, plan.frames_local)
        base = z * plan.patch_ways + inner * plan.groups
        for g in range(plan.groups):
            start = plan.window_start(g)
            send_ref[base + g] = adjoint_attended[
                f * own : (f + 1) * own, start : start + plan.window
            ]
    wait_all(piece_copies)


def final_kernel(plan, *refs):
    pieces = refs[: plan.frame_ways]
    sums = refs[plan.frame_ways : plan.frame_ways + plan.patch_ways // 2]
    video_ref, video_gradient_ref, hidden = refs[plan.frame_ways + len(sums) :]
    size = plan.patches_local
    own = plan.own_patches
    for shift, piece in enumerate(pieces):
        source = plan.other_frame(plan.frame_ways - shift)
        start = pl.multiple_of(source * own, own)
        for f in range(plan.frames_local):
            hidden[f, pl.ds(start, own), :] = piece[f * own : (f + 1) * own, :]
    each = len(sums) // plan.frames_local
    for i in range(plan.frames_local):
        f = plan.frame_of(2 * i * each)
        normed, inverse = normalize(video_ref[f].astype(F32))
        adjoint = sums[i * each][0:size, :].astype(F32)
        for part in sums[i * each + 1 : (i + 1) * each]:
            adjoint = adjoint + part[0:size, :].astype(F32)
        video_gradient_ref[f] = (
            hidden[f].astype(F32) + normalize_backward(adjoint, normed, inverse)
        ).astype(BF16)


def share_kernel(plan, *refs):
    sums, out_ref = refs[:-1], refs[-1]
    size = plan.patches_local
    added = sums[0][size:, :].astype(F32)
    for part in sums[1:]:
        added = added + part[size:, :].astype(F32)
    out_ref[...] = added.astype(BF16)


def sum_kernel(plan, *refs):
    parts, (out_ref, total, turned) = refs[: plan.frame_ways], refs[plan.frame_ways :]
    added = parts[0][...].astype(F32)
    for part in parts[1:]:
        added = added + part[...].astype(F32)
    for k in range(plan.term_tiles):
        total[k * TILE : (k + 1) * TILE, :] = added[:, lanes_of(k)]
    turned[...] = jnp.zeros_like(turned)
    for b in range(plan.term_blocks):
        base = b * 4 * CHUNKS
        for i in range(LANES // BLOCK):
            turned[base + i * CHUNKS : base + (i + 1) * CHUNKS, :] = jnp.concatenate(
                [
                    total[
                        base + t * CHUNKS : base + (t + 1) * CHUNKS, i * BLOCK : (i + 1) * BLOCK
                    ]
                    for t in range(4)
                ],
                axis=1,
            )
    out_ref[...] = turned[...].astype(BF16)


def unpack_kernel(plan, scaling, *refs):
    pieces = refs[: plan.patch_ways]
    out_refs, wide = refs[plan.patch_ways : plan.patch_ways + 4], refs[plan.patch_ways + 4]
    blocks = 4 * CHUNKS
    row = lax.broadcasted_iota(jnp.int32, (blocks, blocks), 0)
    column = lax.broadcasted_iota(jnp.int32, (blocks, blocks), 1)
    order = (row % CHUNKS) * (LANES // BLOCK) + row // CHUNKS
    chosen = jnp.where(order == column, 1.0, 0.0).astype(BF16)
    for r, piece in enumerate(pieces):
        wide[r] = piece[...].astype(F32)
        for inner in range(plan.term_blocks):
            rows = wide[r, inner * blocks : (inner + 1) * blocks, :].astype(BF16)
            turned = dot_tn(rows, chosen) * scaling
            b = plan.peer(r) * plan.term_blocks + inner
            for t, out_ref in enumerate(out_refs):
                out_ref[b] = turned[t * BLOCK : (t + 1) * BLOCK, :]


def estimate(flops, moved):
    return pl.CostEstimate(flops=int(flops), bytes_accessed=int(moved), transcendentals=0)


def per_device(
    video,
    cotangent,
    frame_mask,
    spatial_project,
    spatial_output,
    temporal_project,
    temporal_output,
    spatial_inward,
    spatial_outward,
    temporal_inward,
    temporal_outward,
):
    plan = Plan(video.shape[0], video.shape[1], lax.axis_size("frame"), lax.axis_size("patch"))
    shape = jax.ShapeDtypeStruct
    both = ("frame", "patch")
    dma = pltpu.SemaphoreType.DMA
    exchange = lambda rows, axis: lax.all_to_all(rows, axis, 0, 0, tiled=True)
    mode = lambda kind, arrays: [(kind, array) for array in arrays]

    def shifted(pieces):
        ways = plan.frame_ways
        return [pieces[0]] + [
            lax.ppermute(pieces[s], "frame", [(i, (i + s) % ways) for i in range(ways)])
            for s in range(1, ways)
        ]

    half = plan.patch_ways // 2
    part_shape = shape((plan.patches_local + TILE, D), BF16)
    item_shape = shape((plan.devices, plan.own_patches, plan.window), BF16)

    def swap(rows, distance):
        pairs = [(p, p ^ distance) for p in range(plan.patch_ways)]
        return lax.ppermute(rows, "patch", pairs)

    own, *chips = [
        lax.dynamic_index_in_dim(video, plan.frame_of(distance), 0, keepdims=False)
        for distance in range(0, plan.patch_ways, 2)
    ]
    chips = [swap(rows, 2 * s) for s, rows in enumerate(chips, 1)]
    (early,) = call(
        functools.partial(pack_kernel, plan),
        mode("l", [video, cotangent]),
        [("v", shape((plan.frame_ways, 2, plan.own_rows, D), BF16))],
        limit=62,
    )
    def diagonals(*stacks):
        return call(
            blocks_kernel,
            mode("v", [blocks.reshape(D, BLOCK) for blocks in stacks]),
            mode("d", [shape((1, D, LANES), BF16)] * len(stacks)),
            limit=16,
        )

    (spatial_inward,) = diagonals(spatial_inward)
    early = exchange(early, "frame")
    chips, spatial_inward = lax.optimization_barrier((chips, spatial_inward))
    gathered = [rows for piece in [own] + chips for rows in (piece, swap(piece, 1))]

    normed, stack, weights, send = call(
        functools.partial(spatial_forward_kernel, plan),
        mode("l", gathered) + [("l", spatial_inward), ("h", spatial_project)],
        [
            ("d", shape((1, plan.patches, D), BF16)),
            ("d", shape((3, plan.patches, plan.padded), BF16)),
            ("d", shape((plan.items * plan.parts, plan.patches, plan.part), BF16)),
            ("v", item_shape),
        ],
        [
            pltpu.VMEM((D, 3 * plan.window), BF16),
            pltpu.VMEM((plan.patches, plan.padded), BF16),
            dma((3,)),
        ],
        cost=estimate(8 * plan.items * plan.patches**2 * LANES, 8e6),
    )
    send, early, *stacks = lax.optimization_barrier(
        (send, early, spatial_outward, temporal_inward, temporal_outward)
    )
    arrived = exchange(send, both)
    spatial_outward, temporal_inward, temporal_outward = diagonals(*stacks)

    (prepared,) = call(
        functools.partial(top_kernel, plan),
        [("h", early), ("s", frame_mask), ("l", temporal_output), ("l", temporal_outward)],
        [("d", shape((3, plan.rows, D), BF16))],
        [pltpu.VMEM((plan.rows, D), BF16), dma((plan.frame_ways,))],
        cost=estimate(2 * plan.rows * D * D, 4e6),
    )

    send, factors, *leaving = call(
        functools.partial(temporal_kernel, plan),
        [
            ("h", early),
            ("l", arrived),
            ("s", frame_mask),
            ("l", spatial_outward),
            ("l", spatial_output),
            ("l", temporal_inward),
            ("h", temporal_project),
            ("p", prepared),
        ],
        [("v", item_shape), ("d", shape((5, plan.rows, D), BF16))]
        + mode("h", [shape((plan.own_rows, D), BF16)] * plan.frame_ways),
        [
            pltpu.VMEM((D, 3 * D), BF16),
            dma((len(SPANS),)),
            pltpu.VMEM((plan.rows, D), BF16),
            pltpu.VMEM((plan.rows, 3 * D), BF16),
            pltpu.VMEM((HEADS * plan.rows, plan.rows), BF16),
            pltpu.VMEM((HEADS * plan.rows, plan.rows), BF16),
            pltpu.VMEM((plan.rows, 3 * D), BF16),
            dma((plan.frame_ways,)),
        ],
        cost=estimate(16 * plan.rows * D * D, 12e6),
    )
    adjoint_items = exchange(send, both)
    ordered_scratch = pltpu.VMEM((plan.patch_ways * plan.term_tiles * TILE, LANES), F32)
    even_terms, odd_terms = call(
        functools.partial(term_kernel, plan),
        [("h", prepared), ("l", factors)],
        mode("d", [shape((half, TILE, D), BF16)] * 2),
        [
            pltpu.VMEM((plan.rows, D), BF16),
            pltpu.VMEM((3 * CHUNKS * BLOCK, LANES), F32),
            ordered_scratch,
            dma((1,)),
        ],
        cost=estimate(1e9, 4e6),
    )
    adjoint_items, even_terms, other_terms = lax.optimization_barrier(
        (adjoint_items, even_terms, swap(odd_terms, 1))
    )
    even, odd = call(
        functools.partial(spatial_backward_kernel, plan),
        [
            ("v", adjoint_items),
            ("l", stack),
            ("l", weights),
            ("l", spatial_inward),
            ("l", normed),
            ("h", spatial_project),
        ],
        mode("d", [shape((half,) + part_shape.shape, BF16)] * 2),
        [
            pltpu.VMEM((D, 3 * plan.window), BF16),
            pltpu.VMEM((plan.patches, plan.window), BF16),
            pltpu.VMEM((3, plan.patches, plan.padded), BF16),
            pltpu.VMEM((plan.patches, 3 * plan.window), BF16),
            pltpu.VMEM((CHUNKS * BLOCK, LANES), F32),
            ordered_scratch,
            dma((3,)),
        ],
        limit=52,
        cost=estimate(1e10, 8e6),
    )
    other = swap(odd, 1)
    sums = call(
        functools.partial(pair_kernel, plan),
        mode("v", [even, other, even_terms, other_terms]),
        mode("v", [part_shape] * half),
        limit=16,
    )
    sums = [swap(part, 2 * s) if s else part for s, part in enumerate(sums)]
    sums[1], leaving = lax.optimization_barrier((sums[1], leaving))
    leaving = shifted(leaving)
    (share,) = call(
        functools.partial(share_kernel, plan),
        mode("v", sums),
        [("v", shape((TILE, D), BF16))],
        limit=16,
    )
    shares = shifted([share] * plan.frame_ways)

    (video_gradient,) = call(
        functools.partial(final_kernel, plan),
        mode("v", leaving) + mode("v", sums) + [("v", video)],
        [("v", shape(video.shape, BF16))],
        [pltpu.VMEM(video.shape, BF16)],
        limit=16,
        cost=estimate(2e9, 3e6),
    )

    shares, video_gradient = lax.optimization_barrier((shares, video_gradient))
    share_shape = shape((plan.term_tiles * TILE, LANES), BF16)
    (send,) = call(
        functools.partial(sum_kernel, plan),
        mode("v", shares),
        [("v", share_shape)],
        [pltpu.VMEM(share_shape.shape, F32)] * 2,
        limit=16,
    )
    shared = [swap(send, r) if r else send for r in range(0, plan.patch_ways, 2)]
    shared = [rows for piece in shared for rows in (piece, swap(piece, 1))]
    scaling = 1.0 / math.sqrt(plan.tokens * plan.devices)
    block_shape = shape((BLOCK, BLOCK, D // BLOCK), F32)
    tout, tin, sout, sin = [
        blocks.transpose(2, 0, 1)
        for blocks in call(
            functools.partial(unpack_kernel, plan, scaling),
            mode("v", shared),
            mode("v", [block_shape] * 4),
            [pltpu.VMEM((plan.patch_ways,) + share_shape.shape, F32)],
            limit=16,
        )
    ]
    return (video_gradient, sin, sout, tin, tout)


def solution(mesh):
    in_specs = (P("frame", "patch", None), P("frame", "patch", None)) + (P(),) * 9
    out_specs = (P("frame", "patch", None), P(), P(), P(), P())
    return jax.shard_map(
        per_device, mesh=mesh, in_specs=in_specs, out_specs=out_specs, check_vma=False
    )
```
